512 devices in a mesh: dp: 64 (over y_lo, x, z), tensor: 8 (over y_hi, core).
Axes of the slice: x: 4, y: 8 (y_hi: 4, y_lo: 2; y = y_hi * 2 + y_lo), z: 8, core: 2. Of those that a mesh axis runs over, the one named last changes fastest.
Arguments:
- log_feats: bfloat16 [22528, 2048], P('dp', 'tensor'), may hold values from -6 to 6
- kpi_feats: bfloat16 [4096, 1152], P('dp', 'tensor'), may hold values from -6 to 6
- log_proj: bfloat16 [2048, 1152], P('tensor'), may hold values from -0.125 to 0.125
- kpi_proj: bfloat16 [1152, 1152], P('tensor'), may hold values from -0.1875 to 0.1875
- log_ids: int32 [22528], P('dp'), may hold values from 0 to 2047
- kpi_ids: int32 [4096], P('dp'), may hold values from 0 to 2047
Outputs:
- grad_log_feats: bfloat16 [22528, 2048], P('dp', 'tensor')
- grad_kpi_proj: float32 [1152, 1152], P('tensor')
The draws below stay inside these ranges and needn't reach their ends.
Inputs may be any that keep to these rules, and one draw needn't show every extreme that they name: `kpi_ids`: ids of the KPI series, compared with those of the log windows.
All inputs are finite; a program needn't handle non-finite values.
Results may differ from the reference program's by a relative error of at most 0.008.
Values may be sent and summed in bfloat16 or wider, within the bound.
A program may use at most 64 MiB of HBM per device.

```python
import jax
import jax.numpy as jnp
from jax import lax

DA = 2048
DK = 1152
E = 1152
LOG_DEV = 352
LOG_WINDOW_COUNT = 22528
KPI_B = 4096
N_DP = 64


def with_ends(array, own_key, smallest, largest):
    extent = array.shape
    spot = [jax.random.randint(jax.random.fold_in(own_key, axis), (), 0, extent[axis]) for axis in range(len(extent))]
    array = array.at[tuple(spot)].set(smallest)
    longest = extent.index(max(extent))
    spot[longest] = (spot[longest] + 1) % extent[longest]
    return array.at[tuple(spot)].set(largest)


def level_of(own_key, dims, split, least, largest):
    level, own = 1.0, jax.random.fold_in(own_key, 6)
    for axis_at, parts in split:
        heights = jnp.exp(jax.random.uniform(jax.random.fold_in(own, axis_at), (parts,), jnp.float32, least / len(split), largest / len(split)))
        level = level * jnp.repeat(heights, dims[axis_at] // parts).reshape([-1 if axis == axis_at else 1 for axis in range(len(dims))])
    return level


def scatter_about(stream_key, shape, spread, most, cuts=(), held_as=jnp.bfloat16):
    entries = jax.random.normal(stream_key, shape, jnp.float32) * spread
    if len(cuts) > 0:
        entries = level_of(stream_key, shape, cuts, -0.22, 0.18) * entries
    return jnp.clip(entries, min=-most, max=most).astype(held_as)


def setup_inputs(seed: int = 0) -> dict:
    seeds = jax.random.split(jax.random.key(seed), 7)
    return {
        "log_feats": scatter_about(seeds[0], (LOG_WINDOW_COUNT, DA), 1.0, 6.0, ((0, 64), (1, 8))),
        "kpi_feats": scatter_about(seeds[1], (KPI_B, DK), 1.0, 6.0, ((0, 64), (1, 8))),
        "log_proj": scatter_about(seeds[2], (DA, E), DA ** -0.5, 0.125, ((0, 8),)),
        "kpi_proj": scatter_about(seeds[3], (DK, E), DK ** -0.5, 0.1875, ((0, 8),)),
        "log_ids": with_ends(jax.random.randint(seeds[4], (LOG_WINDOW_COUNT,), 0, KPI_B // 2), jax.random.fold_in(seeds[4], 1), 0, (KPI_B // 2) - 1).astype(jnp.int32),
        "kpi_ids": with_ends(jax.random.randint(seeds[5], (KPI_B,), 0, KPI_B // 2), jax.random.fold_in(seeds[5], 1), 0, (KPI_B // 2) - 1).astype(jnp.int32),
    }


SOFTMAX_TEMPER = 32.0
LOGIT_OFFSET_BIAS = -2.0
LOSS_MULTIPLIER = 4096.0
EPSILON = 1e-06

def normalize(vectors):
    inverse = lax.rsqrt(lax.optimization_barrier(jnp.sum(vectors * vectors, axis=1, keepdims=True)) + EPSILON)
    return (vectors * inverse, inverse)

def backward(unit_rows, inverse, upstream):
    inner = lax.optimization_barrier(jnp.sum(unit_rows * upstream, axis=1, keepdims=True))
    return (inverse * (upstream - unit_rows * inner)).astype(jnp.bfloat16)

def reference(log_feats, kpi_feats, log_proj, kpi_proj, log_ids, kpi_ids):
    log_pre = jnp.dot(log_feats, log_proj, preferred_element_type=jnp.float32)
    kpi_pre = jnp.dot(kpi_feats, kpi_proj, preferred_element_type=jnp.float32)
    log_unit, log_inv = normalize(log_pre)
    kpi_unit, kpi_inv = normalize(kpi_pre)
    log_emb = log_unit.astype(jnp.bfloat16)
    metric_embedding = kpi_unit.astype(jnp.bfloat16)
    gradient_scale = SOFTMAX_TEMPER * LOSS_MULTIPLIER / LOG_WINDOW_COUNT
    emb_blocks = log_emb.reshape(N_DP, LOG_DEV, E)
    id_blocks = log_ids.reshape(N_DP, LOG_DEV)

    def step(kpi_grad, inputs):
        embedding_rows, id_rows = inputs
        pair_logits = SOFTMAX_TEMPER * jnp.dot(embedding_rows, metric_embedding.T, preferred_element_type=jnp.float32) + LOGIT_OFFSET_BIAS
        pair_sign = jnp.where(id_rows[:, None] == kpi_ids[None, :], 1.0, -1.0).astype(pair_logits.dtype)
        margin = -pair_sign * pair_logits
        pair_grad = (-gradient_scale * pair_sign * jax.nn.sigmoid(margin)).astype(jnp.bfloat16)
        log_grad = jnp.dot(pair_grad, metric_embedding, preferred_element_type=jnp.float32)
        kpi_grad = kpi_grad + jnp.dot(pair_grad.T, embedding_rows, preferred_element_type=jnp.float32)
        return (kpi_grad, log_grad)
    kpi_grad, log_grads = lax.scan(step, jnp.zeros((KPI_B, E), jnp.float32), (emb_blocks, id_blocks))
    log_grad = log_grads.reshape(LOG_WINDOW_COUNT, E)
    log_back = backward(log_unit, log_inv, log_grad)
    kpi_back = backward(kpi_unit, kpi_inv, kpi_grad)
    grad_log_feats = jnp.dot(log_back, log_proj.T, preferred_element_type=jnp.float32).astype(jnp.bfloat16)
    grad_kpi_proj = jnp.dot(kpi_feats.T, kpi_back, preferred_element_type=jnp.float32)
    return (grad_log_feats, grad_kpi_proj)
```

```python
import jax
import jax.numpy as jnp
from jax import lax
from jax.experimental import pallas as pl
from jax.experimental.pallas import tpu as pltpu
from jax.sharding import PartitionSpec as P

TEMPER = 32.0
BIAS = -2.0
LOSS = 4096.0
EPS = 1e-06
MESH = pl.DeviceIdType.MESH
BF = jnp.bfloat16
F32 = jnp.float32

NY, NX, NZ, NH = 2, 4, 8, 4
LOG = 352
HALF = LOG // 2
BLK = 48
HP = NH * BLK
E = 1152
ID = 128
EK = E + ID
GROUP = 64
OWN = 8
COUNT = NY * NX * NZ * OWN
SCALE = TEMPER * LOSS / (LOG * NY * NX * NZ)
WROWS = 176
NSEM = 128


def dot(a, b):
    return jnp.dot(a, b, preferred_element_type=F32)


def dot_t(a, b):
    return lax.dot_general(a, b, (((1,), (1,)), ((), ())), preferred_element_type=F32)


def mod(a, n):
    return lax.rem(a, jnp.int32(n))


def digits(ids):
    high = jnp.floor(ids * (1.0 / 256.0))
    rest = ids - 256.0 * high
    middle = jnp.floor(rest * (1.0 / 16.0))
    return high, middle, rest - 16.0 * middle


def on_lanes(values, rows):
    lane = lax.broadcasted_iota(jnp.int32, (rows, ID), 1)
    out = jnp.zeros((rows, ID), F32)
    for at, value in enumerate(values):
        out = jnp.where(lane == at, value, out)
    return out


def pair_gradient(inner, apart):
    sign = jnp.where(apart < 0.5, 1.0, -1.0).astype(F32)
    margin = -sign * (TEMPER * inner + BIAS)
    return (-SCALE * sign * jax.nn.sigmoid(margin)).astype(BF)


def kernel(
    lf, kf, lp, kp, lid, kid, out_g, out_w,
    lsend, lrecv, lacc, lysend, lyrecv, lall, lunit, lext,
    kacc, ksend, krecv, kysend, kyrecv, kmsg, kgot, kall, kunit,
    pg, kg, lg,
    gsend, grecv, gysend, gyrecv, back,
    zrs, zrr, zls, zlr, xrs, xrr, xls, xlr, mid, midsend, midrecv, mid16, ymsg, ygot,
    kback, wbuf, wzr, wx, wy, wall,
    ssem, rsem,
):
    d = lax.axis_index("dp")
    t = lax.axis_index("tensor")
    y = lax.div(d, jnp.int32(NX * NZ))
    x = mod(lax.div(d, jnp.int32(NZ)), NX)
    z = mod(d, NZ)
    h = lax.div(t, jnp.int32(2))
    c = mod(t, 2)
    used = [0]

    def place(y=y, x=x, z=z, h=h, c=c):
        return {"dp": (y * NX + x) * NZ + z, "tensor": h * 2 + c}

    def sem():
        used[0] += 1
        return used[0] - 1

    def copy(at, src, dst, device):
        return pltpu.make_async_remote_copy(
            src_ref=src, dst_ref=dst, send_sem=ssem.at[at], recv_sem=rsem.at[at],
            device_id=device, device_id_type=MESH,
        )

    def rows(start, size, unit):
        return pl.ds(pl.multiple_of(start, unit), size)

    partner = place(c=1 - c)
    other_y = place(y=1 - y)
    hpeer = [place(h=mod(h + r, NH)) for r in range(NH)]
    hfrom = [mod(h + NH - r, NH) for r in range(NH)]
    xpeer = [place(x=mod(x + r, NX)) for r in range(NX)]
    xfrom = [mod(x + NX - r, NX) for r in range(NX)]
    zpeer = [place(z=mod(z + r, NZ)) for r in range(NZ)]
    zfrom = [mod(z + NZ - r, NZ) for r in range(NZ)]

    barrier = pltpu.get_barrier_semaphore()
    peers = [partner, other_y] + hpeer[1:] + xpeer[1:] + zpeer[1:]
    for device in peers:
        pl.semaphore_signal(barrier, inc=1, device_id=device, device_id_type=MESH)

    pending = []

    kacc[...] = dot(kf[...], kp[...])
    ksend[...] = kacc[rows(32 * (1 - c), 32, 32), :]
    lsend[:HALF, :] = dot(lf[rows(HALF * (1 - c), HALF, 16), :], lp[...]).astype(BF)
    lsend[HALF:, :] = jnp.zeros((HP - HALF, E), BF)

    pl.semaphore_wait(barrier, len(peers))
    k_core = copy(sem(), ksend, krecv, partner)
    k_core.start()
    l_core = copy(sem(), lsend, lrecv, partner)
    l_core.start()
    pending += [k_core, l_core]

    lacc[:HALF, :] = dot(lf[rows(HALF * c, HALF, 16), :], lp[...])
    lacc[HALF:, :] = jnp.zeros((HP - HALF, E), F32)

    k_core.wait_recv()
    waits = []
    for r in (2, 1, 3):
        to = mod(h + r, NH)
        kysend[r - 1] = kacc[rows(32 * c + OWN * to, OWN, OWN), :] + krecv[rows(OWN * to, OWN, OWN), :]
        go = copy(sem(), kysend.at[r - 1], kyrecv.at[r - 1], hpeer[r])
        go.start()
        waits.append(go)
    pending += waits

    l_core.wait_recv()
    l_waits = []
    for r in (2, 1, 3):
        at = rows(BLK * mod(h + r, NH), BLK, 16)
        lysend[r - 1] = (lacc[at, :] + lrecv[at, :].astype(F32)).astype(BF)
        go = copy(sem(), lysend.at[r - 1], lyrecv.at[r - 1], hpeer[r])
        go.start()
        l_waits.append(go)
    pending += l_waits

    row_ids = lax.broadcasted_iota(jnp.int32, (OWN, GROUP), 0) + (32 * c + OWN * h)
    col_ids = lax.broadcasted_iota(jnp.int32, (OWN, GROUP), 1)
    own_id = jnp.sum(jnp.where(row_ids == col_ids, kid[...].astype(F32), 0.0), axis=1, keepdims=True)
    one = jnp.ones_like(own_id)
    own_digit = digits(own_id)
    own_ext = on_lanes(list(own_digit) + [g * g for g in own_digit] + [one] * 3, OWN)
    kmsg[:, E:] = own_ext

    at = lax.broadcasted_iota(jnp.int32, (2 * HP, LOG), 0)
    upper = at >= HP
    inside = jnp.where(upper, at - HP, at)
    at = jnp.where(inside < HALF, jnp.where(upper, inside + HALF, inside), -1)
    col = lax.broadcasted_iota(jnp.int32, (2 * HP, LOG), 1)
    log_id = jnp.sum(jnp.where(at == col, lid[...].astype(F32), 0.0), axis=1, keepdims=True)
    one = jnp.ones_like(log_id)
    log_digit = digits(log_id)
    lext[...] = on_lanes([-2.0 * g for g in log_digit] + [one] * 3 + [g * g for g in log_digit], 2 * HP).astype(BF)

    own = kacc[rows(32 * c + OWN * h, OWN, OWN), :] + krecv[rows(OWN * h, OWN, OWN), :]
    for go in waits:
        go.wait_recv()
    own = own + kyrecv[0] + kyrecv[1] + kyrecv[2]
    k_inv = lax.rsqrt(jnp.sum(own * own, axis=1, keepdims=True) + EPS)
    unit = own * k_inv
    kunit[...] = unit
    kmsg[:, :E] = unit.astype(BF).astype(F32)
    y_copy = copy(sem(), kmsg, kgot, other_y)
    y_copy.start()
    pending.append(y_copy)
    y_copy.wait_recv()

    both = jnp.concatenate([jnp.where(y == 0, kmsg[...], kgot[...]), jnp.where(y == 0, kgot[...], kmsg[...])], axis=0)
    both = both.astype(BF)

    at_zx = [lambda zz, xx: 64 * zz + 16 * xx, lambda zz, xx: 128 * xx + 16 * zz]
    first = {0: [], 1: []}
    second = {0: [], 1: []}

    def direct_gather(core, peer, position):
        base = rows(at_zx[core](z, x), 16, 16)
        kall[base, :] = both
        for r in range(1, len(peer)):
            go = copy(first[core][r - 1], kall.at[base, :], kall.at[base, :], peer[r])
            go.start()

    def direct_gather_recv(core, come):
        for r in range(1, len(come)):
            base = rows(at_zx[core](z, come[r]) if core == 0 else at_zx[core](come[r], x), 16, 16)
            copy(first[core][r - 1], kall.at[base, :], kall.at[base, :], partner).wait_recv()

    def direct_gather_sent(core, peer):
        base = rows(at_zx[core](z, x), 16, 16)
        for r in range(1, len(peer)):
            copy(first[core][r - 1], kall.at[base, :], kall.at[base, :], peer[r]).wait_send()

    first[0] = [sem() for _ in range(NX - 1)]
    first[1] = [sem() for _ in range(NZ - 1)]

    @pl.when(c == 0)
    def _():
        direct_gather(0, xpeer, x)

    @pl.when(c == 1)
    def _():
        direct_gather(1, zpeer, z)

    def ring_steps(n, size):
        half = n // 2
        steps = []
        for s in range(half):
            whole = s < half - 1
            steps.append((s, (0, size) if whole else (0, size // 2), (0, size) if whole else (size // 2, size // 2)))
        return steps

    class Ring:
        def __init__(self, n, at, size, peer):
            self.n, self.at, self.size, self.peer = n, at, size, peer
            self.steps = ring_steps(n, size)
            self.right = [sem() for _ in self.steps]
            self.left = [sem() for _ in self.steps]

        def block(self, which, part):
            return kall.at[rows(self.size * mod(which + self.n, self.n) + part[0], part[1], 16), :]

        def start(self, s):
            _, right, left = self.steps[s]
            ref = self.block(self.at - s, right)
            copy(self.right[s], ref, ref, self.peer[1]).start()
            ref = self.block(self.at + s, left)
            copy(self.left[s], ref, ref, self.peer[self.n - 1]).start()

        def recv(self, s):
            _, right, left = self.steps[s]
            ref = self.block(self.at - 1 - s, right)
            copy(self.right[s], ref, ref, self.peer[1]).wait_recv()
            ref = self.block(self.at + 1 + s, left)
            copy(self.left[s], ref, ref, self.peer[self.n - 1]).wait_recv()

        def sent(self):
            for s, right, left in self.steps:
                ref = self.block(self.at - s, right)
                copy(self.right[s], ref, ref, self.peer[1]).wait_send()
                ref = self.block(self.at + s, left)
                copy(self.left[s], ref, ref, self.peer[self.n - 1]).wait_send()

    ring = [Ring(NZ, z, 64, zpeer), Ring(NX, x, 128, xpeer)]

    @pl.when(c == 0)
    def _():
        direct_gather_recv(0, xfrom)
        ring[0].start(0)

    @pl.when(c == 1)
    def _():
        direct_gather_recv(1, zfrom)
        ring[1].start(0)

    mine = rows(BLK * h, BLK, 16)
    for go in l_waits:
        go.wait_recv()
    row = lacc[mine, :] + lrecv[mine, :].astype(F32)
    for r in range(NH - 1):
        row = row + lyrecv[r].astype(F32)
    l_inv = lax.rsqrt(jnp.sum(row * row, axis=1, keepdims=True) + EPS)
    row = row * l_inv
    lunit[...] = row

    def spread(buffer, value):
        mine = rows(HP * c + BLK * h, BLK, 16)
        buffer[mine, :] = value
        ref = buffer.at[mine, :]
        along = []
        across = []
        for r in (2, 1, 3):
            go = copy(sem(), ref, ref, hpeer[r])
            go.start()
            come = buffer.at[rows(HP * c + BLK * hfrom[r], BLK, 16), :]
            along.append((r, go, come))
        go = copy(sem(), ref, ref, partner)
        go.start()
        across.append((0, go))
        pending.extend([g for _, g, _ in along] + [go])
        return along, across

    def spread_end(buffer, along, across):
        for r, go, come in along[1:] + along[:1]:
            go.wait_recv()
            on = copy(sem(), come, come, partner)
            on.start()
            across.append((r, on))
            pending.append(on)
        for r, on in across:
            ref = buffer.at[rows(HP * (1 - c) + BLK * hfrom[r], BLK, 16), :]
            on.wait_recv()

    l_along, l_across = spread(lall, row.astype(BF))

    @pl.when(c == 0)
    def _():
        for s in range(1, NZ // 2):
            ring[0].recv(s - 1)
            ring[0].start(s)

    @pl.when(c == 1)
    def _():
        for s in range(1, NX // 2):
            ring[1].recv(s - 1)
            ring[1].start(s)

    spread_end(lall, l_along, l_across)

    @pl.when(c == 0)
    def _():
        ring[0].recv(NZ // 2 - 1)

    @pl.when(c == 1)
    def _():
        ring[1].recv(NX // 2 - 1)

    def kpi_side(i, carry):
        at = rows(i * 128, 128, 128)
        inner = dot_t(kall[at, :E], lall[...])
        apart = dot_t(kall[at, E:], lext[...])
        kg[at, :] = dot(pair_gradient(inner, apart), lall[...])
        return carry

    lax.fori_loop(0, COUNT // 128, kpi_side, 0)

    class Sum:
        def __init__(self, n, at, size, peer, bufs):
            self.n, self.at, self.size, self.peer = n, at, size, peer
            self.rs, self.rr, self.ls, self.lr = bufs
            self.right = [sem() for _ in range(n // 2)]
            self.left = [sem() for _ in range(n // 2)]

        def part(self, which, start, size):
            return kg[rows(self.size * mod(which + self.n, self.n) + start, size, 16), :]

        def copies(self, s):
            half = self.size // 2
            right, left = (pl.ds(0, half), pl.ds(half, half)) if s == 0 else (pl.ds(0, self.size),) * 2
            return (
                copy(self.right[s], self.rs.at[s, right], self.rr.at[s, right], self.peer[1]),
                copy(self.left[s], self.ls.at[s, left], self.lr.at[s, left], self.peer[self.n - 1]),
            )

        def start(self, s):
            n, half = self.n, self.size // 2
            right, left = self.copies(s)
            if s == 0:
                self.rs[0, :half] = self.part(self.at + n // 2, 0, half).astype(BF)
                self.ls[0, half:] = self.part(self.at + n // 2, half, half).astype(BF)
            elif s == 1:
                to = self.at + n // 2 - 1
                self.rs[1, :half] = (self.part(to, 0, half) + self.rr[0, :half].astype(F32)).astype(BF)
                self.rs[1, half:] = self.part(to, half, half).astype(BF)
                right.start()
                to = self.at - n // 2 + 1
                self.ls[1, :half] = self.part(to, 0, half).astype(BF)
                self.ls[1, half:] = (self.part(to, half, half) + self.lr[0, half:].astype(F32)).astype(BF)
                left.start()
                return
            else:
                to = self.at + n // 2 - s
                self.rs[s] = (self.part(to, 0, self.size) + self.rr[s - 1].astype(F32)).astype(BF)
                right.start()
                to = self.at - n // 2 + s
                self.ls[s] = (self.part(to, 0, self.size) + self.lr[s - 1].astype(F32)).astype(BF)
                left.start()
                return
            right.start()
            left.start()

        def recv(self, s):
            for go in self.copies(s):
                go.wait_recv()

        def result(self):
            last = self.n // 2 - 1
            return self.part(self.at, 0, self.size) + self.rr[last].astype(F32) + self.lr[last].astype(F32)

        def sent(self):
            for s in range(self.n // 2):
                for go in self.copies(s):
                    go.wait_send()

    sums = [Sum(NZ, z, 64, zpeer, (zrs, zrr, zls, zlr)), Sum(NX, x, 128, xpeer, (xrs, xrr, xls, xlr))]
    mid_sem = [[sem() for _ in range(NX - 1)], [sem() for _ in range(NZ - 1)]]

    @pl.when(c == 0)
    def _():
        sums[0].start(0)

    @pl.when(c == 1)
    def _():
        sums[1].start(0)

    def log_pairs(i, carry):
        at = rows(i * 128, 128, 128)
        inner = dot_t(lall[...], kall[at, :E])
        apart = dot_t(lext[...], kall[at, E:])
        pg[:, at] = pair_gradient(inner, apart)
        return carry

    lax.fori_loop(0, COUNT // 128, log_pairs, 0)
    gsend[...] = dot(pg[rows(HP * (1 - c), HP, 16), :], kall[:, :E]).astype(BF)
    g_core = copy(sem(), gsend, grecv, partner)
    g_core.start()
    pending.append(g_core)

    @pl.when(c == 0)
    def _():
        sums[0].recv(0)
        sums[0].start(1)

    @pl.when(c == 1)
    def _():
        sums[1].recv(0)
        sums[1].start(1)

    lg[...] = dot(pg[rows(HP * c, HP, 16), :], kall[:, :E])

    g_core.wait_recv()
    g_waits = []
    for r in (2, 1, 3):
        at = rows(BLK * mod(h + r, NH), BLK, 16)
        gysend[r - 1] = (lg[at, :] + grecv[at, :].astype(F32)).astype(BF)
        go = copy(sem(), gysend.at[r - 1], gyrecv.at[r - 1], hpeer[r])
        go.start()
        g_waits.append(go)
    pending += g_waits

    def middle(core, peer, go_first):
        for r in range(1, len(peer)):
            if go_first:
                to = mod((x if core == 0 else z) + r, len(peer))
                midsend[r - 1] = mid[rows(16 * to, 16, 16), :].astype(BF)
            go = copy(mid_sem[core][r - 1], midsend.at[r - 1], midrecv.at[r - 1], peer[r])
            if go_first:
                go.start()
            else:
                go.wait_send()

    def middle_end(core, peer):
        total = mid[rows(16 * (x if core == 0 else z), 16, 16), :]
        for r in range(1, len(peer)):
            copy(mid_sem[core][r - 1], midsend.at[r - 1], midrecv.at[r - 1], peer[r]).wait_recv()
            total = total + midrecv[r - 1].astype(F32)
        mid16[...] = total

    @pl.when(c == 0)
    def _():
        for s in range(1, NZ // 2):
            sums[0].recv(s)
            if s < NZ // 2 - 1:
                sums[0].start(s + 1)
        mid[:64, :] = sums[0].result()
        middle(0, xpeer, True)
        middle_end(0, xpeer)

    @pl.when(c == 1)
    def _():
        for s in range(1, NX // 2):
            sums[1].recv(s)
            if s < NX // 2 - 1:
                sums[1].start(s + 1)
        mid[...] = sums[1].result()
        middle(1, zpeer, True)
        middle_end(1, zpeer)

    ymsg[...] = mid16[rows(OWN * (1 - y), OWN, OWN), :]
    y_back = copy(sem(), ymsg, ygot, other_y)
    y_back.start()
    pending.append(y_back)

    y_back.wait_recv()
    total = mid16[rows(OWN * y, OWN, OWN), :] + ygot[...]
    unit = kunit[...]
    inner = jnp.sum(unit * total, axis=1, keepdims=True)
    mine8 = rows(32 * c + OWN * h, OWN, OWN)
    kback[mine8, :] = (k_inv * (total - unit * inner)).astype(BF).astype(F32)
    kb_waits = []
    for r in (2, 1, 3):
        go = copy(sem(), kback.at[mine8, :], kback.at[mine8, :], hpeer[r])
        go.start()
        kb_waits.append(go)
    pending += kb_waits

    for go in g_waits:
        go.wait_recv()
    row = lg[mine, :] + grecv[mine, :].astype(F32)
    for r in range(NH - 1):
        row = row + gyrecv[r].astype(F32)
    unit = lunit[...]
    inner = jnp.sum(unit * row, axis=1, keepdims=True)
    b_along, b_across = spread(back, (l_inv * (row - unit * inner)).astype(BF))

    for go in kb_waits:
        go.wait_recv()
    half = kback.at[rows(32 * c, 32, 32), :]
    kb_core = copy(sem(), half, half, partner)
    kb_core.start()
    pending.append(kb_core)
    kb_core.wait_recv()

    part = lax.dot_general(
        kf[...], kback[...].astype(BF), (((0,), (0,)), ((), ())), preferred_element_type=F32
    ).astype(BF)
    tall = part.shape[0]
    for j in range(E // 128):
        wbuf[tall * j : tall * (j + 1), :] = part[:, 128 * j : 128 * (j + 1)]
    wbuf[tall * (E // 128) :, :] = jnp.zeros((NZ * WROWS - tall * (E // 128), 128), BF)
    w_waits = []
    for r in (4, 3, 5, 2, 6, 1, 7):
        go = copy(sem(), wbuf.at[rows(WROWS * mod(z + r, NZ), WROWS, 16), :], wzr.at[r - 1], zpeer[r])
        go.start()
        w_waits.append(go)
    pending += w_waits

    spread_end(back, b_along, b_across)
    for i in range(2):
        out_g[HALF * i : HALF * (i + 1), :] = dot_t(back[HP * i : HP * i + HALF, :], lp[...]).astype(BF)

    total = wbuf[rows(WROWS * z, WROWS, 16), :].astype(F32)
    for go in w_waits:
        go.wait_recv()
    for r in range(NZ - 1):
        total = total + wzr[r].astype(F32)
    wx[x] = total.astype(BF)
    x_waits = []
    for r in (2, 1, 3):
        go = copy(sem(), wx.at[x], wx.at[x], xpeer[r])
        go.start()
        x_waits.append(go)
    pending += x_waits
    for go in x_waits:
        go.wait_recv()
    total = wx[0].astype(F32)
    for i in range(1, NX):
        total = total + wx[i].astype(F32)
    wy[y] = total.astype(BF)
    go = copy(sem(), wy.at[y], wy.at[y], other_y)
    go.start()
    pending.append(go)
    go.wait_recv()
    share = rows(WROWS * z, WROWS, 16)
    wall[share, :] = (wy[0].astype(F32) + wy[1].astype(F32)).astype(BF)
    w_waits = []
    for r in (4, 3, 5, 2, 6, 1, 7):
        go = copy(sem(), wall.at[share, :], wall.at[share, :], zpeer[r])
        go.start()
        w_waits.append(go)
    pending += w_waits
    for go in w_waits:
        go.wait_recv()
    for j in range(E // 128):
        out_w[:, 128 * j : 128 * (j + 1)] = wall[tall * j : tall * (j + 1), :].astype(F32)

    for go in pending:
        go.wait_send()

    @pl.when(c == 0)
    def _():
        direct_gather_sent(0, xpeer)
        ring[0].sent()
        sums[0].sent()
        middle(0, xpeer, False)

    @pl.when(c == 1)
    def _():
        direct_gather_sent(1, zpeer)
        ring[1].sent()
        sums[1].sent()
        middle(1, zpeer, False)

    assert used[0] <= NSEM


def body(log_feats, kpi_feats, log_proj, kpi_proj, log_ids, kpi_ids):
    v = pltpu.VMEM
    scratch = [
        v((HP, E), BF), v((HP, E), BF), v((HP, E), F32), v((3, BLK, E), BF), v((3, BLK, E), BF),
        v((2 * HP, E), BF), v((BLK, E), F32), v((2 * HP, ID), BF),
        v((GROUP, E), F32), v((32, E), F32), v((32, E), F32), v((3, OWN, E), F32), v((3, OWN, E), F32),
        v((OWN, EK), F32), v((OWN, EK), F32), v((COUNT, EK), BF), v((OWN, E), F32),
        v((2 * HP, COUNT), BF), v((COUNT, E), F32), v((HP, E), F32),
        v((HP, E), BF), v((HP, E), BF), v((3, BLK, E), BF), v((3, BLK, E), BF), v((2 * HP, E), BF),
        v((4, 64, E), BF), v((4, 64, E), BF), v((4, 64, E), BF), v((4, 64, E), BF),
        v((2, 128, E), BF), v((2, 128, E), BF), v((2, 128, E), BF), v((2, 128, E), BF),
        v((128, E), F32), v((7, 16, E), BF), v((7, 16, E), BF), v((16, E), F32), v((OWN, E), F32), v((OWN, E), F32),
        v((GROUP, E), F32), v((NZ * WROWS, 128), BF), v((NZ - 1, WROWS, 128), BF), v((NX, WROWS, 128), BF),
        v((NY, WROWS, 128), BF), v((NZ * WROWS, 128), BF),
        pltpu.SemaphoreType.DMA((NSEM,)), pltpu.SemaphoreType.DMA((NSEM,)),
    ]
    return pl.pallas_call(
        kernel,
        out_shape=(
            jax.ShapeDtypeStruct(log_feats.shape, BF),
            jax.ShapeDtypeStruct(kpi_proj.shape, F32),
        ),
        in_specs=[pl.BlockSpec(memory_space=v)] * 6,
        out_specs=(pl.BlockSpec(memory_space=v),) * 2,
        scratch_shapes=scratch,
        compiler_params=pltpu.CompilerParams(
            collective_id=0, has_side_effects=True, vmem_limit_bytes=48 * 1024 * 1024
        ),
    )(log_feats, kpi_feats, log_proj, kpi_proj, log_ids.reshape(1, -1), kpi_ids.reshape(1, -1))


def solution(mesh):
    return jax.shard_map(
        body,
        mesh=mesh,
        in_specs=(
            P("dp", "tensor"),
            P("dp", "tensor"),
            P("tensor", None),
            P("tensor", None),
            P("dp"),
            P("dp"),
        ),
        out_specs=(P("dp", "tensor"), P("tensor", None)),
        check_vma=False,
    )
```

```python
import jax
import jax.numpy as jnp
from jax import lax
from jax.experimental import pallas as pl
from jax.experimental.pallas import tpu as pltpu
from jax.sharding import PartitionSpec as P

TEMPER = 32.0
BIAS = -2.0
LOSS = 4096.0
EPS = 1e-06
MESH = pl.DeviceIdType.MESH
BF = jnp.bfloat16
F32 = jnp.float32

NY, NX, NZ, NH = 2, 4, 8, 4
LOG = 352
HALF = LOG // 2
BLK = 48
HP = NH * BLK
E = 1152
ID = 128
EK = E + ID
GROUP = 64
OWN = 8
COUNT = NY * NX * NZ * OWN
SCALE = TEMPER * LOSS / (LOG * NY * NX * NZ)
PK = EK // 2
CUT = 32
WZ, WX = 176, 336
XS, ZS = (2, 1, 3), (4, 3, 5, 2, 6, 1, 7)
NSEM = 160


def dot(a, b):
    return jnp.dot(a, b, preferred_element_type=F32)


def dot_t(a, b):
    return lax.dot_general(a, b, (((1,), (1,)), ((), ())), preferred_element_type=F32)


def mod(a, n):
    return lax.rem(a, jnp.int32(n))


def digits(ids):
    high = jnp.floor(ids * (1.0 / 256.0))
    rest = ids - 256.0 * high
    middle = jnp.floor(rest * (1.0 / 16.0))
    return high, middle, rest - 16.0 * middle


def on_lanes(values, rows):
    lane = lax.broadcasted_iota(jnp.int32, (rows, ID), 1)
    out = jnp.zeros((rows, ID), F32)
    for at, value in enumerate(values):
        out = jnp.where(lane == at, value, out)
    return out


def pair_gradient(inner, apart):
    sign = jnp.where(apart < 0.5, 1.0, -1.0).astype(F32)
    margin = -sign * (TEMPER * inner + BIAS)
    return (-SCALE * sign * jax.nn.sigmoid(margin)).astype(BF)


def kernel(
    lf_h, kf_h, lp_h, kp_h, lid_h, kid_h, out_g, out_w,
    lf, kf, lp, kp, lid, kid, og, ow,
    lsend, lrecv, lacc, lrs, lrr, lls, llr, lall, lunit, lext,
    kacc, ksend, krecv, kysend, kyrecv, kmsg, kgot, kall, kunit,
    pg, kg, lg, gsend, grecv, grs, grr, gls, glr, back,
    zrs, zrr, zls, zlr, xrs, xrr, xls, xlr, mid, midsend, midrecv, mid16, ymsg, ygot,
    kback, wbuf, wzr, wxr, wx, wy, wxs, wxzr, wys, wxz, wall,
    ssem, rsem, lsem,
):
    d = lax.axis_index("dp")
    t = lax.axis_index("tensor")
    y = lax.div(d, jnp.int32(NX * NZ))
    x = mod(lax.div(d, jnp.int32(NZ)), NX)
    z = mod(d, NZ)
    h = lax.div(t, jnp.int32(2))
    c = mod(t, 2)

    def place(y=y, x=x, z=z, h=h, c=c):
        return {"dp": (y * NX + x) * NZ + z, "tensor": h * 2 + c}

    def rows(start, size, unit=16):
        return pl.ds(pl.multiple_of(start, unit), size)

    started = []

    class Send:
        def __init__(self, src, dst, to, land=None, core=None):
            self.src, self.dst, self.to, self.core = src, dst, to, core
            self.land = land or dst
            self.at = len(started)
            self.open, self.begun = True, False
            started.append(self)
            assert self.at < NSEM

        def copy(self, src, dst):
            return pltpu.make_async_remote_copy(
                src_ref=src(), dst_ref=dst(), send_sem=ssem.at[self.at], recv_sem=rsem.at[self.at],
                device_id=self.to, device_id_type=MESH,
            )

        def start(self):
            self.begun = True
            self.copy(self.src, self.dst).start()

        def recv(self):
            self.open = False
            self.copy(self.land, self.land).wait_recv()

        def sent(self):
            self.copy(self.src, self.dst).wait_send()

    def finish():
        for core in (None, 0, 1):

            def ends(core=core):
                for go in started:
                    if go.core == core and go.begun:
                        if go.open:
                            go.recv()
                        go.sent()

            if core is None:
                ends()
            else:
                pl.when(c == core)(ends)

    inputs = [
        pltpu.make_async_copy(a, b, lsem.at[i])
        for i, (a, b) in enumerate(((kf_h, kf), (kp_h, kp), (lf_h, lf), (lp_h, lp), (kid_h, kid), (lid_h, lid)))
    ]
    for go in inputs:
        go.start()

    partner = place(c=1 - c)
    other_y = place(y=1 - y)
    hpeer = [place(h=mod(h + r, NH)) for r in range(NH)]
    hfrom = [mod(h + NH - r, NH) for r in range(NH)]
    xpeer = [place(x=mod(x + r, NX)) for r in range(NX)]
    xfrom = [mod(x + NX - r, NX) for r in range(NX)]
    zpeer = [place(z=mod(z + r, NZ)) for r in range(NZ)]
    zfrom = [mod(z + NZ - r, NZ) for r in range(NZ)]

    barrier = pltpu.get_barrier_semaphore()
    peers = [partner, other_y] + hpeer[1:] + xpeer[1:] + zpeer[1:]
    for device in peers:
        pl.semaphore_signal(barrier, inc=1, device_id=device, device_id_type=MESH)

    def on_core(run):
        for core in (0, 1):
            pl.when(c == core)(lambda core=core: run(core))

    def packed(v):
        if v.shape[1] < EK:
            v = jnp.concatenate([v, jnp.zeros((OWN, EK - v.shape[1]), F32)], axis=1)
        return jnp.concatenate([v[:, :PK], v[:, PK:]], axis=0).astype(BF)

    def unpacked(v):
        v = v.astype(F32)
        return jnp.concatenate([v[:OWN], v[OWN:]], axis=1)

    class Gather:
        def __init__(self, n, at, size, split, right, left, block, sign=1, core=None):
            self.n, self.go = n, []
            whole = [((0, size), (0, size))] * (n // 2 - 1)
            for s, (a, b) in enumerate(whole + [((0, split), (split, size - split))]):
                there, here = block(at - sign * s, a), block(at - sign * (s + 1), a)
                one = Send(there, there, right, here, core)
                there, here = block(at + sign * s, b), block(at + sign * (s + 1), b)
                self.go.append((one, Send(there, there, left, here, core)))

        def start(self, s):
            for go in self.go[s]:
                go.start()

        def recv(self, s):
            for go in self.go[s]:
                go.recv()

    class Sum:
        def __init__(self, n, at, size, split, right, left, part, bufs, sign=1, core=None):
            self.n, self.at, self.size, self.split, self.part, self.sign = n, at, size, split, part, sign
            self.rs, self.rr, self.ls, self.lr = bufs
            self.go = []
            for s in range(n // 2):
                parts = ((0, split), (split, size - split)) if s == 0 else ((0, size), (0, size))
                pair = []
                for p, send, come, to in ((parts[0], self.rs, self.rr, right), (parts[1], self.ls, self.lr, left)):
                    src = lambda s=s, p=p, send=send: send.at[s, pl.ds(*p)]
                    dst = lambda s=s, p=p, come=come: come.at[s, pl.ds(*p)]
                    pair.append(Send(src, dst, to, core=core))
                self.go.append(pair)

        def start(self, s):
            k, size, part = self.split, self.size, self.part
            away = self.n // 2 - s
            to = self.at + self.sign * away
            if s == 0:
                self.rs[0, :k] = part(to, 0, k).astype(BF)
                self.go[0][0].start()
                self.ls[0, k:] = part(to, k, size - k).astype(BF)
                self.go[0][1].start()
                return
            if s == 1:
                self.rs[1, :k] = (part(to, 0, k) + self.rr[0, :k].astype(F32)).astype(BF)
                self.rs[1, k:] = part(to, k, size - k).astype(BF)
            else:
                self.rs[s] = (part(to, 0, size) + self.rr[s - 1].astype(F32)).astype(BF)
            self.go[s][0].start()
            to = self.at - self.sign * away
            if s == 1:
                self.ls[1, :k] = part(to, 0, k).astype(BF)
                self.ls[1, k:] = (part(to, k, size - k) + self.lr[0, k:].astype(F32)).astype(BF)
            else:
                self.ls[s] = (part(to, 0, size) + self.lr[s - 1].astype(F32)).astype(BF)
            self.go[s][1].start()

        def recv(self, s):
            for go in self.go[s]:
                go.recv()

        def result(self):
            last = self.n // 2 - 1
            return self.part(self.at, 0, self.size) + self.rr[last].astype(F32) + self.lr[last].astype(F32)

    turn = 1 - 2 * c
    h_right = place(h=mod(h + turn + NH, NH))
    h_left = place(h=mod(h - turn + NH, NH))

    def h_sum(own, come, bufs):
        def part(which, start, size):
            at = rows(BLK * mod(which + NH, NH) + start, size)
            return own[at, :] + come[at, :].astype(F32)

        return Sum(NH, h, BLK, CUT, h_right, h_left, part, bufs, turn)

    class Spread:
        def __init__(self, buffer):
            self.buffer = buffer

            def at_core(core):
                def block(hh, part=(0, BLK)):
                    return lambda: buffer.at[rows(HP * core + BLK * mod(hh + NH, NH) + part[0], part[1]), :]

                return block

            mine, other = at_core(c), at_core(1 - c)
            self.along = Gather(NH, h, BLK, CUT, h_right, h_left, mine, turn)
            self.across = {r: Send(mine(h - r), mine(h - r), partner, other(h - r)) for r in (0, 1, 3, 2)}

        def start(self, value):
            self.buffer[rows(HP * c + BLK * h, BLK), :] = value
            self.along.start(0)
            self.across[0].start()

        def step(self):
            self.along.recv(0)
            self.along.start(1)
            self.across[1].start()
            self.across[3].start()

        def last(self):
            self.along.recv(1)
            self.across[2].start()

        def end(self):
            for go in self.across.values():
                go.recv()

    inputs[0].wait()
    inputs[1].wait()
    kacc[...] = dot(kf[...], kp[...])
    ksend[...] = kacc[rows(32 * (1 - c), 32, 32), :].astype(BF)
    inputs[2].wait()
    inputs[3].wait()
    lsend[:HALF, :] = dot(lf[rows(HALF * (1 - c), HALF), :], lp[...]).astype(BF)
    lsend[HALF:, :] = jnp.zeros((HP - HALF, E), BF)
    inputs[4].wait()
    inputs[5].wait()

    pl.semaphore_wait(barrier, len(peers))
    k_core = Send(lambda: ksend, lambda: krecv, partner)
    k_core.start()
    l_core = Send(lambda: lsend, lambda: lrecv, partner)
    l_core.start()

    lacc[:HALF, :] = dot(lf[rows(HALF * c, HALF), :], lp[...])
    lacc[HALF:, :] = jnp.zeros((HP - HALF, E), F32)

    def k_part(to):
        return kacc[rows(32 * c + OWN * to, OWN, OWN), :]

    k_core.recv()
    kacc[rows(32 * c, 32, 32), :] += krecv[...].astype(F32)
    k_waits = []
    for r in (2, 1, 3):
        kysend[r - 1] = packed(k_part(mod(h + r, NH)))
        go = Send(lambda r=r: kysend.at[r - 1], lambda r=r: kyrecv.at[r - 1], hpeer[r])
        go.start()
        k_waits.append(go)

    l_sum = h_sum(lacc, lrecv, (lrs, lrr, lls, llr))
    l_core.recv()
    l_sum.start(0)

    row_ids = lax.broadcasted_iota(jnp.int32, (OWN, GROUP), 0) + (32 * c + OWN * h)
    col_ids = lax.broadcasted_iota(jnp.int32, (OWN, GROUP), 1)
    own_id = jnp.sum(jnp.where(row_ids == col_ids, kid[...].astype(F32), 0.0), axis=1, keepdims=True)
    one = jnp.ones_like(own_id)
    own_digit = digits(own_id)
    k_ext = on_lanes(list(own_digit) + [g * g for g in own_digit] + [one] * 3, OWN)

    l_sum.recv(0)
    l_sum.start(1)

    own = k_part(h)
    for go in k_waits:
        go.recv()
    for r in range(NH - 1):
        own = own + unpacked(kyrecv[r])[:, :E]
    k_inv = lax.rsqrt(jnp.sum(own * own, axis=1, keepdims=True) + EPS)
    unit = own * k_inv
    kunit[...] = unit
    kmsg[...] = packed(jnp.concatenate([unit, k_ext], axis=1))
    y_copy = Send(lambda: kmsg, lambda: kgot, other_y)
    y_copy.start()

    at = lax.broadcasted_iota(jnp.int32, (2 * HP, LOG), 0)
    upper = at >= HP
    inside = jnp.where(upper, at - HP, at)
    at = jnp.where(inside < HALF, jnp.where(upper, inside + HALF, inside), -1)
    col = lax.broadcasted_iota(jnp.int32, (2 * HP, LOG), 1)
    log_id = jnp.sum(jnp.where(at == col, lid[...].astype(F32), 0.0), axis=1, keepdims=True)
    one = jnp.ones_like(log_id)
    log_digit = digits(log_id)
    lext[...] = on_lanes([-2.0 * g for g in log_digit] + [one] * 3 + [g * g for g in log_digit], 2 * HP).astype(BF)

    y_copy.recv()
    sent, got = unpacked(kmsg[...]), unpacked(kgot[...])
    both = jnp.concatenate([jnp.where(y == 0, sent, got), jnp.where(y == 0, got, sent)], axis=0).astype(BF)

    def block0(zz, xx):
        return kall.at[rows(64 * zz + 16 * xx, 16), :]

    def block1(zz, xx):
        return kall.at[rows(128 * xx + 16 * zz, 16), :]

    own0 = lambda: block0(z, x)
    own1 = lambda: block1(z, x)
    first = [
        [Send(own0, own0, xpeer[r], lambda r=r: block0(z, xfrom[r]), 0) for r in XS],
        [Send(own1, own1, zpeer[r], lambda r=r: block1(zfrom[r], x), 1) for r in ZS],
    ]

    def k_block(n, size):
        return lambda which, part: lambda: kall.at[rows(size * mod(which + n, n) + part[0], part[1]), :]

    ring = [
        Gather(NZ, z, 64, 32, zpeer[1], zpeer[NZ - 1], k_block(NZ, 64), core=0),
        Gather(NX, x, 128, 64, xpeer[1], xpeer[NX - 1], k_block(NX, 128), core=1),
    ]

    @on_core
    def _(core):
        base = rows(64 * z + 16 * x, 16) if core == 0 else rows(128 * x + 16 * z, 16)
        kall[base, :] = both
        for go in first[core]:
            go.start()

    @on_core
    def _(core):
        for go in first[core]:
            go.recv()
        ring[core].start(0)


    l_sum.recv(1)
    row = l_sum.result()
    l_inv = lax.rsqrt(jnp.sum(row * row, axis=1, keepdims=True) + EPS)
    row = row * l_inv
    lunit[...] = row
    l_spread = Spread(lall)
    l_spread.start(row.astype(BF))

    @on_core
    def _(core):
        for s in range(1, ring[core].n // 2):
            ring[core].recv(s - 1)
            ring[core].start(s)

    l_spread.step()
    l_spread.last()

    @on_core
    def _(core):
        ring[core].recv(ring[core].n // 2 - 1)

    l_spread.end()

    lead = jnp.where(c == 0, lax.div(mod(z + NZ // 2, NZ), jnp.int32(2)), mod(x + NX // 2, NX))

    def kpi_side(i, carry):
        at = rows(mod(lead + i, 4) * 128, 128, 128)
        inner = dot_t(kall[at, :E], lall[...])
        apart = dot_t(kall[at, E:], lext[...])
        kg[at, :] = dot(pair_gradient(inner, apart), lall[...])
        return carry

    def k_part_of(n, size):
        return lambda which, start, count: kg[rows(size * mod(which + n, n) + start, count), :]

    sums = [
        Sum(NZ, z, 64, 32, zpeer[1], zpeer[NZ - 1], k_part_of(NZ, 64), (zrs, zrr, zls, zlr), core=0),
        Sum(NX, x, 128, 64, xpeer[1], xpeer[NX - 1], k_part_of(NX, 128), (xrs, xrr, xls, xlr), core=1),
    ]

    def step(s):
        @on_core
        def _(core):
            if s < sums[core].n // 2:
                if s > 0:
                    sums[core].recv(s - 1)
                sums[core].start(s)

    kpi_side(0, 0)
    step(0)
    lax.fori_loop(1, COUNT // 128, kpi_side, 0)
    step(1)

    def log_pairs(i, carry):
        at = rows(i * 256, 256, 256)
        inner = dot_t(lall[...], kall[at, :E])
        apart = dot_t(lext[...], kall[at, E:])
        pg[:, at] = pair_gradient(inner, apart)
        return carry

    lax.fori_loop(0, COUNT // 256, log_pairs, 0)
    gsend[...] = dot(pg[rows(HP * (1 - c), HP), :], kall[:, :E]).astype(BF)
    g_core = Send(lambda: gsend, lambda: grecv, partner)
    g_core.start()
    step(2)
    lg[...] = dot(pg[rows(HP * c, HP), :], kall[:, :E])

    g_sum = h_sum(lg, grecv, (grs, grr, gls, glr))
    g_core.recv()
    g_sum.start(0)
    step(3)

    middle = [
        [Send(lambda r=r: midsend.at[r - 1], lambda r=r: midrecv.at[r - 1], xpeer[r], core=0) for r in XS],
        [Send(lambda r=r: midsend.at[r - 1], lambda r=r: midrecv.at[r - 1], zpeer[r], core=1) for r in ZS],
    ]

    g_sum.recv(0)
    g_sum.start(1)

    @on_core
    def _(core):
        at, order = ((x, XS), (z, ZS))[core]
        n = len(order) + 1
        sums[core].recv(sums[core].n // 2 - 1)
        mid[: 16 * n, :] = sums[core].result()
        for r, go in zip(order, middle[core]):
            midsend[r - 1] = mid[rows(16 * mod(at + r, n), 16), :].astype(BF)
            go.start()
        total = mid[rows(16 * at, 16), :]
        for go in middle[core]:
            go.recv()
        for r in range(n - 1):
            total = total + midrecv[r].astype(F32)
        mid16[...] = total

    ymsg[...] = packed(mid16[rows(OWN * (1 - y), OWN, OWN), :])
    y_back = Send(lambda: ymsg, lambda: ygot, other_y)
    y_back.start()
    y_back.recv()
    total = mid16[rows(OWN * y, OWN, OWN), :] + unpacked(ygot[...])[:, :E]
    unit = kunit[...]
    inner = jnp.sum(unit * total, axis=1, keepdims=True)
    kback[c * NH + h] = packed(k_inv * (total - unit * inner))

    def kblock(hh):
        return lambda: kback.at[c * NH + hh]

    kb_waits = [Send(kblock(h), kblock(h), hpeer[r], kblock(hfrom[r])) for r in (2, 1, 3)]
    for go in kb_waits:
        go.start()

    g_sum.recv(1)
    row = g_sum.result()
    unit = lunit[...]
    inner = jnp.sum(unit * row, axis=1, keepdims=True)
    row = (l_inv * (row - unit * inner)).astype(BF)

    def khalf(core):
        return lambda: kback.at[pl.ds(core * NH, NH)]

    for go in kb_waits:
        go.recv()
    kb_core = Send(khalf(c), khalf(c), partner, khalf(1 - c))
    kb_core.start()
    b_spread = Spread(back)
    b_spread.start(row)
    kb_core.recv()

    rows_back = jnp.concatenate([unpacked(kback[i])[:, :E] for i in range(2 * NH)], axis=0).astype(BF)
    part = lax.dot_general(kf[...], rows_back, (((0,), (0,)), ((), ())), preferred_element_type=F32).astype(BF)
    tall = part.shape[0]
    for j in range(E // 128):
        wbuf[tall * j : tall * (j + 1), :] = part[:, 128 * j : 128 * (j + 1)]
    wbuf[tall * (E // 128) :, :] = jnp.zeros((NZ * WZ - tall * (E // 128), 128), BF)

    def cut_of(ref, size, at):
        return lambda: ref.at[rows(size * at, size), :]

    def slot(ref, at):
        return lambda: ref.at[at]

    w_first = [
        [Send(cut_of(wbuf, WZ, mod(z + r, NZ)), slot(wzr, r - 1), zpeer[r], core=0) for r in ZS],
        [Send(cut_of(wbuf, WX, mod(x + r, NX)), slot(wxr, r - 1), xpeer[r], core=1) for r in XS],
    ]
    w_second = [
        [Send(slot(wx, x), slot(wx, x), xpeer[r], slot(wx, xfrom[r]), 0) for r in XS],
        [Send(cut_of(wxs, BLK, mod(z + r, NZ)), slot(wxzr, r - 1), zpeer[r], core=1) for r in ZS],
    ]
    w_pair = [
        [Send(slot(wy, y), slot(wy, y), other_y, slot(wy, 1 - y), 0)],
        [Send(slot(wys, y), slot(wys, y), other_y, slot(wys, 1 - y), 1)],
    ]
    w_third = [
        [],
        [Send(cut_of(wxz, BLK, z), cut_of(wxz, BLK, z), zpeer[r], cut_of(wxz, BLK, zfrom[r]), 1) for r in ZS],
    ]
    w_last = [
        [Send(cut_of(wall, WZ, z), cut_of(wall, WZ, z), zpeer[r], cut_of(wall, WZ, zfrom[r]), 0) for r in ZS],
        [Send(cut_of(wall, WX, x), cut_of(wall, WX, x), xpeer[r], cut_of(wall, WX, xfrom[r]), 1) for r in XS],
    ]

    def begin(copies):
        for go in copies:
            go.start()

    def arrive(copies):
        for go in copies:
            go.recv()

    @on_core
    def _(core):
        begin(w_first[core])

    b_spread.step()

    @on_core
    def _(core):
        if core == 0:
            total = wbuf[rows(WZ * z, WZ), :].astype(F32)
            arrive(w_first[0])
            for r in range(NZ - 1):
                total = total + wzr[r].astype(F32)
            wx[x] = total.astype(BF)
        else:
            total = wbuf[rows(WX * x, WX), :].astype(F32)
            arrive(w_first[1])
            for r in range(NX - 1):
                total = total + wxr[r].astype(F32)
            wxs[:WX, :] = total.astype(BF)
            wxs[WX:, :] = jnp.zeros((NZ * BLK - WX, 128), BF)
        begin(w_second[core])

    b_spread.last()

    @on_core
    def _(core):
        arrive(w_second[core])
        if core == 0:
            total = wx[0].astype(F32)
            for i in range(1, NX):
                total = total + wx[i].astype(F32)
            wy[y] = total.astype(BF)
        else:
            total = wxs[rows(BLK * z, BLK), :].astype(F32)
            for r in range(NZ - 1):
                total = total + wxzr[r].astype(F32)
            wys[y] = total.astype(BF)
        begin(w_pair[core])


    @on_core
    def _(core):
        arrive(w_pair[core])
        if core == 0:
            wall[rows(WZ * z, WZ), :] = (wy[0].astype(F32) + wy[1].astype(F32)).astype(BF)
            begin(w_last[0])
        else:
            wxz[rows(BLK * z, BLK), :] = (wys[0].astype(F32) + wys[1].astype(F32)).astype(BF)
            begin(w_third[1])
            arrive(w_third[1])
            wall[rows(WX * x, WX), :] = wxz[:WX, :]
            begin(w_last[1])

    b_spread.end()
    for i in range(2):
        og[HALF * i : HALF * (i + 1), :] = dot_t(back[HP * i : HP * i + HALF, :], lp[...]).astype(BF)
    g_out = pltpu.make_async_copy(og, out_g, lsem.at[6])
    g_out.start()

    @on_core
    def _(core):
        arrive(w_last[core])

    for j in range(E // 128):
        ow[:, 128 * j : 128 * (j + 1)] = wall[tall * j : tall * (j + 1), :].astype(F32)
    w_out = pltpu.make_async_copy(ow, out_w, lsem.at[7])
    w_out.start()
    finish()
    g_out.wait()
    w_out.wait()


def body(log_feats, kpi_feats, log_proj, kpi_proj, log_ids, kpi_ids):
    v = pltpu.VMEM
    inputs = (log_feats, kpi_feats, log_proj, kpi_proj, log_ids.reshape(1, -1), kpi_ids.reshape(1, -1))
    outs = (jax.ShapeDtypeStruct(log_feats.shape, BF), jax.ShapeDtypeStruct(kpi_proj.shape, F32))
    scratch = [v(a.shape, a.dtype) for a in inputs + outs] + [
        v((HP, E), BF), v((HP, E), BF), v((HP, E), F32), *[v((2, BLK, E), BF)] * 4,
        v((2 * HP, E), BF), v((BLK, E), F32), v((2 * HP, ID), BF),
        v((GROUP, E), F32), v((32, E), BF), v((32, E), BF), v((3, 16, PK), BF), v((3, 16, PK), BF),
        v((16, PK), BF), v((16, PK), BF), v((COUNT, EK), BF), v((OWN, E), F32),
        v((2 * HP, COUNT), BF), v((COUNT, E), F32), v((HP, E), F32),
        v((HP, E), BF), v((HP, E), BF), *[v((2, BLK, E), BF)] * 4, v((2 * HP, E), BF),
        *[v((4, 64, E), BF)] * 4, *[v((2, 128, E), BF)] * 4,
        v((128, E), F32), v((7, 16, E), BF), v((7, 16, E), BF), v((16, E), F32), v((16, PK), BF), v((16, PK), BF),
        v((2 * NH, 16, PK), BF), v((NZ * WZ, 128), BF), v((NZ - 1, WZ, 128), BF), v((NX - 1, WX, 128), BF),
        v((NX, WZ, 128), BF), v((NY, WZ, 128), BF), v((NZ * BLK, 128), BF), v((NZ - 1, BLK, 128), BF),
        v((NY, BLK, 128), BF), v((NZ * BLK, 128), BF), v((NZ * WZ, 128), BF),
        pltpu.SemaphoreType.DMA((NSEM,)), pltpu.SemaphoreType.DMA((NSEM,)),
        pltpu.SemaphoreType.DMA((8,)),
    ]
    return pl.pallas_call(
        kernel,
        out_shape=outs,
        in_specs=[pl.BlockSpec(memory_space=pltpu.HBM)] * 6,
        out_specs=(pl.BlockSpec(memory_space=pltpu.HBM),) * 2,
        scratch_shapes=scratch,
        compiler_params=pltpu.CompilerParams(
            collective_id=0, has_side_effects=True, vmem_limit_bytes=62 * 1024 * 1024
        ),
    )(*inputs)


def solution(mesh):
    return jax.shard_map(
        body,
        mesh=mesh,
        in_specs=(
            P("dp", "tensor"),
            P("dp", "tensor"),
            P("tensor", None),
            P("tensor", None),
            P("dp"),
            P("dp"),
        ),
        out_specs=(P("dp", "tensor"), P("tensor", None)),
        check_vma=False,
    )
```

```python
import jax
import jax.numpy as jnp
from jax import lax
from jax.experimental import pallas as pl
from jax.experimental.pallas import tpu as pltpu
from jax.sharding import PartitionSpec as P

TEMPER = 32.0
BIAS = -2.0
LOSS = 4096.0
EPS = 1e-06
MESH = pl.DeviceIdType.MESH
BF = jnp.bfloat16
F32 = jnp.float32

NY, NX, NZ, NH = 2, 4, 8, 4
LOG = 352
HALF = LOG // 2
BLK = 48
HP = NH * BLK
E = 1152
ID = 128
EK = E + ID
GROUP = 64
OWN = 8
COUNT = NY * NX * NZ * OWN
SCALE = TEMPER * LOSS / (LOG * NY * NX * NZ)
PK = EK // 2
CUT = 32
WZ, WX = 176, 336
XS, ZS = (2, 1, 3), (4, 3, 5, 2, 6, 1, 7)
NSEM = 160


def dot(a, b):
    return jnp.dot(a, b, preferred_element_type=F32)


def dot_t(a, b):
    return lax.dot_general(a, b, (((1,), (1,)), ((), ())), preferred_element_type=F32)


def mod(a, n):
    return lax.rem(a, jnp.int32(n))


def digits(ids):
    high = jnp.floor(ids * (1.0 / 256.0))
    rest = ids - 256.0 * high
    middle = jnp.floor(rest * (1.0 / 16.0))
    return high, middle, rest - 16.0 * middle


def on_lanes(values, rows):
    lane = lax.broadcasted_iota(jnp.int32, (rows, ID), 1)
    out = jnp.zeros((rows, ID), F32)
    for at, value in enumerate(values):
        out = jnp.where(lane == at, value, out)
    return out


def pair_gradient(inner, apart):
    sign = jnp.where(apart < 0.5, 1.0, -1.0).astype(F32)
    margin = -sign * (TEMPER * inner + BIAS)
    return (-SCALE * sign * jax.nn.sigmoid(margin)).astype(BF)


def kernel(
    lf_h, kf_h, lp_h, kp_h, lid_h, kid_h, out_g, out_w,
    lf, kf, lp, kp, lid, kid, og,
    lsend, lrecv, lacc, lrs, lrr, lls, llr, lall, lunit, lext,
    kacc, ksend, krecv, kysend, kyrecv, kfo, kf2, kido, kall, kunit,
    pg, kg, lg, gsend, grecv, grs, grr, gls, glr, back,
    zrs, zrr, zls, zlr, xrs, xrr, xls, xlr, mid, midsend, midrecv, mid16,
    kback, wbuf, wzr, wxr, wx, wy, wxs, wxzr, wys, wxz, wall,
    ssem, rsem, lsem,
):
    d = lax.axis_index("dp")
    t = lax.axis_index("tensor")
    y = lax.div(d, jnp.int32(NX * NZ))
    x = mod(lax.div(d, jnp.int32(NZ)), NX)
    z = mod(d, NZ)
    h = lax.div(t, jnp.int32(2))
    c = mod(t, 2)

    def place(y=y, x=x, z=z, h=h, c=c):
        return {"dp": (y * NX + x) * NZ + z, "tensor": h * 2 + c}

    def rows(start, size, unit=16):
        return pl.ds(pl.multiple_of(start, unit), size)

    started = []

    class Send:
        def __init__(self, src, dst, to, land=None, core=None):
            self.src, self.dst, self.to, self.core = src, dst, to, core
            self.land = land or dst
            self.at = len(started)
            self.open, self.begun = True, False
            started.append(self)
            assert self.at < NSEM

        def copy(self, src, dst):
            return pltpu.make_async_remote_copy(
                src_ref=src(), dst_ref=dst(), send_sem=ssem.at[self.at], recv_sem=rsem.at[self.at],
                device_id=self.to, device_id_type=MESH,
            )

        def start(self):
            self.begun = True
            self.copy(self.src, self.dst).start()

        def recv(self):
            self.open = False
            self.copy(self.land, self.land).wait_recv()

        def sent(self):
            self.copy(self.src, self.dst).wait_send()

    def finish():
        for core in (None, 0, 1):

            def ends(core=core):
                for go in started:
                    if go.core == core and go.begun:
                        if go.open:
                            go.recv()
                        go.sent()

            if core is None:
                ends()
            else:
                pl.when(c == core)(ends)

    inputs = [
        pltpu.make_async_copy(a, b, lsem.at[i])
        for i, (a, b) in enumerate(((kf_h, kf), (kp_h, kp), (lf_h, lf), (lp_h, lp), (kid_h, kid), (lid_h, lid)))
    ]
    for go in inputs:
        go.start()

    partner = place(c=1 - c)
    ypeer = {(r, f): place(h=mod(h + r, NH), y=y if f == 0 else 1 - y) for r in range(NH) for f in (0, 1)}
    hpeer = [place(h=mod(h + r, NH)) for r in range(NH)]
    hfrom = [mod(h + NH - r, NH) for r in range(NH)]
    xpeer = [place(x=mod(x + r, NX)) for r in range(NX)]
    xfrom = [mod(x + NX - r, NX) for r in range(NX)]
    zpeer = [place(z=mod(z + r, NZ)) for r in range(NZ)]
    zfrom = [mod(z + NZ - r, NZ) for r in range(NZ)]

    barrier = pltpu.get_barrier_semaphore()
    peers = [partner] + [ypeer[k] for k in ypeer if k != (0, 0)] + xpeer[1:] + zpeer[1:]
    for device in peers:
        pl.semaphore_signal(barrier, inc=1, device_id=device, device_id_type=MESH)

    def on_core(run):
        for core in (0, 1):
            pl.when(c == core)(lambda core=core: run(core))

    def packed(v):
        if v.shape[1] < EK:
            v = jnp.concatenate([v, jnp.zeros((OWN, EK - v.shape[1]), F32)], axis=1)
        return jnp.concatenate([v[:, :PK], v[:, PK:]], axis=0).astype(BF)

    def unpacked(v):
        v = v.astype(F32)
        return jnp.concatenate([v[:OWN], v[OWN:]], axis=1)

    class Gather:
        def __init__(self, n, at, size, split, right, left, block, sign=1, core=None):
            self.n, self.go = n, []
            low, high = (0, split), (split, size - split)
            ways = [(right, -sign, low), (left, sign, high), (right, -sign, high), (left, sign, low)]
            for s in range(n // 2):
                step = []
                for to, way, part in ways if s < n // 2 - 1 else ways[:2]:
                    there, here = block(at + way * s, part), block(at + way * (s + 1), part)
                    step.append(Send(there, there, to, here, core))
                self.go.append(step)

        def step(self, s):
            for i, go in enumerate(self.go[s]):
                if s > 0:
                    self.go[s - 1][i].recv()
                go.start()

        def recv(self, s):
            for go in self.go[s]:
                if go.open:
                    go.recv()

        def end(self):
            for s in range(self.n // 2):
                self.recv(s)

    class Sum:
        def __init__(self, n, at, size, split, right, left, part, bufs, sign=1, core=None):
            self.n, self.at, self.size, self.part = n, at, size, part
            self.rs, self.rr, self.ls, self.lr = bufs
            low, high = (0, split), (split, size - split)
            r, l = (right, sign, self.rs, self.rr), (left, -sign, self.ls, self.lr)
            self.ways = [(*r, low), (*l, high), (*r, high), (*l, low)]
            self.go = []
            for s in range(n // 2):
                step = []
                for to, _, send, come, p in self.ways[:2] if s == 0 else self.ways:
                    src = lambda s=s, p=p, send=send: send.at[s, pl.ds(*p)]
                    dst = lambda s=s, p=p, come=come: come.at[s, pl.ds(*p)]
                    step.append(Send(src, dst, to, core=core))
                self.go.append(step)

        def step(self, s):
            for i in (0, 1) if s == 0 else (2, 3, 0, 1):
                _, way, send, come, p = self.ways[i]
                value = self.part(self.at + way * (self.n // 2 - s), *p)
                if s > 1 or (s == 1 and i < 2):
                    self.go[s - 1][i].recv()
                    value = value + come[s - 1, pl.ds(*p), :].astype(F32)
                send[s, pl.ds(*p), :] = value.astype(BF)
                self.go[s][i].start()

        def end(self):
            for go in self.go[-1]:
                go.recv()

        def result(self):
            last = self.n // 2 - 1
            return self.part(self.at, 0, self.size) + self.rr[last].astype(F32) + self.lr[last].astype(F32)

    turn = 1 - 2 * c
    h_right = place(h=mod(h + turn + NH, NH))
    h_left = place(h=mod(h - turn + NH, NH))

    def h_sum(own, come, bufs):
        def part(which, start, size):
            at = rows(BLK * mod(which + NH, NH) + start, size)
            return own[at, :] + come[at, :].astype(F32)

        return Sum(NH, h, BLK, CUT, h_right, h_left, part, bufs, turn)

    class Spread:
        def __init__(self, buffer):
            self.buffer = buffer

            def at_core(core):
                def block(hh, part=(0, BLK)):
                    return lambda: buffer.at[rows(HP * core + BLK * mod(hh + NH, NH) + part[0], part[1]), :]

                return block

            mine, other = at_core(c), at_core(1 - c)
            self.along = Gather(NH, h, BLK, CUT, h_right, h_left, mine, turn)
            self.across = {r: Send(mine(h - r), mine(h - r), partner, other(h - r)) for r in (0, 1, 3, 2)}

        def start(self, value):
            self.buffer[rows(HP * c + BLK * h, BLK), :] = value
            self.along.step(0)
            self.across[0].start()

        def step(self):
            self.along.step(1)
            self.along.recv(0)
            self.across[1].start()
            self.across[3].start()

        def last(self):
            self.along.recv(1)
            self.across[2].start()

        def end(self):
            for go in self.across.values():
                go.recv()

    inputs[0].wait()
    inputs[1].wait()
    kacc[...] = dot(kf[...], kp[...])
    ksend[...] = kacc[rows(32 * (1 - c), 32, 32), :].astype(BF)
    inputs[2].wait()
    inputs[3].wait()
    lsend[:HALF, :] = dot(lf[rows(HALF * (1 - c), HALF), :], lp[...]).astype(BF)
    lsend[HALF:, :] = jnp.zeros((HP - HALF, E), BF)
    inputs[4].wait()
    inputs[5].wait()

    pl.semaphore_wait(barrier, len(peers))
    k_core = Send(lambda: ksend, lambda: krecv, partner)
    k_core.start()
    l_core = Send(lambda: lsend, lambda: lrecv, partner)
    l_core.start()

    lacc[:HALF, :] = dot(lf[rows(HALF * c, HALF), :], lp[...])
    lacc[HALF:, :] = jnp.zeros((HP - HALF, E), F32)

    f_copy = Send(lambda: kf, lambda: kfo, ypeer[0, 1])
    f_copy.start()
    i_copy = Send(lambda: kid, lambda: kido, ypeer[0, 1])
    i_copy.start()

    k_core.recv()
    kacc[rows(32 * c, 32, 32), :] += krecv[...].astype(F32)
    k_waits = []
    for r in (2, 1, 3, 0):
        kysend[r] = packed(kacc[rows(32 * c + OWN * mod(h + r, NH), OWN, OWN), :])
        for f in (0, 1):
            if (r, f) != (0, 0):
                go = Send(lambda r=r: kysend.at[r], lambda r=r, f=f: kyrecv.at[f, r], ypeer[r, f])
                go.start()
                k_waits.append(go)

    l_sum = h_sum(lacc, lrecv, (lrs, lrr, lls, llr))
    l_core.recv()
    l_sum.step(0)

    i_copy.recv()
    f_copy.recv()

    def by_group(own, other):
        return jnp.concatenate([jnp.where(y == 0, own, other), jnp.where(y == 0, other, own)], axis=0)

    row_ids = lax.broadcasted_iota(jnp.int32, (OWN, GROUP), 0) + (32 * c + OWN * h)
    col_ids = lax.broadcasted_iota(jnp.int32, (OWN, GROUP), 1)

    def id_column(ref):
        return jnp.sum(jnp.where(row_ids == col_ids, ref[...].astype(F32), 0.0), axis=1, keepdims=True)

    k_id = by_group(id_column(kid), id_column(kido))
    one = jnp.ones_like(k_id)
    k_digit = digits(k_id)
    k_ext = on_lanes(list(k_digit) + [g * g for g in k_digit] + [one] * 3, 2 * OWN)

    at = lax.broadcasted_iota(jnp.int32, (2 * HP, LOG), 0)
    upper = at >= HP
    inside = jnp.where(upper, at - HP, at)
    at = jnp.where(inside < HALF, jnp.where(upper, inside + HALF, inside), -1)
    col = lax.broadcasted_iota(jnp.int32, (2 * HP, LOG), 1)
    log_id = jnp.sum(jnp.where(at == col, lid[...].reshape(1, LOG).astype(F32), 0.0), axis=1, keepdims=True)
    one = jnp.ones_like(log_id)
    log_digit = digits(log_id)
    lext[...] = on_lanes([-2.0 * g for g in log_digit] + [one] * 3 + [g * g for g in log_digit], 2 * HP).astype(BF)

    l_sum.step(1)

    for go in k_waits:
        go.recv()
    own, other = unpacked(kysend[0]), unpacked(kyrecv[1, 0])
    for r in range(1, NH):
        own = own + unpacked(kyrecv[0, r])
        other = other + unpacked(kyrecv[1, r])
    unit = by_group(own, other)[:, :E]
    k_inv = lax.rsqrt(jnp.sum(unit * unit, axis=1, keepdims=True) + EPS)
    unit = unit * k_inv
    kunit[...] = unit
    both = jnp.concatenate([unit, k_ext], axis=1).astype(BF)

    def block0(zz, xx):
        return kall.at[rows(64 * zz + 16 * xx, 16), :]

    def block1(zz, xx):
        return kall.at[rows(128 * xx + 16 * zz, 16), :]

    own0 = lambda: block0(z, x)
    own1 = lambda: block1(z, x)
    first = [
        [Send(own0, own0, xpeer[r], lambda r=r: block0(z, xfrom[r]), 0) for r in XS],
        [Send(own1, own1, zpeer[r], lambda r=r: block1(zfrom[r], x), 1) for r in ZS],
    ]

    def k_block(n, size):
        return lambda which, part: lambda: kall.at[rows(size * mod(which + n, n) + part[0], part[1]), :]

    ring = [
        Gather(NZ, z, 64, 32, zpeer[1], zpeer[NZ - 1], k_block(NZ, 64), core=0),
        Gather(NX, x, 128, 64, xpeer[1], xpeer[NX - 1], k_block(NX, 128), core=1),
    ]

    @on_core
    def _(core):
        base = rows(64 * z + 16 * x, 16) if core == 0 else rows(128 * x + 16 * z, 16)
        kall[base, :] = both
        for go in first[core]:
            go.start()

    l_sum.end()
    row = l_sum.result()
    l_inv = lax.rsqrt(jnp.sum(row * row, axis=1, keepdims=True) + EPS)
    row = row * l_inv
    lunit[...] = row
    l_spread = Spread(lall)
    l_spread.start(row.astype(BF))

    @on_core
    def _(core):
        for go in first[core]:
            go.recv()
        ring[core].step(0)
        ring[core].step(1)

    l_spread.step()

    @on_core
    def _(core):
        for s in range(2, ring[core].n // 2):
            ring[core].step(s)

    l_spread.last()

    mine, theirs = kf[...].astype(F32), kfo[...].astype(F32)
    pieces = []
    for i in range(2 * NH):
        pieces.append(by_group(mine[OWN * i : OWN * (i + 1)], theirs[OWN * i : OWN * (i + 1)]))
    kf2[...] = jnp.concatenate(pieces, axis=0).astype(BF)

    @on_core
    def _(core):
        ring[core].end()

    l_spread.end()

    lead = jnp.where(c == 0, lax.div(mod(z + NZ // 2, NZ), jnp.int32(2)), mod(x + NX // 2, NX))

    def kpi_side(i, carry):
        at = rows(mod(lead + i, 4) * 128, 128, 128)
        inner = dot_t(kall[at, :E], lall[...])
        apart = dot_t(kall[at, E:], lext[...])
        kg[at, :] = dot(pair_gradient(inner, apart), lall[...])
        return carry

    def k_part_of(n, size):
        return lambda which, start, count: kg[rows(size * mod(which + n, n) + start, count), :]

    sums = [
        Sum(NZ, z, 64, 32, zpeer[1], zpeer[NZ - 1], k_part_of(NZ, 64), (zrs, zrr, zls, zlr), core=0),
        Sum(NX, x, 128, 64, xpeer[1], xpeer[NX - 1], k_part_of(NX, 128), (xrs, xrr, xls, xlr), core=1),
    ]

    def step(s):
        @on_core
        def _(core):
            if s < sums[core].n // 2:
                sums[core].step(s)

    kpi_side(0, 0)
    step(0)
    lax.fori_loop(1, COUNT // 128, kpi_side, 0)
    step(1)

    def log_pairs(i, carry):
        at = rows(i * 256, 256, 256)
        inner = dot_t(lall[...], kall[at, :E])
        apart = dot_t(lext[...], kall[at, E:])
        pg[:, at] = pair_gradient(inner, apart)
        return carry

    lax.fori_loop(0, COUNT // 256, log_pairs, 0)
    gsend[...] = dot(pg[rows(HP * (1 - c), HP), :], kall[:, :E]).astype(BF)
    g_core = Send(lambda: gsend, lambda: grecv, partner)
    g_core.start()
    step(2)
    lg[...] = dot(pg[rows(HP * c, HP), :], kall[:, :E])

    g_sum = h_sum(lg, grecv, (grs, grr, gls, glr))
    g_core.recv()
    g_sum.step(0)
    step(3)

    middle = [
        [Send(lambda r=r: midsend.at[r - 1], lambda r=r: midrecv.at[r - 1], xpeer[r], core=0) for r in XS],
        [Send(lambda r=r: midsend.at[r - 1], lambda r=r: midrecv.at[r - 1], zpeer[r], core=1) for r in ZS],
    ]

    g_sum.step(1)

    @on_core
    def _(core):
        at, order = ((x, XS), (z, ZS))[core]
        n = len(order) + 1
        sums[core].end()
        mid[: 16 * n, :] = sums[core].result()
        for r, go in zip(order, middle[core]):
            midsend[r - 1] = mid[rows(16 * mod(at + r, n), 16), :].astype(BF)
            go.start()
        total = mid[rows(16 * at, 16), :]
        for go in middle[core]:
            go.recv()
        for r in range(n - 1):
            total = total + midrecv[r].astype(F32)
        mid16[...] = total

    total = mid16[...]
    unit = kunit[...]
    inner = jnp.sum(unit * total, axis=1, keepdims=True)

    def kblock(hh):
        return lambda: kback.at[rows(16 * (c * NH + hh), 16), :]

    kback[rows(16 * (c * NH + h), 16), :] = (k_inv * (total - unit * inner)).astype(BF)
    kb_waits = [Send(kblock(h), kblock(h), hpeer[r], kblock(hfrom[r])) for r in (2, 1, 3)]
    for go in kb_waits:
        go.start()

    g_sum.end()
    row = g_sum.result()
    unit = lunit[...]
    inner = jnp.sum(unit * row, axis=1, keepdims=True)
    row = (l_inv * (row - unit * inner)).astype(BF)

    def khalf(core):
        return lambda: kback.at[rows(16 * NH * core, 16 * NH), :]

    for go in kb_waits:
        go.recv()
    kb_core = Send(khalf(c), khalf(c), partner, khalf(1 - c))
    kb_core.start()
    b_spread = Spread(back)
    b_spread.start(row)
    kb_core.recv()

    part = lax.dot_general(
        kf2[...], kback[...], (((0,), (0,)), ((), ())), preferred_element_type=F32
    ).astype(BF)
    tall = part.shape[0]
    for j in range(E // 128):
        wbuf[tall * j : tall * (j + 1), :] = part[:, 128 * j : 128 * (j + 1)]
    wbuf[tall * (E // 128) :, :] = jnp.zeros((NZ * WZ - tall * (E // 128), 128), BF)

    def cut_of(ref, size, at):
        return lambda: ref.at[rows(size * at, size), :]

    def slot(ref, at):
        return lambda: ref.at[at]

    w_first = [
        [Send(cut_of(wbuf, WZ, mod(z + r, NZ)), slot(wzr, r - 1), zpeer[r], core=0) for r in ZS],
        [Send(cut_of(wbuf, WX, mod(x + r, NX)), slot(wxr, r - 1), xpeer[r], core=1) for r in XS],
    ]
    w_second = [
        [Send(slot(wx, x), slot(wx, x), xpeer[r], slot(wx, xfrom[r]), 0) for r in XS],
        [Send(cut_of(wxs, BLK, mod(z + r, NZ)), slot(wxzr, r - 1), zpeer[r], core=1) for r in ZS],
    ]
    w_pair = [
        [Send(slot(wy, y), slot(wy, y), ypeer[0, 1], slot(wy, 1 - y), 0)],
        [Send(slot(wys, y), slot(wys, y), ypeer[0, 1], slot(wys, 1 - y), 1)],
    ]
    w_third = [
        [],
        [Send(cut_of(wxz, BLK, z), cut_of(wxz, BLK, z), zpeer[r], cut_of(wxz, BLK, zfrom[r]), 1) for r in ZS],
    ]
    w_last = [
        [Send(cut_of(wall, WZ, z), cut_of(wall, WZ, z), zpeer[r], cut_of(wall, WZ, zfrom[r]), 0) for r in ZS],
        [Send(cut_of(wall, WX, x), cut_of(wall, WX, x), xpeer[r], cut_of(wall, WX, xfrom[r]), 1) for r in XS],
    ]

    def begin(copies):
        for go in copies:
            go.start()

    def arrive(copies):
        for go in copies:
            go.recv()

    @on_core
    def _(core):
        begin(w_first[core])

    b_spread.step()

    @on_core
    def _(core):
        if core == 0:
            total = wbuf[rows(WZ * z, WZ), :].astype(F32)
            arrive(w_first[0])
            for r in range(NZ - 1):
                total = total + wzr[r].astype(F32)
            wx[x] = total.astype(BF)
        else:
            total = wbuf[rows(WX * x, WX), :].astype(F32)
            arrive(w_first[1])
            for r in range(NX - 1):
                total = total + wxr[r].astype(F32)
            wxs[:WX, :] = total.astype(BF)
            wxs[WX:, :] = jnp.zeros((NZ * BLK - WX, 128), BF)
        begin(w_second[core])

    b_spread.last()

    @on_core
    def _(core):
        arrive(w_second[core])
        if core == 0:
            total = wx[0].astype(F32)
            for i in range(1, NX):
                total = total + wx[i].astype(F32)
            wy[y] = total.astype(BF)
        else:
            total = wxs[rows(BLK * z, BLK), :].astype(F32)
            for r in range(NZ - 1):
                total = total + wxzr[r].astype(F32)
            wys[y] = total.astype(BF)
        begin(w_pair[core])


    @on_core
    def _(core):
        arrive(w_pair[core])
        if core == 0:
            wall[rows(WZ * z, WZ), :] = (wy[0].astype(F32) + wy[1].astype(F32)).astype(BF)
            begin(w_last[0])
        else:
            wxz[rows(BLK * z, BLK), :] = (wys[0].astype(F32) + wys[1].astype(F32)).astype(BF)
            begin(w_third[1])
            arrive(w_third[1])
            wall[rows(WX * x, WX), :] = wxz[:WX, :]
            begin(w_last[1])

    b_spread.end()
    for i in range(2):
        og[HALF * i : HALF * (i + 1), :] = dot_t(back[HP * i : HP * i + HALF, :], lp[...]).astype(BF)
    g_out = pltpu.make_async_copy(og, out_g, lsem.at[6])
    g_out.start()

    @on_core
    def _(core):
        arrive(w_last[core])

    w_out = pltpu.make_async_copy(wall, out_w, lsem.at[7])
    w_out.start()
    finish()
    g_out.wait()
    w_out.wait()


def deliver(g, w, out_g, out_w, wall, ow, sem):
    first = pltpu.make_async_copy(g, out_g, sem.at[0])
    second = pltpu.make_async_copy(w, wall, sem.at[1])
    first.start()
    second.start()
    second.wait()
    tall = out_w.shape[0]
    for j in range(E // 128):
        ow[:, 128 * j : 128 * (j + 1)] = wall[tall * j : tall * (j + 1), :].astype(F32)
    third = pltpu.make_async_copy(ow, out_w, sem.at[2])
    third.start()
    first.wait()
    third.wait()


def body(log_feats, kpi_feats, log_proj, kpi_proj, log_ids, kpi_ids):
    v = pltpu.VMEM
    inputs = (log_feats, kpi_feats, log_proj, kpi_proj, log_ids, kpi_ids.reshape(1, -1))
    outs = (jax.ShapeDtypeStruct(log_feats.shape, BF), jax.ShapeDtypeStruct((NZ * WZ, 128), BF))
    hbm = pl.BlockSpec(memory_space=pltpu.HBM)
    scratch = [v(a.shape, a.dtype) for a in inputs + outs[:1]] + [
        v((HP, E), BF), v((HP, E), BF), v((HP, E), F32), *[v((2, BLK, E), BF)] * 4,
        v((2 * HP, E), BF), v((BLK, E), F32), v((2 * HP, ID), BF),
        v((GROUP, E), F32), v((32, E), BF), v((32, E), BF), v((NH, 16, PK), BF), v((2, NH, 16, PK), BF),
        v(kpi_feats.shape, BF), v((2 * GROUP, kpi_feats.shape[1]), BF), v((1, GROUP), jnp.int32),
        v((COUNT, EK), BF), v((2 * OWN, E), F32),
        v((2 * HP, COUNT), BF), v((COUNT, E), F32), v((HP, E), F32),
        v((HP, E), BF), v((HP, E), BF), *[v((2, BLK, E), BF)] * 4, v((2 * HP, E), BF),
        *[v((4, 64, E), BF)] * 4, *[v((2, 128, E), BF)] * 4,
        v((128, E), F32), v((7, 16, E), BF), v((7, 16, E), BF), v((16, E), F32),
        v((2 * NH * 16, E), BF), v((NZ * WZ, 128), BF), v((NZ - 1, WZ, 128), BF), v((NX - 1, WX, 128), BF),
        v((NX, WZ, 128), BF), v((NY, WZ, 128), BF), v((NZ * BLK, 128), BF), v((NZ - 1, BLK, 128), BF),
        v((NY, BLK, 128), BF), v((NZ * BLK, 128), BF), v((NZ * WZ, 128), BF),
        pltpu.SemaphoreType.DMA((NSEM,)), pltpu.SemaphoreType.DMA((NSEM,)),
        pltpu.SemaphoreType.DMA((8,)),
    ]
    grads = pl.pallas_call(
        kernel,
        out_shape=outs,
        in_specs=[hbm] * 6,
        out_specs=(hbm,) * 2,
        scratch_shapes=scratch,
        compiler_params=pltpu.CompilerParams(
            collective_id=0, has_side_effects=True, vmem_limit_bytes=62 * 1024 * 1024
        ),
    )(*inputs)
    return pl.pallas_call(
        deliver,
        out_shape=(outs[0], jax.ShapeDtypeStruct(kpi_proj.shape, F32)),
        in_specs=[hbm] * 2,
        out_specs=(hbm,) * 2,
        scratch_shapes=[v(outs[1].shape, BF), v(kpi_proj.shape, F32), pltpu.SemaphoreType.DMA((3,))],
        compiler_params=pltpu.CompilerParams(vmem_limit_bytes=62 * 1024 * 1024),
    )(*grads)


def solution(mesh):
    return jax.shard_map(
        body,
        mesh=mesh,
        in_specs=(
            P("dp", "tensor"),
            P("dp", "tensor"),
            P("tensor", None),
            P("tensor", None),
            P("dp"),
            P("dp"),
        ),
        out_specs=(P("dp", "tensor"), P("tensor", None)),
        check_vma=False,
    )
```

```python
import jax
import jax.numpy as jnp
from jax import lax
from jax.experimental import pallas as pl
from jax.experimental.pallas import tpu as pltpu
from jax.sharding import PartitionSpec as P

TEMPER = 32.0
BIAS = -2.0
LOSS = 4096.0
EPS = 1e-06
MESH = pl.DeviceIdType.MESH
BF = jnp.bfloat16
F32 = jnp.float32

NY, NX, NZ, NH = 2, 4, 8, 4
LOG = 352
HALF = LOG // 2
BLK = 48
HP = NH * BLK
E = 1152
ID = 128
EK = E + ID
GROUP = 64
OWN = 8
COUNT = NY * NX * NZ * OWN
SCALE = TEMPER * LOSS / (LOG * NY * NX * NZ)
PK = EK // 2
CUT = 32
WZ, WX = 176, 336
XS, ZS = (2, 1, 3), (4, 3, 5, 2, 6, 1, 7)
NSEM = 160


def dot(a, b):
    return jnp.dot(a, b, preferred_element_type=F32)


def dot_t(a, b):
    return lax.dot_general(a, b, (((1,), (1,)), ((), ())), preferred_element_type=F32)


def mod(a, n):
    return lax.rem(a, jnp.int32(n))


def digits(ids):
    high = jnp.floor(ids * (1.0 / 256.0))
    rest = ids - 256.0 * high
    middle = jnp.floor(rest * (1.0 / 16.0))
    return high, middle, rest - 16.0 * middle


def on_lanes(values, rows):
    lane = lax.broadcasted_iota(jnp.int32, (rows, ID), 1)
    out = jnp.zeros((rows, ID), F32)
    for at, value in enumerate(values):
        out = jnp.where(lane == at, value, out)
    return out


def pair_gradient(inner, apart):
    sign = jnp.where(apart < 0.5, 1.0, -1.0).astype(F32)
    margin = -sign * (TEMPER * inner + BIAS)
    return (-SCALE * sign * jax.nn.sigmoid(margin)).astype(BF)


def kernel(
    lf_h, kf_h, lp_h, kp_h, lid_h, kid_h, out_g, out_w,
    lf, kf, lp, kp, lid, kid, og,
    lsend, lrecv, lacc, lrs, lrr, lls, llr, lall, lunit, lext,
    kacc, ksend, krecv, kysend, kyrecv, kfo, kf2, kido, kall, kunit,
    pg, kg, lg, gsend, grecv, grs, grr, gls, glr, back,
    zrs, zrr, zls, zlr, xrs, xrr, xls, xlr, mid, midsend, midrecv, mid16,
    kback, wbuf, wzr, wxr, wx, wy, wxs, wxzr, wys, wxz, wlast,
    ssem, rsem, lsem,
):
    d = lax.axis_index("dp")
    t = lax.axis_index("tensor")
    y = lax.div(d, jnp.int32(NX * NZ))
    x = mod(lax.div(d, jnp.int32(NZ)), NX)
    z = mod(d, NZ)
    h = lax.div(t, jnp.int32(2))
    c = mod(t, 2)

    def place(y=y, x=x, z=z, h=h, c=c):
        return {"dp": (y * NX + x) * NZ + z, "tensor": h * 2 + c}

    def rows(start, size, unit=16):
        return pl.ds(pl.multiple_of(start, unit), size)

    started = []

    class Send:
        def __init__(self, src, dst, to, land=None, core=None):
            self.src, self.dst, self.to, self.core = src, dst, to, core
            self.land = land or dst
            self.at = len(started)
            self.open, self.begun = True, False
            started.append(self)
            assert self.at < NSEM

        def copy(self, src, dst):
            return pltpu.make_async_remote_copy(
                src_ref=src(), dst_ref=dst(), send_sem=ssem.at[self.at], recv_sem=rsem.at[self.at],
                device_id=self.to, device_id_type=MESH,
            )

        def start(self):
            self.begun = True
            self.copy(self.src, self.dst).start()

        def recv(self):
            self.open = False
            self.copy(self.land, self.land).wait_recv()

        def sent(self):
            self.copy(self.src, self.dst).wait_send()

    def finish():
        for core in (None, 0, 1):

            def ends(core=core):
                for go in started:
                    if go.core == core and go.begun:
                        if go.open:
                            go.recv()
                        go.sent()

            if core is None:
                ends()
            else:
                pl.when(c == core)(ends)

    inputs = [
        pltpu.make_async_copy(a, b, lsem.at[i])
        for i, (a, b) in enumerate(((kf_h, kf), (kp_h, kp), (lf_h, lf), (lp_h, lp), (kid_h, kid), (lid_h, lid)))
    ]
    for go in inputs:
        go.start()

    partner = place(c=1 - c)
    ypeer = {(r, f): place(h=mod(h + r, NH), y=y if f == 0 else 1 - y) for r in range(NH) for f in (0, 1)}
    hpeer = [place(h=mod(h + r, NH)) for r in range(NH)]
    hfrom = [mod(h + NH - r, NH) for r in range(NH)]
    xpeer = [place(x=mod(x + r, NX)) for r in range(NX)]
    xfrom = [mod(x + NX - r, NX) for r in range(NX)]
    zpeer = [place(z=mod(z + r, NZ)) for r in range(NZ)]
    zfrom = [mod(z + NZ - r, NZ) for r in range(NZ)]

    barrier = pltpu.get_barrier_semaphore()
    peers = [partner] + [ypeer[k] for k in ypeer if k != (0, 0)] + xpeer[1:] + zpeer[1:]
    for device in peers:
        pl.semaphore_signal(barrier, inc=1, device_id=device, device_id_type=MESH)

    def on_core(run):
        for core in (0, 1):
            pl.when(c == core)(lambda core=core: run(core))

    def packed(v):
        if v.shape[1] < EK:
            v = jnp.concatenate([v, jnp.zeros((OWN, EK - v.shape[1]), F32)], axis=1)
        return jnp.concatenate([v[:, :PK], v[:, PK:]], axis=0).astype(BF)

    def unpacked(v):
        v = v.astype(F32)
        return jnp.concatenate([v[:OWN], v[OWN:]], axis=1)

    class Gather:
        def __init__(self, n, at, size, split, right, left, block, sign=1, core=None):
            self.n, self.go = n, []
            low, high = (0, split), (split, size - split)
            ways = [(right, -sign, low), (left, sign, high), (right, -sign, high), (left, sign, low)]
            for s in range(n // 2):
                step = []
                for to, way, part in ways if s < n // 2 - 1 else ways[:2]:
                    there, here = block(at + way * s, part), block(at + way * (s + 1), part)
                    step.append(Send(there, there, to, here, core))
                self.go.append(step)

        def step(self, s):
            for i, go in enumerate(self.go[s]):
                if s > 0:
                    self.go[s - 1][i].recv()
                go.start()

        def recv(self, s):
            for go in self.go[s]:
                if go.open:
                    go.recv()

        def end(self):
            for s in range(self.n // 2):
                self.recv(s)

    class Sum:
        def __init__(self, n, at, size, split, right, left, part, bufs, sign=1, core=None):
            self.n, self.at, self.size, self.part = n, at, size, part
            self.rs, self.rr, self.ls, self.lr = bufs
            low, high = (0, split), (split, size - split)
            r, l = (right, sign, self.rs, self.rr), (left, -sign, self.ls, self.lr)
            self.ways = [(*r, low), (*l, high), (*r, high), (*l, low)]
            self.go = []
            for s in range(n // 2):
                step = []
                for to, _, send, come, p in self.ways[:2] if s == 0 else self.ways:
                    src = lambda s=s, p=p, send=send: send.at[s, pl.ds(*p)]
                    dst = lambda s=s, p=p, come=come: come.at[s, pl.ds(*p)]
                    step.append(Send(src, dst, to, core=core))
                self.go.append(step)

        def step(self, s):
            for i in (0, 1) if s == 0 else (2, 3, 0, 1):
                _, way, send, come, p = self.ways[i]
                value = self.part(self.at + way * (self.n // 2 - s), *p)
                if s > 1 or (s == 1 and i < 2):
                    self.go[s - 1][i].recv()
                    value = value + come[s - 1, pl.ds(*p), :].astype(F32)
                send[s, pl.ds(*p), :] = value.astype(BF)
                self.go[s][i].start()

        def end(self):
            for go in self.go[-1]:
                go.recv()

        def result(self):
            last = self.n // 2 - 1
            return self.part(self.at, 0, self.size) + self.rr[last].astype(F32) + self.lr[last].astype(F32)

    turn = 1 - 2 * c
    h_right = place(h=mod(h + turn + NH, NH))
    h_left = place(h=mod(h - turn + NH, NH))

    def h_sum(own, come, bufs):
        def part(which, start, size):
            at = rows(BLK * mod(which + NH, NH) + start, size)
            return own[at, :] + come[at, :].astype(F32)

        return Sum(NH, h, BLK, CUT, h_right, h_left, part, bufs, turn)

    class Spread:
        def __init__(self, buffer):
            self.buffer = buffer

            def at_core(core):
                def block(hh, part=(0, BLK)):
                    return lambda: buffer.at[rows(HP * core + BLK * mod(hh + NH, NH) + part[0], part[1]), :]

                return block

            mine, other = at_core(c), at_core(1 - c)
            self.along = Gather(NH, h, BLK, CUT, h_right, h_left, mine, turn)
            self.across = {r: Send(mine(h - r), mine(h - r), partner, other(h - r)) for r in (0, 1, 3, 2)}

        def start(self, value):
            self.buffer[rows(HP * c + BLK * h, BLK), :] = value
            self.along.step(0)
            self.across[0].start()

        def step(self):
            self.along.step(1)
            self.along.recv(0)
            self.across[1].start()
            self.across[3].start()

        def last(self):
            self.along.recv(1)
            self.across[2].start()

        def end(self):
            for go in self.across.values():
                go.recv()

    inputs[0].wait()
    inputs[1].wait()
    kacc[...] = dot(kf[...], kp[...])
    ksend[...] = kacc[rows(32 * (1 - c), 32, 32), :].astype(BF)
    inputs[2].wait()
    inputs[3].wait()
    lsend[:HALF, :] = dot(lf[rows(HALF * (1 - c), HALF), :], lp[...]).astype(BF)
    lsend[HALF:, :] = jnp.zeros((HP - HALF, E), BF)
    inputs[4].wait()
    inputs[5].wait()

    pl.semaphore_wait(barrier, len(peers))
    k_core = Send(lambda: ksend, lambda: krecv, partner)
    k_core.start()
    l_core = {}
    for r in (2, 1, 3, 0):
        out = lambda r=r: lsend.at[rows(BLK * mod(h + r, NH), BLK), :]
        come = lambda r=r: lrecv.at[rows(BLK * mod(h + r, NH), BLK), :]
        l_core[r] = Send(out, come, partner)
        l_core[r].start()

    lacc[:HALF, :] = dot(lf[rows(HALF * c, HALF), :], lp[...])
    lacc[HALF:, :] = jnp.zeros((HP - HALF, E), F32)

    f_copy = Send(lambda: kf, lambda: kfo, ypeer[0, 1])
    f_copy.start()
    i_copy = Send(lambda: kid, lambda: kido, ypeer[0, 1])
    i_copy.start()

    k_core.recv()
    kacc[rows(32 * c, 32, 32), :] += krecv[...].astype(F32)
    k_waits = []
    for r in (2, 1, 3, 0):
        kysend[r] = packed(kacc[rows(32 * c + OWN * mod(h + r, NH), OWN, OWN), :])
        for f in (0, 1):
            if (r, f) != (0, 0):
                go = Send(lambda r=r: kysend.at[r], lambda r=r, f=f: kyrecv.at[f, r], ypeer[r, f])
                go.start()
                k_waits.append(go)

    l_sum = h_sum(lacc, lrecv, (lrs, lrr, lls, llr))
    l_core[2].recv()
    l_sum.step(0)
    for r in (1, 3, 0):
        l_core[r].recv()

    i_copy.recv()
    f_copy.recv()

    def by_group(own, other):
        return jnp.concatenate([jnp.where(y == 0, own, other), jnp.where(y == 0, other, own)], axis=0)

    row_ids = lax.broadcasted_iota(jnp.int32, (OWN, GROUP), 0) + (32 * c + OWN * h)
    col_ids = lax.broadcasted_iota(jnp.int32, (OWN, GROUP), 1)

    def id_column(ref):
        return jnp.sum(jnp.where(row_ids == col_ids, ref[...].astype(F32), 0.0), axis=1, keepdims=True)

    k_id = by_group(id_column(kid), id_column(kido))
    one = jnp.ones_like(k_id)
    k_digit = digits(k_id)
    k_ext = on_lanes(list(k_digit) + [g * g for g in k_digit] + [one] * 3, 2 * OWN)

    at = lax.broadcasted_iota(jnp.int32, (2 * HP, LOG), 0)
    upper = at >= HP
    inside = jnp.where(upper, at - HP, at)
    at = jnp.where(inside < HALF, jnp.where(upper, inside + HALF, inside), -1)
    col = lax.broadcasted_iota(jnp.int32, (2 * HP, LOG), 1)
    log_id = jnp.sum(jnp.where(at == col, lid[...].reshape(1, LOG).astype(F32), 0.0), axis=1, keepdims=True)
    one = jnp.ones_like(log_id)
    log_digit = digits(log_id)
    lext[...] = on_lanes([-2.0 * g for g in log_digit] + [one] * 3 + [g * g for g in log_digit], 2 * HP).astype(BF)

    l_sum.step(1)

    for go in k_waits:
        go.recv()
    own, other = unpacked(kysend[0]), unpacked(kyrecv[1, 0])
    for r in range(1, NH):
        own = own + unpacked(kyrecv[0, r])
        other = other + unpacked(kyrecv[1, r])
    unit = by_group(own, other)[:, :E]
    k_inv = lax.rsqrt(jnp.sum(unit * unit, axis=1, keepdims=True) + EPS)
    unit = unit * k_inv
    kunit[...] = unit
    both = jnp.concatenate([unit, k_ext], axis=1).astype(BF)

    def block0(zz, xx):
        return kall.at[rows(64 * zz + 16 * xx, 16), :]

    def block1(zz, xx):
        return kall.at[rows(128 * xx + 16 * zz, 16), :]

    own0 = lambda: block0(z, x)
    own1 = lambda: block1(z, x)
    first = [
        [Send(own0, own0, xpeer[r], lambda r=r: block0(z, xfrom[r]), 0) for r in XS],
        [Send(own1, own1, zpeer[r], lambda r=r: block1(zfrom[r], x), 1) for r in ZS],
    ]

    def k_block(n, size):
        return lambda which, part: lambda: kall.at[rows(size * mod(which + n, n) + part[0], part[1]), :]

    ring = [
        Gather(NZ, z, 64, 32, zpeer[1], zpeer[NZ - 1], k_block(NZ, 64), core=0),
        Gather(NX, x, 128, 64, xpeer[1], xpeer[NX - 1], k_block(NX, 128), core=1),
    ]

    @on_core
    def _(core):
        base = rows(64 * z + 16 * x, 16) if core == 0 else rows(128 * x + 16 * z, 16)
        kall[base, :] = both
        for go in first[core]:
            go.start()

    l_sum.end()
    row = l_sum.result()
    l_inv = lax.rsqrt(jnp.sum(row * row, axis=1, keepdims=True) + EPS)
    row = row * l_inv
    lunit[...] = row
    l_spread = Spread(lall)
    l_spread.start(row.astype(BF))

    @on_core
    def _(core):
        for go in first[core]:
            go.recv()
        ring[core].step(0)
        ring[core].step(1)

    l_spread.step()

    @on_core
    def _(core):
        for s in range(2, ring[core].n // 2):
            ring[core].step(s)

    l_spread.last()

    mine, theirs = kf[...].astype(F32), kfo[...].astype(F32)
    pieces = []
    for i in range(2 * NH):
        pieces.append(by_group(mine[OWN * i : OWN * (i + 1)], theirs[OWN * i : OWN * (i + 1)]))
    kf2[...] = jnp.concatenate(pieces, axis=0).astype(BF)

    @on_core
    def _(core):
        ring[core].end()

    l_spread.end()

    lead = jnp.where(c == 0, lax.div(mod(z + NZ // 2, NZ), jnp.int32(2)), mod(x + NX // 2, NX))

    def kpi_side(i, carry):
        at = rows(mod(lead + i, 4) * 128, 128, 128)
        inner = dot_t(kall[at, :E], lall[...])
        apart = dot_t(kall[at, E:], lext[...])
        kg[at, :] = dot(pair_gradient(inner, apart), lall[...])
        return carry

    def k_part_of(n, size):
        return lambda which, start, count: kg[rows(size * mod(which + n, n) + start, count), :]

    sums = [
        Sum(NZ, z, 64, 32, zpeer[1], zpeer[NZ - 1], k_part_of(NZ, 64), (zrs, zrr, zls, zlr), core=0),
        Sum(NX, x, 128, 64, xpeer[1], xpeer[NX - 1], k_part_of(NX, 128), (xrs, xrr, xls, xlr), core=1),
    ]

    def step(s):
        @on_core
        def _(core):
            if s < sums[core].n // 2:
                sums[core].step(s)

    kpi_side(0, 0)
    step(0)
    lax.fori_loop(1, COUNT // 128, kpi_side, 0)
    step(1)

    def log_pairs(i, carry):
        at = rows(i * 256, 256, 256)
        inner = dot_t(lall[...], kall[at, :E])
        apart = dot_t(lext[...], kall[at, E:])
        pg[:, at] = pair_gradient(inner, apart)
        return carry

    lax.fori_loop(0, COUNT // 256, log_pairs, 0)
    gsend[...] = dot(pg[rows(HP * (1 - c), HP), :], kall[:, :E]).astype(BF)
    g_core = Send(lambda: gsend, lambda: grecv, partner)
    g_core.start()
    step(2)
    lg[...] = dot(pg[rows(HP * c, HP), :], kall[:, :E])

    g_sum = h_sum(lg, grecv, (grs, grr, gls, glr))
    g_core.recv()
    g_sum.step(0)
    step(3)

    middle = [
        [Send(lambda r=r: midsend.at[r - 1], lambda r=r: midrecv.at[r - 1], xpeer[r], core=0) for r in XS],
        [Send(lambda r=r: midsend.at[r - 1], lambda r=r: midrecv.at[r - 1], zpeer[r], core=1) for r in ZS],
    ]

    g_sum.step(1)

    @on_core
    def _(core):
        at, order = ((x, XS), (z, ZS))[core]
        n = len(order) + 1
        sums[core].end()
        mid[: 16 * n, :] = sums[core].result()
        for r, go in zip(order, middle[core]):
            midsend[r - 1] = mid[rows(16 * mod(at + r, n), 16), :].astype(BF)
            go.start()
        total = mid[rows(16 * at, 16), :]
        for go in middle[core]:
            go.recv()
        for r in range(n - 1):
            total = total + midrecv[r].astype(F32)
        mid16[...] = total

    total = mid16[...]
    unit = kunit[...]
    inner = jnp.sum(unit * total, axis=1, keepdims=True)

    def kblock(hh):
        return lambda: kback.at[rows(16 * (c * NH + hh), 16), :]

    kback[rows(16 * (c * NH + h), 16), :] = (k_inv * (total - unit * inner)).astype(BF)
    kb_waits = [Send(kblock(h), kblock(h), hpeer[r], kblock(hfrom[r])) for r in (2, 1, 3)]
    for go in kb_waits:
        go.start()

    g_sum.end()
    row = g_sum.result()
    unit = lunit[...]
    inner = jnp.sum(unit * row, axis=1, keepdims=True)
    row = (l_inv * (row - unit * inner)).astype(BF)

    def khalf(core):
        return lambda: kback.at[rows(16 * NH * core, 16 * NH), :]

    for go in kb_waits:
        go.recv()
    kb_core = Send(khalf(c), khalf(c), partner, khalf(1 - c))
    kb_core.start()
    b_spread = Spread(back)
    b_spread.start(row)
    kb_core.recv()

    part = lax.dot_general(
        kf2[...], kback[...], (((0,), (0,)), ((), ())), preferred_element_type=F32
    ).astype(BF)
    tall = part.shape[0]
    for j in range(E // 128):
        wbuf[tall * j : tall * (j + 1), :] = part[:, 128 * j : 128 * (j + 1)]
    wbuf[tall * (E // 128) :, :] = jnp.zeros((NZ * WZ - tall * (E // 128), 128), BF)

    def cut_of(ref, size, at):
        return lambda: ref.at[rows(size * at, size), :]

    def slot(ref, at):
        return lambda: ref.at[at]

    w_first = [
        [Send(cut_of(wbuf, WZ, mod(z + r, NZ)), slot(wzr, r - 1), zpeer[r], core=0) for r in ZS],
        [Send(cut_of(wbuf, WX, mod(x + r, NX)), slot(wxr, r - 1), xpeer[r], core=1) for r in XS],
    ]
    w_second = [
        [Send(slot(wx, x), slot(wx, x), xpeer[r], slot(wx, xfrom[r]), 0) for r in XS],
        [Send(cut_of(wxs, BLK, mod(z + r, NZ)), slot(wxzr, r - 1), zpeer[r], core=1) for r in ZS],
    ]
    w_pair = [
        [Send(slot(wy, y), slot(wy, y), ypeer[0, 1], slot(wy, 1 - y), 0)],
        [Send(slot(wys, y), slot(wys, y), ypeer[0, 1], slot(wys, 1 - y), 1)],
    ]
    w_third = [
        [],
        [Send(cut_of(wxz, BLK, z), cut_of(wxz, BLK, z), zpeer[r], cut_of(wxz, BLK, zfrom[r]), 1) for r in ZS],
    ]
    w_last = [
        [Send(slot(wlast, pl.ds(0, WZ)), cut_of(out_w, WZ, z), zpeer[r], cut_of(out_w, WZ, zfrom[r]), 0) for r in ZS],
        [Send(slot(wlast, pl.ds(0, WX)), cut_of(out_w, WX, x), xpeer[r], cut_of(out_w, WX, xfrom[r]), 1) for r in XS],
    ]

    def keep(core):
        size, at = ((WZ, z), (WX, x))[core]
        return pltpu.make_async_copy(wlast.at[pl.ds(0, size)], cut_of(out_w, size, at)(), lsem.at[7])

    def begin(copies):
        for go in copies:
            go.start()

    def arrive(copies):
        for go in copies:
            go.recv()

    @on_core
    def _(core):
        begin(w_first[core])

    b_spread.step()

    @on_core
    def _(core):
        if core == 0:
            total = wbuf[rows(WZ * z, WZ), :].astype(F32)
            arrive(w_first[0])
            for r in range(NZ - 1):
                total = total + wzr[r].astype(F32)
            wx[x] = total.astype(BF)
        else:
            total = wbuf[rows(WX * x, WX), :].astype(F32)
            arrive(w_first[1])
            for r in range(NX - 1):
                total = total + wxr[r].astype(F32)
            wxs[:WX, :] = total.astype(BF)
            wxs[WX:, :] = jnp.zeros((NZ * BLK - WX, 128), BF)
        begin(w_second[core])

    b_spread.last()

    @on_core
    def _(core):
        arrive(w_second[core])
        if core == 0:
            total = wx[0].astype(F32)
            for i in range(1, NX):
                total = total + wx[i].astype(F32)
            wy[y] = total.astype(BF)
        else:
            total = wxs[rows(BLK * z, BLK), :].astype(F32)
            for r in range(NZ - 1):
                total = total + wxzr[r].astype(F32)
            wys[y] = total.astype(BF)
        begin(w_pair[core])


    @on_core
    def _(core):
        arrive(w_pair[core])
        if core == 0:
            wlast[:WZ, :] = (wy[0].astype(F32) + wy[1].astype(F32)).astype(BF)
        else:
            wxz[rows(BLK * z, BLK), :] = (wys[0].astype(F32) + wys[1].astype(F32)).astype(BF)
            begin(w_third[1])
            arrive(w_third[1])
            wlast[...] = wxz[:WX, :]
        begin(w_last[core])
        keep(core).start()

    b_spread.end()
    for i in range(2):
        og[HALF * i : HALF * (i + 1), :] = dot_t(back[HP * i : HP * i + HALF, :], lp[...]).astype(BF)
    g_out = pltpu.make_async_copy(og, out_g, lsem.at[6])
    g_out.start()

    @on_core
    def _(core):
        arrive(w_last[core])
        keep(core).wait()

    finish()
    g_out.wait()


def deliver(g, w, out_g, out_w, held, wall, ow, sem):
    copies = [
        pltpu.make_async_copy(*pair, sem.at[i])
        for i, pair in enumerate(((w, wall), (g, held), (held, out_g), (ow, out_w)))
    ]
    copies[0].start()
    copies[1].start()
    copies[1].wait()
    copies[2].start()
    copies[0].wait()
    tall = out_w.shape[0]
    for j in range(E // 128):
        ow[:, 128 * j : 128 * (j + 1)] = wall[tall * j : tall * (j + 1), :].astype(F32)
    copies[3].start()
    copies[2].wait()
    copies[3].wait()


def body(log_feats, kpi_feats, log_proj, kpi_proj, log_ids, kpi_ids):
    v = pltpu.VMEM
    inputs = (log_feats, kpi_feats, log_proj, kpi_proj, log_ids, kpi_ids.reshape(1, -1))
    outs = (jax.ShapeDtypeStruct(log_feats.shape, BF), jax.ShapeDtypeStruct((NZ * WZ, 128), BF))
    hbm = pl.BlockSpec(memory_space=pltpu.HBM)
    scratch = [v(a.shape, a.dtype) for a in inputs + outs[:1]] + [
        v((HP, E), BF), v((HP, E), BF), v((HP, E), F32), *[v((2, BLK, E), BF)] * 4,
        v((2 * HP, E), BF), v((BLK, E), F32), v((2 * HP, ID), BF),
        v((GROUP, E), F32), v((32, E), BF), v((32, E), BF), v((NH, 16, PK), BF), v((2, NH, 16, PK), BF),
        v(kpi_feats.shape, BF), v((2 * GROUP, kpi_feats.shape[1]), BF), v((1, GROUP), jnp.int32),
        v((COUNT, EK), BF), v((2 * OWN, E), F32),
        v((2 * HP, COUNT), BF), v((COUNT, E), F32), v((HP, E), F32),
        v((HP, E), BF), v((HP, E), BF), *[v((2, BLK, E), BF)] * 4, v((2 * HP, E), BF),
        *[v((4, 64, E), BF)] * 4, *[v((2, 128, E), BF)] * 4,
        v((128, E), F32), v((7, 16, E), BF), v((7, 16, E), BF), v((16, E), F32),
        v((2 * NH * 16, E), BF), v((NZ * WZ, 128), BF), v((NZ - 1, WZ, 128), BF), v((NX - 1, WX, 128), BF),
        v((NX, WZ, 128), BF), v((NY, WZ, 128), BF), v((NZ * BLK, 128), BF), v((NZ - 1, BLK, 128), BF),
        v((NY, BLK, 128), BF), v((NZ * BLK, 128), BF), v((WX, 128), BF),
        pltpu.SemaphoreType.DMA((NSEM,)), pltpu.SemaphoreType.DMA((NSEM,)),
        pltpu.SemaphoreType.DMA((8,)),
    ]
    grads = pl.pallas_call(
        kernel,
        out_shape=outs,
        in_specs=[hbm] * 6,
        out_specs=(hbm,) * 2,
        scratch_shapes=scratch,
        compiler_params=pltpu.CompilerParams(
            collective_id=0, has_side_effects=True, vmem_limit_bytes=62 * 1024 * 1024
        ),
    )(*inputs)
    return pl.pallas_call(
        deliver,
        out_shape=(outs[0], jax.ShapeDtypeStruct(kpi_proj.shape, F32)),
        in_specs=[hbm] * 2,
        out_specs=(hbm,) * 2,
        scratch_shapes=[v(outs[0].shape, BF), v(outs[1].shape, BF), v(kpi_proj.shape, F32), pltpu.SemaphoreType.DMA((4,))],
        compiler_params=pltpu.CompilerParams(vmem_limit_bytes=62 * 1024 * 1024),
    )(*grads)


def solution(mesh):
    return jax.shard_map(
        body,
        mesh=mesh,
        in_specs=(
            P("dp", "tensor"),
            P("dp", "tensor"),
            P("tensor", None),
            P("tensor", None),
            P("dp"),
            P("dp"),
        ),
        out_specs=(P("dp", "tensor"), P("tensor", None)),
        check_vma=False,
    )
```

```python
import jax
import jax.numpy as jnp
from jax import lax
from jax.experimental import pallas as pl
from jax.experimental.pallas import tpu as pltpu
from jax.sharding import PartitionSpec as P

TEMPER = 32.0
BIAS = -2.0
LOSS = 4096.0
EPS = 1e-06
MESH = pl.DeviceIdType.MESH
BF = jnp.bfloat16
F32 = jnp.float32

NY, NX, NZ, NH = 2, 4, 8, 4
LOG = 352
HALF = LOG // 2
BLK = 48
HP = NH * BLK
E = 1152
ID = 128
EK = E + ID
GROUP = 64
OWN = 8
COUNT = NY * NX * NZ * OWN
SCALE = TEMPER * LOSS / (LOG * NY * NX * NZ)
PK = EK // 2
CUT = 32
WZ, WX = 176, 336
XS, ZS = (2, 1, 3), (4, 3, 5, 2, 6, 1, 7)
NSEM = 160


def dot(a, b):
    return jnp.dot(a, b, preferred_element_type=F32)


def dot_t(a, b):
    return lax.dot_general(a, b, (((1,), (1,)), ((), ())), preferred_element_type=F32)


def mod(a, n):
    return lax.rem(a, jnp.int32(n))


def digits(ids):
    high = jnp.floor(ids * (1.0 / 256.0))
    rest = ids - 256.0 * high
    middle = jnp.floor(rest * (1.0 / 16.0))
    return high, middle, rest - 16.0 * middle


def on_lanes(values, rows):
    lane = lax.broadcasted_iota(jnp.int32, (rows, ID), 1)
    out = jnp.zeros((rows, ID), F32)
    for at, value in enumerate(values):
        out = jnp.where(lane == at, value, out)
    return out


def pair_gradient(inner, apart):
    sign = jnp.where(apart < 0.5, 1.0, -1.0).astype(F32)
    margin = -sign * (TEMPER * inner + BIAS)
    return (-SCALE * sign * jax.nn.sigmoid(margin)).astype(BF)


def kernel(
    lf_h, kf_h, lp_h, kp_h, lid_h, kid_h, out_g, out_w,
    lf, kf, lp, kp, lid, kid, og,
    lsend, lrecv, lacc, lrs, lrr, lls, llr, lall, lunit, lext,
    kacc, ksend, krecv, kysend, kyrecv, kfo, kf2, kido, kall, kunit,
    pg, kg, lg, gsend, grecv, grs, grr, gls, glr, back,
    zrs, zrr, zls, zlr, xrs, xrr, xls, xlr, mid, midsend, midrecv, mid16,
    kback, wbuf, wzr, wxr, wx, wy, wxs, wxzr, wys, wxz, wlast,
    ssem, rsem, lsem,
):
    d = lax.axis_index("dp")
    t = lax.axis_index("tensor")
    y = lax.div(d, jnp.int32(NX * NZ))
    x = mod(lax.div(d, jnp.int32(NZ)), NX)
    z = mod(d, NZ)
    h = lax.div(t, jnp.int32(2))
    c = mod(t, 2)

    def place(y=y, x=x, z=z, h=h, c=c):
        return {"dp": (y * NX + x) * NZ + z, "tensor": h * 2 + c}

    def rows(start, size, unit=16):
        return pl.ds(pl.multiple_of(start, unit), size)

    started = []

    class Send:
        def __init__(self, src, dst, to, land=None, core=None):
            self.src, self.dst, self.to, self.core = src, dst, to, core
            self.land = land or dst
            self.at = len(started)
            self.open, self.begun = True, False
            started.append(self)
            assert self.at < NSEM

        def copy(self, src, dst):
            return pltpu.make_async_remote_copy(
                src_ref=src(), dst_ref=dst(), send_sem=ssem.at[self.at], recv_sem=rsem.at[self.at],
                device_id=self.to, device_id_type=MESH,
            )

        def start(self):
            self.begun = True
            self.copy(self.src, self.dst).start()

        def recv(self):
            self.open = False
            self.copy(self.land, self.land).wait_recv()

        def sent(self):
            self.copy(self.src, self.dst).wait_send()

    def finish():
        for core in (None, 0, 1):

            def ends(core=core):
                for go in started:
                    if go.core == core and go.begun:
                        if go.open:
                            go.recv()
                        go.sent()

            if core is None:
                ends()
            else:
                pl.when(c == core)(ends)

    inputs = [
        pltpu.make_async_copy(a, b, lsem.at[i])
        for i, (a, b) in enumerate(((kf_h, kf), (kp_h, kp), (lf_h, lf), (lp_h, lp), (kid_h, kid), (lid_h, lid)))
    ]
    for go in inputs:
        go.start()

    partner = place(c=1 - c)
    ypeer = {(r, f): place(h=mod(h + r, NH), y=y if f == 0 else 1 - y) for r in range(NH) for f in (0, 1)}
    hpeer = [place(h=mod(h + r, NH)) for r in range(NH)]
    hfrom = [mod(h + NH - r, NH) for r in range(NH)]
    xpeer = [place(x=mod(x + r, NX)) for r in range(NX)]
    xfrom = [mod(x + NX - r, NX) for r in range(NX)]
    zpeer = [place(z=mod(z + r, NZ)) for r in range(NZ)]
    zfrom = [mod(z + NZ - r, NZ) for r in range(NZ)]

    barrier = pltpu.get_barrier_semaphore()
    peers = [partner] + [ypeer[k] for k in ypeer if k != (0, 0)] + xpeer[1:] + zpeer[1:]
    for device in peers:
        pl.semaphore_signal(barrier, inc=1, device_id=device, device_id_type=MESH)

    def on_core(run):
        for core in (0, 1):
            pl.when(c == core)(lambda core=core: run(core))

    def packed(v):
        if v.shape[1] < EK:
            v = jnp.concatenate([v, jnp.zeros((OWN, EK - v.shape[1]), F32)], axis=1)
        return jnp.concatenate([v[:, :PK], v[:, PK:]], axis=0).astype(BF)

    def unpacked(v):
        v = v.astype(F32)
        return jnp.concatenate([v[:OWN], v[OWN:]], axis=1)

    class Gather:
        def __init__(self, n, at, size, split, right, left, block, sign=1, core=None):
            self.n, self.go = n, []
            low, high = (0, split), (split, size - split)
            ways = [(right, -sign, low), (left, sign, high), (right, -sign, high), (left, sign, low)]
            for s in range(n // 2):
                step = []
                for to, way, part in ways if s < n // 2 - 1 else ways[:2]:
                    there, here = block(at + way * s, part), block(at + way * (s + 1), part)
                    step.append(Send(there, there, to, here, core))
                self.go.append(step)

        def step(self, s):
            for i, go in enumerate(self.go[s]):
                if s > 0:
                    self.go[s - 1][i].recv()
                go.start()

        def recv(self, s):
            for go in self.go[s]:
                if go.open:
                    go.recv()

        def end(self):
            for s in range(self.n // 2):
                self.recv(s)

    class Sum:
        def __init__(self, n, at, size, split, right, left, part, bufs, sign=1, core=None):
            self.n, self.at, self.size, self.part = n, at, size, part
            self.rs, self.rr, self.ls, self.lr = bufs
            low, high = (0, split), (split, size - split)
            r, l = (right, sign, self.rs, self.rr), (left, -sign, self.ls, self.lr)
            self.ways = [(*r, low), (*l, high), (*r, high), (*l, low)]
            self.go = []
            for s in range(n // 2):
                step = []
                for to, _, send, come, p in self.ways[:2] if s == 0 else self.ways:
                    src = lambda s=s, p=p, send=send: send.at[s, pl.ds(*p)]
                    dst = lambda s=s, p=p, come=come: come.at[s, pl.ds(*p)]
                    step.append(Send(src, dst, to, core=core))
                self.go.append(step)

        def step(self, s):
            for i in (0, 1) if s == 0 else (2, 3, 0, 1):
                _, way, send, come, p = self.ways[i]
                value = self.part(self.at + way * (self.n // 2 - s), *p)
                if s > 1 or (s == 1 and i < 2):
                    self.go[s - 1][i].recv()
                    value = value + come[s - 1, pl.ds(*p), :].astype(F32)
                send[s, pl.ds(*p), :] = value.astype(BF)
                self.go[s][i].start()

        def end(self):
            for go in self.go[-1]:
                go.recv()

        def result(self):
            last = self.n // 2 - 1
            return self.part(self.at, 0, self.size) + self.rr[last].astype(F32) + self.lr[last].astype(F32)

    turn = 1 - 2 * c
    h_right = place(h=mod(h + turn + NH, NH))
    h_left = place(h=mod(h - turn + NH, NH))

    def h_sum(own, come, bufs):
        def part(which, start, size):
            at = rows(BLK * mod(which + NH, NH) + start, size)
            return own[at, :] + come[at, :].astype(F32)

        return Sum(NH, h, BLK, CUT, h_right, h_left, part, bufs, turn)

    class Spread:
        def __init__(self, buffer):
            self.buffer = buffer

            def at_core(core):
                def block(hh, part=(0, BLK)):
                    return lambda: buffer.at[rows(HP * core + BLK * mod(hh + NH, NH) + part[0], part[1]), :]

                return block

            mine, other = at_core(c), at_core(1 - c)
            self.along = Gather(NH, h, BLK, CUT, h_right, h_left, mine, turn)
            self.across = {r: Send(mine(h - r), mine(h - r), partner, other(h - r)) for r in (0, 1, 3, 2)}

        def start(self, value):
            self.buffer[rows(HP * c + BLK * h, BLK), :] = value
            self.along.step(0)
            self.across[0].start()

        def step(self):
            self.along.step(1)
            self.along.recv(0)
            self.across[1].start()
            self.across[3].start()

        def last(self):
            self.along.recv(1)
            self.across[2].start()

        def end(self):
            for go in self.across.values():
                go.recv()

    inputs[0].wait()
    inputs[1].wait()
    kacc[...] = dot(kf[...], kp[...])
    ksend[...] = kacc[rows(32 * (1 - c), 32, 32), :].astype(BF)
    inputs[2].wait()
    inputs[3].wait()
    lsend[:HALF, :] = dot(lf[rows(HALF * (1 - c), HALF), :], lp[...]).astype(BF)
    lsend[HALF:, :] = jnp.zeros((HP - HALF, E), BF)
    inputs[4].wait()
    inputs[5].wait()

    pl.semaphore_wait(barrier, len(peers))
    k_core = Send(lambda: ksend, lambda: krecv, partner)
    k_core.start()
    l_core = {}
    for r in (2, 1, 3, 0):
        out = lambda r=r: lsend.at[rows(BLK * mod(h + r, NH), BLK), :]
        come = lambda r=r: lrecv.at[rows(BLK * mod(h + r, NH), BLK), :]
        l_core[r] = Send(out, come, partner)
        l_core[r].start()

    lacc[:HALF, :] = dot(lf[rows(HALF * c, HALF), :], lp[...])
    lacc[HALF:, :] = jnp.zeros((HP - HALF, E), F32)

    f_copy = Send(lambda: kf, lambda: kfo, ypeer[0, 1])
    f_copy.start()
    i_copy = Send(lambda: kid, lambda: kido, ypeer[0, 1])
    i_copy.start()

    k_core.recv()
    kacc[rows(32 * c, 32, 32), :] += krecv[...].astype(F32)
    k_waits = []
    for r in (2, 1, 3, 0):
        kysend[r] = packed(kacc[rows(32 * c + OWN * mod(h + r, NH), OWN, OWN), :])
        for f in (0, 1):
            if (r, f) != (0, 0):
                go = Send(lambda r=r: kysend.at[r], lambda r=r, f=f: kyrecv.at[f, r], ypeer[r, f])
                go.start()
                k_waits.append(go)

    l_sum = h_sum(lacc, lrecv, (lrs, lrr, lls, llr))
    l_core[2].recv()
    l_sum.step(0)
    for r in (1, 3, 0):
        l_core[r].recv()

    i_copy.recv()
    f_copy.recv()

    def by_group(own, other):
        return jnp.concatenate([jnp.where(y == 0, own, other), jnp.where(y == 0, other, own)], axis=0)

    row_ids = lax.broadcasted_iota(jnp.int32, (OWN, GROUP), 0) + (32 * c + OWN * h)
    col_ids = lax.broadcasted_iota(jnp.int32, (OWN, GROUP), 1)

    def id_column(ref):
        return jnp.sum(jnp.where(row_ids == col_ids, ref[...].astype(F32), 0.0), axis=1, keepdims=True)

    k_id = by_group(id_column(kid), id_column(kido))
    one = jnp.ones_like(k_id)
    k_digit = digits(k_id)
    k_ext = on_lanes(list(k_digit) + [g * g for g in k_digit] + [one] * 3, 2 * OWN)

    at = lax.broadcasted_iota(jnp.int32, (2 * HP, LOG), 0)
    upper = at >= HP
    inside = jnp.where(upper, at - HP, at)
    at = jnp.where(inside < HALF, jnp.where(upper, inside + HALF, inside), -1)
    col = lax.broadcasted_iota(jnp.int32, (2 * HP, LOG), 1)
    log_id = jnp.sum(jnp.where(at == col, lid[...].reshape(1, LOG).astype(F32), 0.0), axis=1, keepdims=True)
    one = jnp.ones_like(log_id)
    log_digit = digits(log_id)
    lext[...] = on_lanes([-2.0 * g for g in log_digit] + [one] * 3 + [g * g for g in log_digit], 2 * HP).astype(BF)

    l_sum.step(1)

    for go in k_waits:
        go.recv()
    own, other = unpacked(kysend[0]), unpacked(kyrecv[1, 0])
    for r in range(1, NH):
        own = own + unpacked(kyrecv[0, r])
        other = other + unpacked(kyrecv[1, r])
    unit = by_group(own, other)[:, :E]
    k_inv = lax.rsqrt(jnp.sum(unit * unit, axis=1, keepdims=True) + EPS)
    unit = unit * k_inv
    kunit[...] = unit
    both = jnp.concatenate([unit, k_ext], axis=1).astype(BF)

    def block0(zz, xx):
        return kall.at[rows(64 * zz + 16 * xx, 16), :]

    def block1(zz, xx):
        return kall.at[rows(128 * xx + 16 * zz, 16), :]

    own0 = lambda: block0(z, x)
    own1 = lambda: block1(z, x)
    first = [
        [Send(own0, own0, xpeer[r], lambda r=r: block0(z, xfrom[r]), 0) for r in XS],
        [Send(own1, own1, zpeer[r], lambda r=r: block1(zfrom[r], x), 1) for r in ZS],
    ]

    def k_block(n, size):
        return lambda which, part: lambda: kall.at[rows(size * mod(which + n, n) + part[0], part[1]), :]

    ring = [
        Gather(NZ, z, 64, 32, zpeer[1], zpeer[NZ - 1], k_block(NZ, 64), core=0),
        Gather(NX, x, 128, 64, xpeer[1], xpeer[NX - 1], k_block(NX, 128), core=1),
    ]

    @on_core
    def _(core):
        base = rows(64 * z + 16 * x, 16) if core == 0 else rows(128 * x + 16 * z, 16)
        kall[base, :] = both
        for go in first[core]:
            go.start()

    l_sum.end()
    row = l_sum.result()
    l_inv = lax.rsqrt(jnp.sum(row * row, axis=1, keepdims=True) + EPS)
    row = row * l_inv
    lunit[...] = row
    l_spread = Spread(lall)
    l_spread.start(row.astype(BF))

    @on_core
    def _(core):
        for go in first[core]:
            go.recv()
        ring[core].step(0)
        ring[core].step(1)

    l_spread.step()

    @on_core
    def _(core):
        for s in range(2, ring[core].n // 2):
            ring[core].step(s)

    l_spread.last()

    mine, theirs = kf[...].astype(F32), kfo[...].astype(F32)
    pieces = []
    for i in range(2 * NH):
        pieces.append(by_group(mine[OWN * i : OWN * (i + 1)], theirs[OWN * i : OWN * (i + 1)]))
    kf2[...] = jnp.concatenate(pieces, axis=0).astype(BF)

    @on_core
    def _(core):
        ring[core].end()

    l_spread.end()

    lead = jnp.where(c == 0, lax.div(mod(z + NZ // 2, NZ), jnp.int32(2)), mod(x + NX // 2, NX))

    def kpi_side(i, carry):
        at = rows(mod(lead + i, 4) * 128, 128, 128)
        inner = dot_t(kall[at, :E], lall[...])
        apart = dot_t(kall[at, E:], lext[...])
        kg[at, :] = dot(pair_gradient(inner, apart), lall[...])
        return carry

    def k_part_of(n, size):
        return lambda which, start, count: kg[rows(size * mod(which + n, n) + start, count), :]

    sums = [
        Sum(NZ, z, 64, 32, zpeer[1], zpeer[NZ - 1], k_part_of(NZ, 64), (zrs, zrr, zls, zlr), core=0),
        Sum(NX, x, 128, 64, xpeer[1], xpeer[NX - 1], k_part_of(NX, 128), (xrs, xrr, xls, xlr), core=1),
    ]

    def step(s):
        @on_core
        def _(core):
            if s < sums[core].n // 2:
                sums[core].step(s)

    kpi_side(0, 0)
    step(0)
    lax.fori_loop(1, COUNT // 128, kpi_side, 0)
    step(1)

    def log_pairs(i, carry):
        at = rows(i * 256, 256, 256)
        inner = dot_t(lall[...], kall[at, :E])
        apart = dot_t(lext[...], kall[at, E:])
        pg[:, at] = pair_gradient(inner, apart)
        return carry

    lax.fori_loop(0, COUNT // 256, log_pairs, 0)
    step(2)
    gsend[...] = dot(pg[rows(HP * (1 - c), HP), :], kall[:, :E]).astype(BF)
    g_core = Send(lambda: gsend, lambda: grecv, partner)
    g_core.start()
    lg[...] = dot(pg[rows(HP * c, HP), :], kall[:, :E])

    g_sum = h_sum(lg, grecv, (grs, grr, gls, glr))
    step(3)
    g_core.recv()
    g_sum.step(0)

    middle = [
        [Send(lambda r=r: midsend.at[r - 1], lambda r=r: midrecv.at[r - 1], xpeer[r], core=0) for r in XS],
        [Send(lambda r=r: midsend.at[r - 1], lambda r=r: midrecv.at[r - 1], zpeer[r], core=1) for r in ZS],
    ]

    @on_core
    def _(core):
        at, order = ((x, XS), (z, ZS))[core]
        n = len(order) + 1
        sums[core].end()
        mid[: 16 * n, :] = sums[core].result()
        for r, go in zip(order, middle[core]):
            midsend[r - 1] = mid[rows(16 * mod(at + r, n), 16), :].astype(BF)
            go.start()

    g_sum.step(1)

    @on_core
    def _(core):
        at, order = ((x, XS), (z, ZS))[core]
        n = len(order) + 1
        total = mid[rows(16 * at, 16), :]
        for go in middle[core]:
            go.recv()
        for r in range(n - 1):
            total = total + midrecv[r].astype(F32)
        mid16[...] = total

    total = mid16[...]
    unit = kunit[...]
    inner = jnp.sum(unit * total, axis=1, keepdims=True)

    def kblock(core, hh):
        return lambda: kback.at[rows(16 * (core * NH + hh), 16), :]

    kback[rows(16 * (c * NH + h), 16), :] = (k_inv * (total - unit * inner)).astype(BF)
    kb_waits = {r: Send(kblock(c, h), kblock(c, h), hpeer[r], kblock(c, hfrom[r])) for r in (2, 1, 3)}
    for go in kb_waits.values():
        go.start()
    kb_core = {
        r: Send(kblock(c, hfrom[r]), kblock(c, hfrom[r]), partner, kblock(1 - c, hfrom[r])) for r in range(NH)
    }
    kb_core[0].start()

    g_sum.end()
    row = g_sum.result()
    unit = lunit[...]
    inner = jnp.sum(unit * row, axis=1, keepdims=True)
    row = (l_inv * (row - unit * inner)).astype(BF)

    for r in (1, 3, 2):
        kb_waits[r].recv()
        kb_core[r].start()
    b_spread = Spread(back)
    b_spread.start(row)
    for r in (0, 1, 3, 2):
        kb_core[r].recv()

    part = lax.dot_general(
        kf2[...], kback[...], (((0,), (0,)), ((), ())), preferred_element_type=F32
    ).astype(BF)
    tall = part.shape[0]
    for j in range(E // 128):
        wbuf[tall * j : tall * (j + 1), :] = part[:, 128 * j : 128 * (j + 1)]
    wbuf[tall * (E // 128) :, :] = jnp.zeros((NZ * WZ - tall * (E // 128), 128), BF)

    def cut_of(ref, size, at):
        return lambda: ref.at[rows(size * at, size), :]

    def slot(ref, at):
        return lambda: ref.at[at]

    w_first = [
        [Send(cut_of(wbuf, WZ, mod(z + r, NZ)), slot(wzr, r - 1), zpeer[r], core=0) for r in ZS],
        [Send(cut_of(wbuf, WX, mod(x + r, NX)), slot(wxr, r - 1), xpeer[r], core=1) for r in XS],
    ]
    w_second = [
        [Send(slot(wx, x), slot(wx, x), xpeer[r], slot(wx, xfrom[r]), 0) for r in XS],
        [Send(cut_of(wxs, BLK, mod(z + r, NZ)), slot(wxzr, r - 1), zpeer[r], core=1) for r in ZS],
    ]
    w_pair = [
        [Send(slot(wy, y), slot(wy, y), ypeer[0, 1], slot(wy, 1 - y), 0)],
        [Send(slot(wys, y), slot(wys, y), ypeer[0, 1], slot(wys, 1 - y), 1)],
    ]
    w_third = [
        [],
        [Send(cut_of(wxz, BLK, z), cut_of(wxz, BLK, z), zpeer[r], cut_of(wxz, BLK, zfrom[r]), 1) for r in ZS],
    ]
    w_last = [
        [Send(slot(wlast, pl.ds(0, WZ)), cut_of(out_w, WZ, z), zpeer[r], cut_of(out_w, WZ, zfrom[r]), 0) for r in ZS],
        [Send(slot(wlast, pl.ds(0, WX)), cut_of(out_w, WX, x), xpeer[r], cut_of(out_w, WX, xfrom[r]), 1) for r in XS],
    ]

    def keep(core):
        size, at = ((WZ, z), (WX, x))[core]
        return pltpu.make_async_copy(wlast.at[pl.ds(0, size)], cut_of(out_w, size, at)(), lsem.at[7])

    def begin(copies):
        for go in copies:
            go.start()

    def arrive(copies):
        for go in copies:
            go.recv()

    @on_core
    def _(core):
        begin(w_first[core])

    b_spread.step()

    @on_core
    def _(core):
        if core == 0:
            total = wbuf[rows(WZ * z, WZ), :].astype(F32)
            arrive(w_first[0])
            for r in range(NZ - 1):
                total = total + wzr[r].astype(F32)
            wx[x] = total.astype(BF)
        else:
            total = wbuf[rows(WX * x, WX), :].astype(F32)
            arrive(w_first[1])
            for r in range(NX - 1):
                total = total + wxr[r].astype(F32)
            wxs[:WX, :] = total.astype(BF)
            wxs[WX:, :] = jnp.zeros((NZ * BLK - WX, 128), BF)
        begin(w_second[core])

    b_spread.last()

    @on_core
    def _(core):
        arrive(w_second[core])
        if core == 0:
            total = wx[0].astype(F32)
            for i in range(1, NX):
                total = total + wx[i].astype(F32)
            wy[y] = total.astype(BF)
        else:
            total = wxs[rows(BLK * z, BLK), :].astype(F32)
            for r in range(NZ - 1):
                total = total + wxzr[r].astype(F32)
            wys[y] = total.astype(BF)
        begin(w_pair[core])


    @on_core
    def _(core):
        arrive(w_pair[core])
        if core == 0:
            wlast[:WZ, :] = (wy[0].astype(F32) + wy[1].astype(F32)).astype(BF)
        else:
            wxz[rows(BLK * z, BLK), :] = (wys[0].astype(F32) + wys[1].astype(F32)).astype(BF)
            begin(w_third[1])
            arrive(w_third[1])
            wlast[...] = wxz[:WX, :]
        begin(w_last[core])
        keep(core).start()

    b_spread.end()
    for i in range(2):
        og[HALF * i : HALF * (i + 1), :] = dot_t(back[HP * i : HP * i + HALF, :], lp[...]).astype(BF)
    g_out = pltpu.make_async_copy(og, out_g, lsem.at[6])
    g_out.start()

    @on_core
    def _(core):
        arrive(w_last[core])
        keep(core).wait()

    finish()
    g_out.wait()


def deliver(g, w, out_g, out_w, held, wall, ow, sem):
    copies = [
        pltpu.make_async_copy(*pair, sem.at[i])
        for i, pair in enumerate(((w, wall), (g, held), (held, out_g), (ow, out_w)))
    ]
    copies[0].start()
    copies[1].start()
    copies[1].wait()
    copies[2].start()
    copies[0].wait()
    tall = out_w.shape[0]
    for j in range(E // 128):
        ow[:, 128 * j : 128 * (j + 1)] = wall[tall * j : tall * (j + 1), :].astype(F32)
    copies[3].start()
    copies[2].wait()
    copies[3].wait()


def body(log_feats, kpi_feats, log_proj, kpi_proj, log_ids, kpi_ids):
    v = pltpu.VMEM
    inputs = (log_feats, kpi_feats, log_proj, kpi_proj, log_ids, kpi_ids.reshape(1, -1))
    outs = (jax.ShapeDtypeStruct(log_feats.shape, BF), jax.ShapeDtypeStruct((NZ * WZ, 128), BF))
    hbm = pl.BlockSpec(memory_space=pltpu.HBM)
    scratch = [v(a.shape, a.dtype) for a in inputs + outs[:1]] + [
        v((HP, E), BF), v((HP, E), BF), v((HP, E), F32), *[v((2, BLK, E), BF)] * 4,
        v((2 * HP, E), BF), v((BLK, E), F32), v((2 * HP, ID), BF),
        v((GROUP, E), F32), v((32, E), BF), v((32, E), BF), v((NH, 16, PK), BF), v((2, NH, 16, PK), BF),
        v(kpi_feats.shape, BF), v((2 * GROUP, kpi_feats.shape[1]), BF), v((1, GROUP), jnp.int32),
        v((COUNT, EK), BF), v((2 * OWN, E), F32),
        v((2 * HP, COUNT), BF), v((COUNT, E), F32), v((HP, E), F32),
        v((HP, E), BF), v((HP, E), BF), *[v((2, BLK, E), BF)] * 4, v((2 * HP, E), BF),
        *[v((4, 64, E), BF)] * 4, *[v((2, 128, E), BF)] * 4,
        v((128, E), F32), v((7, 16, E), BF), v((7, 16, E), BF), v((16, E), F32),
        v((2 * NH * 16, E), BF), v((NZ * WZ, 128), BF), v((NZ - 1, WZ, 128), BF), v((NX - 1, WX, 128), BF),
        v((NX, WZ, 128), BF), v((NY, WZ, 128), BF), v((NZ * BLK, 128), BF), v((NZ - 1, BLK, 128), BF),
        v((NY, BLK, 128), BF), v((NZ * BLK, 128), BF), v((WX, 128), BF),
        pltpu.SemaphoreType.DMA((NSEM,)), pltpu.SemaphoreType.DMA((NSEM,)),
        pltpu.SemaphoreType.DMA((8,)),
    ]
    grads = pl.pallas_call(
        kernel,
        out_shape=outs,
        in_specs=[hbm] * 6,
        out_specs=(hbm,) * 2,
        scratch_shapes=scratch,
        compiler_params=pltpu.CompilerParams(
            collective_id=0, has_side_effects=True, vmem_limit_bytes=62 * 1024 * 1024
        ),
    )(*inputs)
    return pl.pallas_call(
        deliver,
        out_shape=(outs[0], jax.ShapeDtypeStruct(kpi_proj.shape, F32)),
        in_specs=[hbm] * 2,
        out_specs=(hbm,) * 2,
        scratch_shapes=[v(outs[0].shape, BF), v(outs[1].shape, BF), v(kpi_proj.shape, F32), pltpu.SemaphoreType.DMA((4,))],
        compiler_params=pltpu.CompilerParams(vmem_limit_bytes=62 * 1024 * 1024),
    )(*grads)


def solution(mesh):
    return jax.shard_map(
        body,
        mesh=mesh,
        in_specs=(
            P("dp", "tensor"),
            P("dp", "tensor"),
            P("tensor", None),
            P("tensor", None),
            P("dp"),
            P("dp"),
        ),
        out_specs=(P("dp", "tensor"), P("tensor", None)),
        check_vma=False,
    )
```

```python
import jax
import jax.numpy as jnp
from jax import lax
from jax.experimental import pallas as pl
from jax.experimental.pallas import tpu as pltpu
from jax.sharding import PartitionSpec as P

TEMPER = 32.0
BIAS = -2.0
LOSS = 4096.0
EPS = 1e-06
MESH = pl.DeviceIdType.MESH
BF = jnp.bfloat16
F32 = jnp.float32

NY, NX, NZ, NH = 2, 4, 8, 4
LOG = 352
HALF = LOG // 2
BLK = 48
HP = NH * BLK
E = 1152
ID = 128
EK = E + ID
GROUP = 64
OWN = 8
COUNT = NY * NX * NZ * OWN
SCALE = TEMPER * LOSS / (LOG * NY * NX * NZ)
PK = EK // 2
CUT = 32
WZ, WX = 176, 336
XS, ZS = (2, 1, 3), (4, 3, 5, 2, 6, 1, 7)
NSEM = 160


def dot(a, b):
    return jnp.dot(a, b, preferred_element_type=F32)


def dot_t(a, b):
    return lax.dot_general(a, b, (((1,), (1,)), ((), ())), preferred_element_type=F32)


def mod(a, n):
    return lax.rem(a, jnp.int32(n))


def digits(ids):
    high = jnp.floor(ids * (1.0 / 256.0))
    rest = ids - 256.0 * high
    middle = jnp.floor(rest * (1.0 / 16.0))
    return high, middle, rest - 16.0 * middle


def on_lanes(values, rows):
    lane = lax.broadcasted_iota(jnp.int32, (rows, ID), 1)
    out = jnp.zeros((rows, ID), F32)
    for at, value in enumerate(values):
        out = jnp.where(lane == at, value, out)
    return out


def pair_gradient(inner, apart):
    sign = jnp.where(apart < 0.5, 1.0, -1.0).astype(F32)
    margin = -sign * (TEMPER * inner + BIAS)
    return (-SCALE * sign * jax.nn.sigmoid(margin)).astype(BF)


def kernel(
    lf_h, kf_h, lp_h, kp_h, lid_h, kid_h, out_g, out_w,
    lf, kf, lp, kp, lid, kid, og,
    lsend, lrecv, lacc, lrs, lrr, lls, llr, lall, lunit, lext,
    kacc, ksend, krecv, kysend, kyrecv, kfo, kf2, kido, kall, kunit,
    pg, kg, lg, gsend, grecv, grs, grr, gls, glr, back,
    zrs, zrr, zls, zlr, xrs, xrr, xls, xlr, mid, midsend, midrecv, mid16,
    kback, wbuf, wzr, wxr, wx, wy, wxs, wxzr, wys, wxz, wlast,
    ssem, rsem, lsem,
):
    d = lax.axis_index("dp")
    t = lax.axis_index("tensor")
    y = lax.div(d, jnp.int32(NX * NZ))
    x = mod(lax.div(d, jnp.int32(NZ)), NX)
    z = mod(d, NZ)
    h = lax.div(t, jnp.int32(2))
    c = mod(t, 2)

    def place(y=y, x=x, z=z, h=h, c=c):
        return {"dp": (y * NX + x) * NZ + z, "tensor": h * 2 + c}

    def rows(start, size, unit=16):
        return pl.ds(pl.multiple_of(start, unit), size)

    started = []

    class Send:
        def __init__(self, src, dst, to, land=None, core=None):
            self.src, self.dst, self.to, self.core = src, dst, to, core
            self.land = land or dst
            self.at = len(started)
            self.open, self.begun = True, False
            started.append(self)
            assert self.at < NSEM

        def copy(self, src, dst):
            return pltpu.make_async_remote_copy(
                src_ref=src(), dst_ref=dst(), send_sem=ssem.at[self.at], recv_sem=rsem.at[self.at],
                device_id=self.to, device_id_type=MESH,
            )

        def start(self):
            self.begun = True
            self.copy(self.src, self.dst).start()

        def recv(self):
            self.open = False
            self.copy(self.land, self.land).wait_recv()

        def sent(self):
            self.copy(self.src, self.dst).wait_send()

    def finish():
        for core in (None, 0, 1):

            def ends(core=core):
                for go in started:
                    if go.core == core and go.begun:
                        if go.open:
                            go.recv()
                        go.sent()

            if core is None:
                ends()
            else:
                pl.when(c == core)(ends)

    inputs = [
        pltpu.make_async_copy(a, b, lsem.at[i])
        for i, (a, b) in enumerate(((kf_h, kf), (kp_h, kp), (lf_h, lf), (lp_h, lp), (kid_h, kid), (lid_h, lid)))
    ]
    for go in inputs:
        go.start()

    partner = place(c=1 - c)
    ypeer = {(r, f): place(h=mod(h + r, NH), y=y if f == 0 else 1 - y) for r in range(NH) for f in (0, 1)}
    hpeer = [place(h=mod(h + r, NH)) for r in range(NH)]
    hfrom = [mod(h + NH - r, NH) for r in range(NH)]
    xpeer = [place(x=mod(x + r, NX)) for r in range(NX)]
    xfrom = [mod(x + NX - r, NX) for r in range(NX)]
    zpeer = [place(z=mod(z + r, NZ)) for r in range(NZ)]
    zfrom = [mod(z + NZ - r, NZ) for r in range(NZ)]

    barrier = pltpu.get_barrier_semaphore()
    peers = [partner] + [ypeer[k] for k in ypeer if k != (0, 0)] + xpeer[1:] + zpeer[1:]
    for device in peers:
        pl.semaphore_signal(barrier, inc=1, device_id=device, device_id_type=MESH)

    def on_core(run):
        for core in (0, 1):
            pl.when(c == core)(lambda core=core: run(core))

    def packed(v):
        if v.shape[1] < EK:
            v = jnp.concatenate([v, jnp.zeros((OWN, EK - v.shape[1]), F32)], axis=1)
        return jnp.concatenate([v[:, :PK], v[:, PK:]], axis=0).astype(BF)

    def unpacked(v):
        v = v.astype(F32)
        return jnp.concatenate([v[:OWN], v[OWN:]], axis=1)

    class Gather:
        def __init__(self, n, at, size, split, right, left, block, sign=1, core=None):
            self.n, self.go = n, []
            low, high = (0, split), (split, size - split)
            ways = [(right, -sign, low), (left, sign, high), (right, -sign, high), (left, sign, low)]
            for s in range(n // 2):
                step = []
                for to, way, part in ways if s < n // 2 - 1 else ways[:2]:
                    there, here = block(at + way * s, part), block(at + way * (s + 1), part)
                    step.append(Send(there, there, to, here, core))
                self.go.append(step)

        def step(self, s):
            for i, go in enumerate(self.go[s]):
                if s > 0:
                    self.go[s - 1][i].recv()
                go.start()

        def recv(self, s):
            for go in self.go[s]:
                if go.open:
                    go.recv()

        def end(self):
            for s in range(self.n // 2):
                self.recv(s)

    class Sum:
        def __init__(self, n, at, size, split, right, left, part, bufs, sign=1, core=None):
            self.n, self.at, self.size, self.part = n, at, size, part
            self.rs, self.rr, self.ls, self.lr = bufs
            low, high = (0, split), (split, size - split)
            r, l = (right, sign, self.rs, self.rr), (left, -sign, self.ls, self.lr)
            self.ways = [(*r, low), (*l, high), (*r, high), (*l, low)]
            self.go = []
            for s in range(n // 2):
                step = []
                for to, _, send, come, p in self.ways[:2] if s == 0 else self.ways:
                    src = lambda s=s, p=p, send=send: send.at[s, pl.ds(*p)]
                    dst = lambda s=s, p=p, come=come: come.at[s, pl.ds(*p)]
                    step.append(Send(src, dst, to, core=core))
                self.go.append(step)

        def step(self, s):
            for i in (0, 1) if s == 0 else (2, 3, 0, 1):
                _, way, send, come, p = self.ways[i]
                value = self.part(self.at + way * (self.n // 2 - s), *p)
                if s > 1 or (s == 1 and i < 2):
                    self.go[s - 1][i].recv()
                    value = value + come[s - 1, pl.ds(*p), :].astype(F32)
                send[s, pl.ds(*p), :] = value.astype(BF)
                self.go[s][i].start()

        def end(self):
            for go in self.go[-1]:
                go.recv()

        def result(self):
            last = self.n // 2 - 1
            return self.part(self.at, 0, self.size) + self.rr[last].astype(F32) + self.lr[last].astype(F32)

    turn = 1 - 2 * c
    h_right = place(h=mod(h + turn + NH, NH))
    h_left = place(h=mod(h - turn + NH, NH))

    def h_sum(own, come, bufs):
        def part(which, start, size):
            at = rows(BLK * mod(which + NH, NH) + start, size)
            return own[at, :] + come[at, :].astype(F32)

        return Sum(NH, h, BLK, CUT, h_right, h_left, part, bufs, turn)

    class Spread:
        def __init__(self, buffer):
            self.buffer = buffer

            def at_core(core):
                def block(hh, part=(0, BLK)):
                    return lambda: buffer.at[rows(HP * core + BLK * mod(hh + NH, NH) + part[0], part[1]), :]

                return block

            mine, other = at_core(c), at_core(1 - c)
            self.along = Gather(NH, h, BLK, CUT, h_right, h_left, mine, turn)
            self.across = {r: Send(mine(h - r), mine(h - r), partner, other(h - r)) for r in (0, 1, 3, 2)}

        def start(self, value):
            self.buffer[rows(HP * c + BLK * h, BLK), :] = value
            self.along.step(0)
            self.across[0].start()

        def step(self):
            self.along.step(1)
            self.along.recv(0)
            self.across[1].start()
            self.across[3].start()

        def last(self):
            self.along.recv(1)
            self.across[2].start()

        def end(self):
            for go in self.across.values():
                go.recv()

    inputs[0].wait()
    inputs[1].wait()
    kacc[...] = dot(kf[...], kp[...])
    ksend[...] = kacc[rows(32 * (1 - c), 32, 32), :].astype(BF)
    inputs[2].wait()
    inputs[3].wait()
    lsend[:HALF, :] = dot(lf[rows(HALF * (1 - c), HALF), :], lp[...]).astype(BF)
    lsend[HALF:, :] = jnp.zeros((HP - HALF, E), BF)
    inputs[4].wait()
    inputs[5].wait()

    pl.semaphore_wait(barrier, len(peers))
    k_core = Send(lambda: ksend, lambda: krecv, partner)
    k_core.start()
    l_core = {}
    for r in (2, 1, 3, 0):
        out = lambda r=r: lsend.at[rows(BLK * mod(h + r, NH), BLK), :]
        come = lambda r=r: lrecv.at[rows(BLK * mod(h + r, NH), BLK), :]
        l_core[r] = Send(out, come, partner)
        l_core[r].start()

    lacc[:HALF, :] = dot(lf[rows(HALF * c, HALF), :], lp[...])
    lacc[HALF:, :] = jnp.zeros((HP - HALF, E), F32)

    f_copy = Send(lambda: kf, lambda: kfo, ypeer[0, 1])
    f_copy.start()
    i_copy = Send(lambda: kid, lambda: kido, ypeer[0, 1])
    i_copy.start()

    k_core.recv()
    kacc[rows(32 * c, 32, 32), :] += krecv[...].astype(F32)
    k_waits = []
    for r in (2, 1, 3, 0):
        kysend[r] = packed(kacc[rows(32 * c + OWN * mod(h + r, NH), OWN, OWN), :])
        for f in (0, 1):
            if (r, f) != (0, 0):
                go = Send(lambda r=r: kysend.at[r], lambda r=r, f=f: kyrecv.at[f, r], ypeer[r, f])
                go.start()
                k_waits.append(go)

    l_sum = h_sum(lacc, lrecv, (lrs, lrr, lls, llr))
    l_core[2].recv()
    l_sum.step(0)
    for r in (1, 3, 0):
        l_core[r].recv()

    i_copy.recv()
    f_copy.recv()

    def by_group(own, other):
        return jnp.concatenate([jnp.where(y == 0, own, other), jnp.where(y == 0, other, own)], axis=0)

    row_ids = lax.broadcasted_iota(jnp.int32, (OWN, GROUP), 0) + (32 * c + OWN * h)
    col_ids = lax.broadcasted_iota(jnp.int32, (OWN, GROUP), 1)

    def id_column(ref):
        return jnp.sum(jnp.where(row_ids == col_ids, ref[...].astype(F32), 0.0), axis=1, keepdims=True)

    k_id = by_group(id_column(kid), id_column(kido))
    one = jnp.ones_like(k_id)
    k_digit = digits(k_id)
    k_ext = on_lanes(list(k_digit) + [g * g for g in k_digit] + [one] * 3, 2 * OWN)

    at = lax.broadcasted_iota(jnp.int32, (2 * HP, LOG), 0)
    upper = at >= HP
    inside = jnp.where(upper, at - HP, at)
    at = jnp.where(inside < HALF, jnp.where(upper, inside + HALF, inside), -1)
    col = lax.broadcasted_iota(jnp.int32, (2 * HP, LOG), 1)
    log_id = jnp.sum(jnp.where(at == col, lid[...].reshape(1, LOG).astype(F32), 0.0), axis=1, keepdims=True)
    one = jnp.ones_like(log_id)
    log_digit = digits(log_id)
    lext[...] = on_lanes([-2.0 * g for g in log_digit] + [one] * 3 + [g * g for g in log_digit], 2 * HP).astype(BF)

    l_sum.step(1)

    for go in k_waits:
        go.recv()
    own, other = unpacked(kysend[0]), unpacked(kyrecv[1, 0])
    for r in range(1, NH):
        own = own + unpacked(kyrecv[0, r])
        other = other + unpacked(kyrecv[1, r])
    unit = by_group(own, other)[:, :E]
    k_inv = lax.rsqrt(jnp.sum(unit * unit, axis=1, keepdims=True) + EPS)
    unit = unit * k_inv
    kunit[...] = unit
    both = jnp.concatenate([unit, k_ext], axis=1).astype(BF)

    def block0(zz, xx):
        return kall.at[rows(64 * zz + 16 * xx, 16), :]

    def block1(zz, xx):
        return kall.at[rows(128 * xx + 16 * zz, 16), :]

    own0 = lambda: block0(z, x)
    own1 = lambda: block1(z, x)
    first = [
        [Send(own0, own0, xpeer[r], lambda r=r: block0(z, xfrom[r]), 0) for r in XS],
        [Send(own1, own1, zpeer[r], lambda r=r: block1(zfrom[r], x), 1) for r in ZS],
    ]

    def k_block(n, size):
        return lambda which, part: lambda: kall.at[rows(size * mod(which + n, n) + part[0], part[1]), :]

    ring = [
        Gather(NZ, z, 64, 32, zpeer[1], zpeer[NZ - 1], k_block(NZ, 64), core=0),
        Gather(NX, x, 128, 64, xpeer[1], xpeer[NX - 1], k_block(NX, 128), core=1),
    ]

    @on_core
    def _(core):
        base = rows(64 * z + 16 * x, 16) if core == 0 else rows(128 * x + 16 * z, 16)
        kall[base, :] = both
        for go in first[core]:
            go.start()

    l_sum.end()
    row = l_sum.result()
    l_inv = lax.rsqrt(jnp.sum(row * row, axis=1, keepdims=True) + EPS)
    row = row * l_inv
    lunit[...] = row
    l_spread = Spread(lall)
    l_spread.start(row.astype(BF))

    @on_core
    def _(core):
        for go in first[core]:
            go.recv()
        ring[core].step(0)
        ring[core].step(1)

    l_spread.step()

    @on_core
    def _(core):
        for s in range(2, ring[core].n // 2):
            ring[core].step(s)

    l_spread.last()

    mine, theirs = kf[...].astype(F32), kfo[...].astype(F32)
    pieces = []
    for i in range(2 * NH):
        pieces.append(by_group(mine[OWN * i : OWN * (i + 1)], theirs[OWN * i : OWN * (i + 1)]))
    kf2[...] = jnp.concatenate(pieces, axis=0).astype(BF)

    @on_core
    def _(core):
        ring[core].end()

    l_spread.end()

    lead = jnp.where(c == 0, lax.div(mod(z + NZ // 2, NZ), jnp.int32(2)), mod(x + NX // 2, NX))

    def kpi_side(i, carry):
        at = rows(mod(lead + i, 4) * 128, 128, 128)
        inner = dot_t(kall[at, :E], lall[...])
        apart = dot_t(kall[at, E:], lext[...])
        kg[at, :] = dot(pair_gradient(inner, apart), lall[...])
        return carry

    def k_part_of(n, size):
        return lambda which, start, count: kg[rows(size * mod(which + n, n) + start, count), :]

    sums = [
        Sum(NZ, z, 64, 32, zpeer[1], zpeer[NZ - 1], k_part_of(NZ, 64), (zrs, zrr, zls, zlr), core=0),
        Sum(NX, x, 128, 64, xpeer[1], xpeer[NX - 1], k_part_of(NX, 128), (xrs, xrr, xls, xlr), core=1),
    ]

    def step(s):
        @on_core
        def _(core):
            if s < sums[core].n // 2:
                sums[core].step(s)

    kpi_side(0, 0)
    step(0)
    lax.fori_loop(1, COUNT // 128, kpi_side, 0)
    step(1)

    def log_pairs(i, carry):
        at = rows(i * 256, 256, 256)
        inner = dot_t(lall[...], kall[at, :E])
        apart = dot_t(lext[...], kall[at, E:])
        pg[:, at] = pair_gradient(inner, apart)
        return carry

    log_pairs(0, 0)
    step(2)
    log_pairs(1, 0)
    step(3)
    middle = [
        [Send(lambda r=r: midsend.at[r - 1], lambda r=r: midrecv.at[r - 1], xpeer[r], core=0) for r in XS],
        [Send(lambda r=r: midsend.at[r - 1], lambda r=r: midrecv.at[r - 1], zpeer[r], core=1) for r in ZS],
    ]

    def middle_begin(core):
        at, order = ((x, XS), (z, ZS))[core]
        n = len(order) + 1
        sums[core].end()
        mid[: 16 * n, :] = sums[core].result()
        for r, go in zip(order, middle[core]):
            midsend[r - 1] = mid[rows(16 * mod(at + r, n), 16), :].astype(BF)
            go.start()

    pl.when(c == 1)(lambda: middle_begin(1))
    gsend[...] = dot(pg[rows(HP * (1 - c), HP), :], kall[:, :E]).astype(BF)
    g_core = Send(lambda: gsend, lambda: grecv, partner)
    g_core.start()

    pl.when(c == 0)(lambda: middle_begin(0))
    lg[...] = dot(pg[rows(HP * c, HP), :], kall[:, :E])
    g_sum = h_sum(lg, grecv, (grs, grr, gls, glr))
    g_core.recv()
    g_sum.step(0)

    @on_core
    def _(core):
        at, order = ((x, XS), (z, ZS))[core]
        n = len(order) + 1
        total = mid[rows(16 * at, 16), :]
        for go in middle[core]:
            go.recv()
        for r in range(n - 1):
            total = total + midrecv[r].astype(F32)
        mid16[...] = total

    total = mid16[...]
    unit = kunit[...]
    inner = jnp.sum(unit * total, axis=1, keepdims=True)

    def kblock(core, hh):
        return lambda: kback.at[rows(16 * (core * NH + hh), 16), :]

    kback[rows(16 * (c * NH + h), 16), :] = (k_inv * (total - unit * inner)).astype(BF)
    kb_waits = {r: Send(kblock(c, h), kblock(c, h), hpeer[r], kblock(c, hfrom[r])) for r in (2, 1, 3)}
    for go in kb_waits.values():
        go.start()
    kb_core = {
        r: Send(kblock(c, hfrom[r]), kblock(c, hfrom[r]), partner, kblock(1 - c, hfrom[r])) for r in range(NH)
    }
    kb_core[0].start()

    g_sum.step(1)
    for r in (1, 3, 2):
        kb_waits[r].recv()
        kb_core[r].start()
    for r in (0, 1, 3, 2):
        kb_core[r].recv()

    part = lax.dot_general(
        kf2[...], kback[...], (((0,), (0,)), ((), ())), preferred_element_type=F32
    ).astype(BF)
    tall = part.shape[0]
    for j in range(E // 128):
        wbuf[tall * j : tall * (j + 1), :] = part[:, 128 * j : 128 * (j + 1)]
    wbuf[tall * (E // 128) :, :] = jnp.zeros((NZ * WZ - tall * (E // 128), 128), BF)

    def cut_of(ref, size, at):
        return lambda: ref.at[rows(size * at, size), :]

    def slot(ref, at):
        return lambda: ref.at[at]

    w_first = [
        [Send(cut_of(wbuf, WZ, mod(z + r, NZ)), slot(wzr, r - 1), zpeer[r], core=0) for r in ZS],
        [Send(cut_of(wbuf, WX, mod(x + r, NX)), slot(wxr, r - 1), xpeer[r], core=1) for r in XS],
    ]
    w_second = [
        [Send(slot(wx, x), slot(wx, x), xpeer[r], slot(wx, xfrom[r]), 0) for r in XS],
        [Send(cut_of(wxs, BLK, mod(z + r, NZ)), slot(wxzr, r - 1), zpeer[r], core=1) for r in ZS],
    ]
    w_pair = [
        [Send(slot(wy, y), slot(wy, y), ypeer[0, 1], slot(wy, 1 - y), 0)],
        [Send(slot(wys, y), slot(wys, y), ypeer[0, 1], slot(wys, 1 - y), 1)],
    ]
    w_third = [
        [],
        [Send(cut_of(wxz, BLK, z), cut_of(wxz, BLK, z), zpeer[r], cut_of(wxz, BLK, zfrom[r]), 1) for r in ZS],
    ]
    w_last = [
        [Send(slot(wlast, pl.ds(0, WZ)), cut_of(out_w, WZ, z), zpeer[r], cut_of(out_w, WZ, zfrom[r]), 0) for r in ZS],
        [Send(slot(wlast, pl.ds(0, WX)), cut_of(out_w, WX, x), xpeer[r], cut_of(out_w, WX, xfrom[r]), 1) for r in XS],
    ]

    def keep(core):
        size, at = ((WZ, z), (WX, x))[core]
        return pltpu.make_async_copy(wlast.at[pl.ds(0, size)], cut_of(out_w, size, at)(), lsem.at[7])

    def begin(copies):
        for go in copies:
            go.start()

    def arrive(copies):
        for go in copies:
            go.recv()

    @on_core
    def _(core):
        begin(w_first[core])

    g_sum.end()
    row = g_sum.result()
    unit = lunit[...]
    inner = jnp.sum(unit * row, axis=1, keepdims=True)
    row = (l_inv * (row - unit * inner)).astype(BF)
    b_spread = Spread(back)
    b_spread.start(row)

    @on_core
    def _(core):
        if core == 0:
            total = wbuf[rows(WZ * z, WZ), :].astype(F32)
            arrive(w_first[0])
            for r in range(NZ - 1):
                total = total + wzr[r].astype(F32)
            wx[x] = total.astype(BF)
        else:
            total = wbuf[rows(WX * x, WX), :].astype(F32)
            arrive(w_first[1])
            for r in range(NX - 1):
                total = total + wxr[r].astype(F32)
            wxs[:WX, :] = total.astype(BF)
            wxs[WX:, :] = jnp.zeros((NZ * BLK - WX, 128), BF)
        begin(w_second[core])

    b_spread.step()

    @on_core
    def _(core):
        arrive(w_second[core])
        if core == 0:
            total = wx[0].astype(F32)
            for i in range(1, NX):
                total = total + wx[i].astype(F32)
            wy[y] = total.astype(BF)
        else:
            total = wxs[rows(BLK * z, BLK), :].astype(F32)
            for r in range(NZ - 1):
                total = total + wxzr[r].astype(F32)
            wys[y] = total.astype(BF)
        begin(w_pair[core])


    @on_core
    def _(core):
        arrive(w_pair[core])
        if core == 0:
            wlast[:WZ, :] = (wy[0].astype(F32) + wy[1].astype(F32)).astype(BF)
        else:
            wxz[rows(BLK * z, BLK), :] = (wys[0].astype(F32) + wys[1].astype(F32)).astype(BF)
            begin(w_third[1])
            arrive(w_third[1])
            wlast[...] = wxz[:WX, :]
        begin(w_last[core])
        keep(core).start()

    b_spread.last()
    b_spread.end()
    for i in range(2):
        og[HALF * i : HALF * (i + 1), :] = dot_t(back[HP * i : HP * i + HALF, :], lp[...]).astype(BF)
    g_out = pltpu.make_async_copy(og, out_g, lsem.at[6])
    g_out.start()

    @on_core
    def _(core):
        arrive(w_last[core])
        keep(core).wait()

    finish()
    g_out.wait()


def deliver(g, w, out_g, out_w, held, wall, ow, sem):
    copies = [
        pltpu.make_async_copy(*pair, sem.at[i])
        for i, pair in enumerate(((w, wall), (g, held), (held, out_g), (ow, out_w)))
    ]
    copies[0].start()
    copies[1].start()
    copies[1].wait()
    copies[2].start()
    copies[0].wait()
    tall = out_w.shape[0]
    for j in range(E // 128):
        ow[:, 128 * j : 128 * (j + 1)] = wall[tall * j : tall * (j + 1), :].astype(F32)
    copies[3].start()
    copies[2].wait()
    copies[3].wait()


def body(log_feats, kpi_feats, log_proj, kpi_proj, log_ids, kpi_ids):
    v = pltpu.VMEM
    inputs = (log_feats, kpi_feats, log_proj, kpi_proj, log_ids, kpi_ids.reshape(1, -1))
    outs = (jax.ShapeDtypeStruct(log_feats.shape, BF), jax.ShapeDtypeStruct((NZ * WZ, 128), BF))
    hbm = pl.BlockSpec(memory_space=pltpu.HBM)
    scratch = [v(a.shape, a.dtype) for a in inputs + outs[:1]] + [
        v((HP, E), BF), v((HP, E), BF), v((HP, E), F32), *[v((2, BLK, E), BF)] * 4,
        v((2 * HP, E), BF), v((BLK, E), F32), v((2 * HP, ID), BF),
        v((GROUP, E), F32), v((32, E), BF), v((32, E), BF), v((NH, 16, PK), BF), v((2, NH, 16, PK), BF),
        v(kpi_feats.shape, BF), v((2 * GROUP, kpi_feats.shape[1]), BF), v((1, GROUP), jnp.int32),
        v((COUNT, EK), BF), v((2 * OWN, E), F32),
        v((2 * HP, COUNT), BF), v((COUNT, E), F32), v((HP, E), F32),
        v((HP, E), BF), v((HP, E), BF), *[v((2, BLK, E), BF)] * 4, v((2 * HP, E), BF),
        *[v((4, 64, E), BF)] * 4, *[v((2, 128, E), BF)] * 4,
        v((128, E), F32), v((7, 16, E), BF), v((7, 16, E), BF), v((16, E), F32),
        v((2 * NH * 16, E), BF), v((NZ * WZ, 128), BF), v((NZ - 1, WZ, 128), BF), v((NX - 1, WX, 128), BF),
        v((NX, WZ, 128), BF), v((NY, WZ, 128), BF), v((NZ * BLK, 128), BF), v((NZ - 1, BLK, 128), BF),
        v((NY, BLK, 128), BF), v((NZ * BLK, 128), BF), v((WX, 128), BF),
        pltpu.SemaphoreType.DMA((NSEM,)), pltpu.SemaphoreType.DMA((NSEM,)),
        pltpu.SemaphoreType.DMA((8,)),
    ]
    grads = pl.pallas_call(
        kernel,
        out_shape=outs,
        in_specs=[hbm] * 6,
        out_specs=(hbm,) * 2,
        scratch_shapes=scratch,
        compiler_params=pltpu.CompilerParams(
            collective_id=0, has_side_effects=True, vmem_limit_bytes=62 * 1024 * 1024
        ),
    )(*inputs)
    return pl.pallas_call(
        deliver,
        out_shape=(outs[0], jax.ShapeDtypeStruct(kpi_proj.shape, F32)),
        in_specs=[hbm] * 2,
        out_specs=(hbm,) * 2,
        scratch_shapes=[v(outs[0].shape, BF), v(outs[1].shape, BF), v(kpi_proj.shape, F32), pltpu.SemaphoreType.DMA((4,))],
        compiler_params=pltpu.CompilerParams(vmem_limit_bytes=62 * 1024 * 1024),
    )(*grads)


def solution(mesh):
    return jax.shard_map(
        body,
        mesh=mesh,
        in_specs=(
            P("dp", "tensor"),
            P("dp", "tensor"),
            P("tensor", None),
            P("tensor", None),
            P("dp"),
            P("dp"),
        ),
        out_specs=(P("dp", "tensor"), P("tensor", None)),
        check_vma=False,
    )
```

```python
import jax
import jax.numpy as jnp
from jax import lax
from jax.experimental import pallas as pl
from jax.experimental.pallas import tpu as pltpu
from jax.sharding import PartitionSpec as P

TEMPER = 32.0
BIAS = -2.0
LOSS = 4096.0
EPS = 1e-06
MESH = pl.DeviceIdType.MESH
BF = jnp.bfloat16
F32 = jnp.float32

NY, NX, NZ, NH = 2, 4, 8, 4
LOG = 352
HALF = LOG // 2
BLK = 48
HP = NH * BLK
E = 1152
ID = 128
EK = E + ID
GROUP = 64
OWN = 8
COUNT = NY * NX * NZ * OWN
SCALE = TEMPER * LOSS / (LOG * NY * NX * NZ)
PK = EK // 2
CUT = 32
WZ, WX = 176, 336
XS, ZS = (2, 1, 3), (4, 3, 5, 2, 6, 1, 7)
NSEM = 160


def dot(a, b):
    return jnp.dot(a, b, preferred_element_type=F32)


def dot_t(a, b):
    return lax.dot_general(a, b, (((1,), (1,)), ((), ())), preferred_element_type=F32)


def mod(a, n):
    return lax.rem(a, jnp.int32(n))


def digits(ids):
    high = jnp.floor(ids * (1.0 / 256.0))
    rest = ids - 256.0 * high
    middle = jnp.floor(rest * (1.0 / 16.0))
    return high, middle, rest - 16.0 * middle


def on_lanes(values, rows):
    lane = lax.broadcasted_iota(jnp.int32, (rows, ID), 1)
    out = jnp.zeros((rows, ID), F32)
    for at, value in enumerate(values):
        out = jnp.where(lane == at, value, out)
    return out


def pair_gradient(inner, apart):
    sign = jnp.where(apart < 0.5, 1.0, -1.0).astype(F32)
    margin = -sign * (TEMPER * inner + BIAS)
    return (-SCALE * sign * jax.nn.sigmoid(margin)).astype(BF)


def kernel(
    lf_h, kf_h, lp_h, kp_h, lid_h, kid_h, out_g, out_w,
    lf, kf, lp, kp, lid, kid, og,
    lsend, lrecv, lacc, lrs, lrr, lls, llr, lall, lunit, lext,
    kacc, ksend, krecv, kysend, kyrecv, kfo, kf2, kido, kall, kunit,
    pg, kg, lg, gsend, grecv, grs, grr, gls, glr, back,
    zrs, zrr, zls, zlr, xrs, xrr, xls, xlr, mid, midsend, midrecv, mid16,
    kback, wbuf, wzr, wxr, wx, wy, wxs, wxzr, wys, wxz, wlast,
    ssem, rsem, lsem,
):
    d = lax.axis_index("dp")
    t = lax.axis_index("tensor")
    y = lax.div(d, jnp.int32(NX * NZ))
    x = mod(lax.div(d, jnp.int32(NZ)), NX)
    z = mod(d, NZ)
    h = lax.div(t, jnp.int32(2))
    c = mod(t, 2)

    def place(y=y, x=x, z=z, h=h, c=c):
        return {"dp": (y * NX + x) * NZ + z, "tensor": h * 2 + c}

    def rows(start, size, unit=16):
        return pl.ds(pl.multiple_of(start, unit), size)

    started = []

    class Send:
        def __init__(self, src, dst, to, land=None, core=None):
            self.src, self.dst, self.to, self.core = src, dst, to, core
            self.land = land or dst
            self.at = len(started)
            self.open, self.begun = True, False
            started.append(self)
            assert self.at < NSEM

        def copy(self, src, dst):
            return pltpu.make_async_remote_copy(
                src_ref=src(), dst_ref=dst(), send_sem=ssem.at[self.at], recv_sem=rsem.at[self.at],
                device_id=self.to, device_id_type=MESH,
            )

        def start(self):
            self.begun = True
            self.copy(self.src, self.dst).start()

        def recv(self):
            self.open = False
            self.copy(self.land, self.land).wait_recv()

        def sent(self):
            self.copy(self.src, self.dst).wait_send()

    def finish():
        for core in (None, 0, 1):

            def ends(core=core):
                for go in started:
                    if go.core == core and go.begun:
                        if go.open:
                            go.recv()
                        go.sent()

            if core is None:
                ends()
            else:
                pl.when(c == core)(ends)

    inputs = [
        pltpu.make_async_copy(a, b, lsem.at[i])
        for i, (a, b) in enumerate(((lf_h, lf), (lp_h, lp), (kf_h, kf), (kp_h, kp), (kid_h, kid), (lid_h, lid)))
    ]
    for go in inputs:
        go.start()

    partner = place(c=1 - c)
    ypeer = {(r, f): place(h=mod(h + r, NH), y=y if f == 0 else 1 - y) for r in range(NH) for f in (0, 1)}
    hpeer = [place(h=mod(h + r, NH)) for r in range(NH)]
    hfrom = [mod(h + NH - r, NH) for r in range(NH)]
    xpeer = [place(x=mod(x + r, NX)) for r in range(NX)]
    xfrom = [mod(x + NX - r, NX) for r in range(NX)]
    zpeer = [place(z=mod(z + r, NZ)) for r in range(NZ)]
    zfrom = [mod(z + NZ - r, NZ) for r in range(NZ)]

    barrier = pltpu.get_barrier_semaphore()
    peers = [partner] + [ypeer[k] for k in ypeer if k != (0, 0)] + xpeer[1:] + zpeer[1:]
    for device in peers:
        pl.semaphore_signal(barrier, inc=1, device_id=device, device_id_type=MESH)

    def on_core(run):
        for core in (0, 1):
            pl.when(c == core)(lambda core=core: run(core))

    def packed(v):
        if v.shape[1] < EK:
            v = jnp.concatenate([v, jnp.zeros((OWN, EK - v.shape[1]), F32)], axis=1)
        return jnp.concatenate([v[:, :PK], v[:, PK:]], axis=0).astype(BF)

    def unpacked(v):
        v = v.astype(F32)
        return jnp.concatenate([v[:OWN], v[OWN:]], axis=1)

    class Gather:
        def __init__(self, n, at, size, split, right, left, block, sign=1, core=None):
            self.n, self.go = n, []
            low, high = (0, split), (split, size - split)
            ways = [(right, -sign, low), (left, sign, high), (right, -sign, high), (left, sign, low)]
            for s in range(n // 2):
                step = []
                for to, way, part in ways if s < n // 2 - 1 else ways[:2]:
                    there, here = block(at + way * s, part), block(at + way * (s + 1), part)
                    step.append(Send(there, there, to, here, core))
                self.go.append(step)

        def step(self, s):
            for i, go in enumerate(self.go[s]):
                if s > 0:
                    self.go[s - 1][i].recv()
                go.start()

        def recv(self, s):
            for go in self.go[s]:
                if go.open:
                    go.recv()

        def end(self):
            for s in range(self.n // 2):
                self.recv(s)

    class Sum:
        def __init__(self, n, at, size, split, right, left, part, bufs, sign=1, core=None):
            self.n, self.at, self.size, self.part = n, at, size, part
            self.rs, self.rr, self.ls, self.lr = bufs
            low, high = (0, split), (split, size - split)
            r, l = (right, sign, self.rs, self.rr), (left, -sign, self.ls, self.lr)
            self.ways = [(*r, low), (*l, high), (*r, high), (*l, low)]
            self.go = []
            for s in range(n // 2):
                step = []
                for to, _, send, come, p in self.ways[:2] if s == 0 else self.ways:
                    src = lambda s=s, p=p, send=send: send.at[s, pl.ds(*p)]
                    dst = lambda s=s, p=p, come=come: come.at[s, pl.ds(*p)]
                    step.append(Send(src, dst, to, core=core))
                self.go.append(step)

        def step(self, s):
            for i in (0, 1) if s == 0 else (2, 3, 0, 1):
                _, way, send, come, p = self.ways[i]
                value = self.part(self.at + way * (self.n // 2 - s), *p)
                if s > 1 or (s == 1 and i < 2):
                    self.go[s - 1][i].recv()
                    value = value + come[s - 1, pl.ds(*p), :].astype(F32)
                send[s, pl.ds(*p), :] = value.astype(BF)
                self.go[s][i].start()

        def end(self):
            for go in self.go[-1]:
                go.recv()

        def result(self):
            last = self.n // 2 - 1
            return self.part(self.at, 0, self.size) + self.rr[last].astype(F32) + self.lr[last].astype(F32)

    turn = 1 - 2 * c
    h_right = place(h=mod(h + turn + NH, NH))
    h_left = place(h=mod(h - turn + NH, NH))

    def h_sum(own, come, bufs):
        def part(which, start, size):
            at = rows(BLK * mod(which + NH, NH) + start, size)
            return own[at, :] + come[at, :].astype(F32)

        return Sum(NH, h, BLK, CUT, h_right, h_left, part, bufs, turn)

    class Spread:
        def __init__(self, buffer):
            self.buffer = buffer

            def at_core(core):
                def block(hh, part=(0, BLK)):
                    return lambda: buffer.at[rows(HP * core + BLK * mod(hh + NH, NH) + part[0], part[1]), :]

                return block

            mine, other = at_core(c), at_core(1 - c)
            self.along = Gather(NH, h, BLK, CUT, h_right, h_left, mine, turn)
            self.across = {r: Send(mine(h - r), mine(h - r), partner, other(h - r)) for r in (0, 1, 3, 2)}

        def start(self, value):
            self.buffer[rows(HP * c + BLK * h, BLK), :] = value
            self.along.step(0)
            self.across[0].start()

        def step(self):
            self.along.step(1)
            self.along.recv(0)
            self.across[1].start()
            self.across[3].start()

        def last(self):
            self.along.recv(1)
            self.across[2].start()

        def end(self):
            for go in self.across.values():
                go.recv()

    inputs[0].wait()
    inputs[1].wait()
    lsend[:HALF, :] = dot(lf[rows(HALF * (1 - c), HALF), :], lp[...]).astype(BF)
    lsend[HALF:, :] = jnp.zeros((HP - HALF, E), BF)
    for go in inputs[2:]:
        go.wait()

    pl.semaphore_wait(barrier, len(peers))
    l_core = {}
    for r in (2, 1, 3, 0):
        out = lambda r=r: lsend.at[rows(BLK * mod(h + r, NH), BLK), :]
        come = lambda r=r: lrecv.at[rows(BLK * mod(h + r, NH), BLK), :]
        l_core[r] = Send(out, come, partner)
        l_core[r].start()
    kacc[...] = dot(kf[...], kp[...])
    ksend[...] = kacc[rows(32 * (1 - c), 32, 32), :].astype(BF)
    k_core = Send(lambda: ksend, lambda: krecv, partner)
    k_core.start()

    lacc[:HALF, :] = dot(lf[rows(HALF * c, HALF), :], lp[...])
    lacc[HALF:, :] = jnp.zeros((HP - HALF, E), F32)

    f_copy = Send(lambda: kf, lambda: kfo, ypeer[0, 1])
    f_copy.start()
    i_copy = Send(lambda: kid, lambda: kido, ypeer[0, 1])
    i_copy.start()

    l_sum = h_sum(lacc, lrecv, (lrs, lrr, lls, llr))
    l_core[2].recv()
    l_sum.step(0)
    for r in (1, 3, 0):
        l_core[r].recv()

    k_core.recv()
    kacc[rows(32 * c, 32, 32), :] += krecv[...].astype(F32)
    k_waits = []
    for r in (2, 1, 3, 0):
        kysend[r] = packed(kacc[rows(32 * c + OWN * mod(h + r, NH), OWN, OWN), :])
        for f in (0, 1):
            if (r, f) != (0, 0):
                go = Send(lambda r=r: kysend.at[r], lambda r=r, f=f: kyrecv.at[f, r], ypeer[r, f])
                go.start()
                k_waits.append(go)

    i_copy.recv()
    f_copy.recv()

    def by_group(own, other):
        return jnp.concatenate([jnp.where(y == 0, own, other), jnp.where(y == 0, other, own)], axis=0)

    row_ids = lax.broadcasted_iota(jnp.int32, (OWN, GROUP), 0) + (32 * c + OWN * h)
    col_ids = lax.broadcasted_iota(jnp.int32, (OWN, GROUP), 1)

    def id_column(ref):
        return jnp.sum(jnp.where(row_ids == col_ids, ref[...].astype(F32), 0.0), axis=1, keepdims=True)

    k_id = by_group(id_column(kid), id_column(kido))
    one = jnp.ones_like(k_id)
    k_digit = digits(k_id)
    k_ext = on_lanes(list(k_digit) + [g * g for g in k_digit] + [one] * 3, 2 * OWN)

    at = lax.broadcasted_iota(jnp.int32, (2 * HP, LOG), 0)
    upper = at >= HP
    inside = jnp.where(upper, at - HP, at)
    at = jnp.where(inside < HALF, jnp.where(upper, inside + HALF, inside), -1)
    col = lax.broadcasted_iota(jnp.int32, (2 * HP, LOG), 1)
    log_id = jnp.sum(jnp.where(at == col, lid[...].reshape(1, LOG).astype(F32), 0.0), axis=1, keepdims=True)
    one = jnp.ones_like(log_id)
    log_digit = digits(log_id)
    lext[...] = on_lanes([-2.0 * g for g in log_digit] + [one] * 3 + [g * g for g in log_digit], 2 * HP).astype(BF)

    l_sum.step(1)

    for go in k_waits:
        go.recv()
    own, other = unpacked(kysend[0]), unpacked(kyrecv[1, 0])
    for r in range(1, NH):
        own = own + unpacked(kyrecv[0, r])
        other = other + unpacked(kyrecv[1, r])
    unit = by_group(own, other)[:, :E]
    k_inv = lax.rsqrt(jnp.sum(unit * unit, axis=1, keepdims=True) + EPS)
    unit = unit * k_inv
    kunit[...] = unit
    both = jnp.concatenate([unit, k_ext], axis=1).astype(BF)

    def block0(zz, xx):
        return kall.at[rows(64 * zz + 16 * xx, 16), :]

    def block1(zz, xx):
        return kall.at[rows(128 * xx + 16 * zz, 16), :]

    own0 = lambda: block0(z, x)
    own1 = lambda: block1(z, x)
    first = [
        [Send(own0, own0, xpeer[r], lambda r=r: block0(z, xfrom[r]), 0) for r in XS],
        [Send(own1, own1, zpeer[r], lambda r=r: block1(zfrom[r], x), 1) for r in ZS],
    ]

    def k_block(n, size):
        return lambda which, part: lambda: kall.at[rows(size * mod(which + n, n) + part[0], part[1]), :]

    ring = [
        Gather(NZ, z, 64, 32, zpeer[1], zpeer[NZ - 1], k_block(NZ, 64), core=0),
        Gather(NX, x, 128, 64, xpeer[1], xpeer[NX - 1], k_block(NX, 128), core=1),
    ]

    @on_core
    def _(core):
        base = rows(64 * z + 16 * x, 16) if core == 0 else rows(128 * x + 16 * z, 16)
        kall[base, :] = both
        for go in first[core]:
            go.start()

    l_sum.end()
    row = l_sum.result()
    l_inv = lax.rsqrt(jnp.sum(row * row, axis=1, keepdims=True) + EPS)
    row = row * l_inv
    lunit[...] = row
    l_spread = Spread(lall)
    l_spread.start(row.astype(BF))

    @on_core
    def _(core):
        for go in first[core]:
            go.recv()
        ring[core].step(0)
        ring[core].step(1)

    l_spread.step()

    @on_core
    def _(core):
        for s in range(2, ring[core].n // 2):
            ring[core].step(s)

    l_spread.last()

    mine, theirs = kf[...].astype(F32), kfo[...].astype(F32)
    pieces = []
    for i in range(2 * NH):
        pieces.append(by_group(mine[OWN * i : OWN * (i + 1)], theirs[OWN * i : OWN * (i + 1)]))
    kf2[...] = jnp.concatenate(pieces, axis=0).astype(BF)

    @on_core
    def _(core):
        ring[core].end()

    l_spread.end()

    lead = jnp.where(c == 0, lax.div(mod(z + NZ // 2, NZ), jnp.int32(2)), mod(x + NX // 2, NX))

    def kpi_side(i, carry):
        at = rows(mod(lead + i, 4) * 128, 128, 128)
        inner = dot_t(kall[at, :E], lall[...])
        apart = dot_t(kall[at, E:], lext[...])
        kg[at, :] = dot(pair_gradient(inner, apart), lall[...])
        return carry

    def k_part_of(n, size):
        return lambda which, start, count: kg[rows(size * mod(which + n, n) + start, count), :]

    sums = [
        Sum(NZ, z, 64, 32, zpeer[1], zpeer[NZ - 1], k_part_of(NZ, 64), (zrs, zrr, zls, zlr), core=0),
        Sum(NX, x, 128, 64, xpeer[1], xpeer[NX - 1], k_part_of(NX, 128), (xrs, xrr, xls, xlr), core=1),
    ]

    def step(s):
        @on_core
        def _(core):
            if s < sums[core].n // 2:
                sums[core].step(s)

    kpi_side(0, 0)
    step(0)
    lax.fori_loop(1, COUNT // 128, kpi_side, 0)
    step(1)

    def log_pairs(i, carry):
        at = rows(i * 256, 256, 256)
        inner = dot_t(lall[...], kall[at, :E])
        apart = dot_t(lext[...], kall[at, E:])
        pg[:, at] = pair_gradient(inner, apart)
        return carry

    lax.fori_loop(0, COUNT // 256, log_pairs, 0)
    step(2)
    gsend[...] = dot(pg[rows(HP * (1 - c), HP), :], kall[:, :E]).astype(BF)
    g_core = Send(lambda: gsend, lambda: grecv, partner)
    g_core.start()
    lg[...] = dot(pg[rows(HP * c, HP), :], kall[:, :E])

    g_sum = h_sum(lg, grecv, (grs, grr, gls, glr))
    step(3)
    g_core.recv()
    g_sum.step(0)

    middle = [
        [Send(lambda r=r: midsend.at[r - 1], lambda r=r: midrecv.at[r - 1], xpeer[r], core=0) for r in XS],
        [Send(lambda r=r: midsend.at[r - 1], lambda r=r: midrecv.at[r - 1], zpeer[r], core=1) for r in ZS],
    ]

    @on_core
    def _(core):
        at, order = ((x, XS), (z, ZS))[core]
        n = len(order) + 1
        sums[core].end()
        mid[: 16 * n, :] = sums[core].result()
        for r, go in zip(order, middle[core]):
            midsend[r - 1] = mid[rows(16 * mod(at + r, n), 16), :].astype(BF)
            go.start()

    g_sum.step(1)

    @on_core
    def _(core):
        at, order = ((x, XS), (z, ZS))[core]
        n = len(order) + 1
        total = mid[rows(16 * at, 16), :]
        for go in middle[core]:
            go.recv()
        for r in range(n - 1):
            total = total + midrecv[r].astype(F32)
        mid16[...] = total

    total = mid16[...]
    unit = kunit[...]
    inner = jnp.sum(unit * total, axis=1, keepdims=True)

    def kblock(core, hh):
        return lambda: kback.at[rows(16 * (core * NH + hh), 16), :]

    kback[rows(16 * (c * NH + h), 16), :] = (k_inv * (total - unit * inner)).astype(BF)
    kb_waits = {r: Send(kblock(c, h), kblock(c, h), hpeer[r], kblock(c, hfrom[r])) for r in (2, 1, 3)}
    for go in kb_waits.values():
        go.start()
    kb_core = {
        r: Send(kblock(c, hfrom[r]), kblock(c, hfrom[r]), partner, kblock(1 - c, hfrom[r])) for r in range(NH)
    }
    kb_core[0].start()

    g_sum.end()
    row = g_sum.result()
    unit = lunit[...]
    inner = jnp.sum(unit * row, axis=1, keepdims=True)
    row = (l_inv * (row - unit * inner)).astype(BF)

    for r in (1, 3, 2):
        kb_waits[r].recv()
        kb_core[r].start()
    b_spread = Spread(back)
    b_spread.start(row)
    for r in (0, 1, 3, 2):
        kb_core[r].recv()

    part = lax.dot_general(
        kf2[...], kback[...], (((0,), (0,)), ((), ())), preferred_element_type=F32
    ).astype(BF)
    tall = part.shape[0]
    for j in range(E // 128):
        wbuf[tall * j : tall * (j + 1), :] = part[:, 128 * j : 128 * (j + 1)]
    wbuf[tall * (E // 128) :, :] = jnp.zeros((NZ * WZ - tall * (E // 128), 128), BF)

    def cut_of(ref, size, at):
        return lambda: ref.at[rows(size * at, size), :]

    def slot(ref, at):
        return lambda: ref.at[at]

    w_first = [
        [Send(cut_of(wbuf, WZ, mod(z + r, NZ)), slot(wzr, r - 1), zpeer[r], core=0) for r in ZS],
        [Send(cut_of(wbuf, WX, mod(x + r, NX)), slot(wxr, r - 1), xpeer[r], core=1) for r in XS],
    ]
    w_second = [
        [Send(slot(wx, x), slot(wx, x), xpeer[r], slot(wx, xfrom[r]), 0) for r in XS],
        [Send(cut_of(wxs, BLK, mod(z + r, NZ)), slot(wxzr, r - 1), zpeer[r], core=1) for r in ZS],
    ]
    w_pair = [
        [Send(slot(wy, y), slot(wy, y), ypeer[0, 1], slot(wy, 1 - y), 0)],
        [Send(slot(wys, y), slot(wys, y), ypeer[0, 1], slot(wys, 1 - y), 1)],
    ]
    w_third = [
        [],
        [Send(cut_of(wxz, BLK, z), cut_of(wxz, BLK, z), zpeer[r], cut_of(wxz, BLK, zfrom[r]), 1) for r in ZS],
    ]
    w_last = [
        [Send(slot(wlast, pl.ds(0, WZ)), cut_of(out_w, WZ, z), zpeer[r], cut_of(out_w, WZ, zfrom[r]), 0) for r in ZS],
        [Send(slot(wlast, pl.ds(0, WX)), cut_of(out_w, WX, x), xpeer[r], cut_of(out_w, WX, xfrom[r]), 1) for r in XS],
    ]

    def keep(core):
        size, at = ((WZ, z), (WX, x))[core]
        return pltpu.make_async_copy(wlast.at[pl.ds(0, size)], cut_of(out_w, size, at)(), lsem.at[7])

    def begin(copies):
        for go in copies:
            go.start()

    def arrive(copies):
        for go in copies:
            go.recv()

    @on_core
    def _(core):
        begin(w_first[core])

    b_spread.step()

    @on_core
    def _(core):
        if core == 0:
            total = wbuf[rows(WZ * z, WZ), :].astype(F32)
            arrive(w_first[0])
            for r in range(NZ - 1):
                total = total + wzr[r].astype(F32)
            wx[x] = total.astype(BF)
        else:
            total = wbuf[rows(WX * x, WX), :].astype(F32)
            arrive(w_first[1])
            for r in range(NX - 1):
                total = total + wxr[r].astype(F32)
            wxs[:WX, :] = total.astype(BF)
            wxs[WX:, :] = jnp.zeros((NZ * BLK - WX, 128), BF)
        begin(w_second[core])

    b_spread.last()

    @on_core
    def _(core):
        arrive(w_second[core])
        if core == 0:
            total = wx[0].astype(F32)
            for i in range(1, NX):
                total = total + wx[i].astype(F32)
            wy[y] = total.astype(BF)
        else:
            total = wxs[rows(BLK * z, BLK), :].astype(F32)
            for r in range(NZ - 1):
                total = total + wxzr[r].astype(F32)
            wys[y] = total.astype(BF)
        begin(w_pair[core])


    @on_core
    def _(core):
        arrive(w_pair[core])
        if core == 0:
            wlast[:WZ, :] = (wy[0].astype(F32) + wy[1].astype(F32)).astype(BF)
        else:
            wxz[rows(BLK * z, BLK), :] = (wys[0].astype(F32) + wys[1].astype(F32)).astype(BF)
            begin(w_third[1])
            arrive(w_third[1])
            wlast[...] = wxz[:WX, :]
        begin(w_last[core])
        keep(core).start()

    b_spread.end()
    for i in range(2):
        og[HALF * i : HALF * (i + 1), :] = dot_t(back[HP * i : HP * i + HALF, :], lp[...]).astype(BF)
    g_out = pltpu.make_async_copy(og, out_g, lsem.at[6])
    g_out.start()

    @on_core
    def _(core):
        arrive(w_last[core])
        keep(core).wait()

    finish()
    g_out.wait()


def deliver(g, w, out_g, out_w, held, wall, ow, sem):
    copies = [
        pltpu.make_async_copy(*pair, sem.at[i])
        for i, pair in enumerate(((w, wall), (g, held), (held, out_g), (ow, out_w)))
    ]
    copies[0].start()
    copies[1].start()
    copies[1].wait()
    copies[2].start()
    copies[0].wait()
    tall = out_w.shape[0]
    for j in range(E // 128):
        ow[:, 128 * j : 128 * (j + 1)] = wall[tall * j : tall * (j + 1), :].astype(F32)
    copies[3].start()
    copies[2].wait()
    copies[3].wait()


def body(log_feats, kpi_feats, log_proj, kpi_proj, log_ids, kpi_ids):
    v = pltpu.VMEM
    inputs = (log_feats, kpi_feats, log_proj, kpi_proj, log_ids, kpi_ids.reshape(1, -1))
    outs = (jax.ShapeDtypeStruct(log_feats.shape, BF), jax.ShapeDtypeStruct((NZ * WZ, 128), BF))
    hbm = pl.BlockSpec(memory_space=pltpu.HBM)
    scratch = [v(a.shape, a.dtype) for a in inputs + outs[:1]] + [
        v((HP, E), BF), v((HP, E), BF), v((HP, E), F32), *[v((2, BLK, E), BF)] * 4,
        v((2 * HP, E), BF), v((BLK, E), F32), v((2 * HP, ID), BF),
        v((GROUP, E), F32), v((32, E), BF), v((32, E), BF), v((NH, 16, PK), BF), v((2, NH, 16, PK), BF),
        v(kpi_feats.shape, BF), v((2 * GROUP, kpi_feats.shape[1]), BF), v((1, GROUP), jnp.int32),
        v((COUNT, EK), BF), v((2 * OWN, E), F32),
        v((2 * HP, COUNT), BF), v((COUNT, E), F32), v((HP, E), F32),
        v((HP, E), BF), v((HP, E), BF), *[v((2, BLK, E), BF)] * 4, v((2 * HP, E), BF),
        *[v((4, 64, E), BF)] * 4, *[v((2, 128, E), BF)] * 4,
        v((128, E), F32), v((7, 16, E), BF), v((7, 16, E), BF), v((16, E), F32),
        v((2 * NH * 16, E), BF), v((NZ * WZ, 128), BF), v((NZ - 1, WZ, 128), BF), v((NX - 1, WX, 128), BF),
        v((NX, WZ, 128), BF), v((NY, WZ, 128), BF), v((NZ * BLK, 128), BF), v((NZ - 1, BLK, 128), BF),
        v((NY, BLK, 128), BF), v((NZ * BLK, 128), BF), v((WX, 128), BF),
        pltpu.SemaphoreType.DMA((NSEM,)), pltpu.SemaphoreType.DMA((NSEM,)),
        pltpu.SemaphoreType.DMA((8,)),
    ]
    grads = pl.pallas_call(
        kernel,
        out_shape=outs,
        in_specs=[hbm] * 6,
        out_specs=(hbm,) * 2,
        scratch_shapes=scratch,
        compiler_params=pltpu.CompilerParams(
            collective_id=0, has_side_effects=True, vmem_limit_bytes=62 * 1024 * 1024
        ),
    )(*inputs)
    return pl.pallas_call(
        deliver,
        out_shape=(outs[0], jax.ShapeDtypeStruct(kpi_proj.shape, F32)),
        in_specs=[hbm] * 2,
        out_specs=(hbm,) * 2,
        scratch_shapes=[v(outs[0].shape, BF), v(outs[1].shape, BF), v(kpi_proj.shape, F32), pltpu.SemaphoreType.DMA((4,))],
        compiler_params=pltpu.CompilerParams(vmem_limit_bytes=62 * 1024 * 1024),
    )(*grads)


def solution(mesh):
    return jax.shard_map(
        body,
        mesh=mesh,
        in_specs=(
            P("dp", "tensor"),
            P("dp", "tensor"),
            P("tensor", None),
            P("tensor", None),
            P("dp"),
            P("dp"),
        ),
        out_specs=(P("dp", "tensor"), P("tensor", None)),
        check_vma=False,
    )
```

```python
import jax
import jax.numpy as jnp
from jax import lax
from jax.experimental import pallas as pl
from jax.experimental.pallas import tpu as pltpu
from jax.sharding import PartitionSpec as P

TEMPER = 32.0
BIAS = -2.0
LOSS = 4096.0
EPS = 1e-06
MESH = pl.DeviceIdType.MESH
BF = jnp.bfloat16
F32 = jnp.float32

NY, NX, NZ, NH = 2, 4, 8, 4
LOG = 352
HALF = LOG // 2
BLK = 48
HP = NH * BLK
E = 1152
ID = 128
EK = E + ID
GROUP = 64
OWN = 8
COUNT = NY * NX * NZ * OWN
SCALE = TEMPER * LOSS / (LOG * NY * NX * NZ)
PK = EK // 2
CUT = 32
WZ, WX = 176, 336
XS, ZS = (2, 1, 3), (4, 3, 5, 2, 6, 1, 7)
NSEM = 160


def dot(a, b):
    return jnp.dot(a, b, preferred_element_type=F32)


def dot_t(a, b):
    return lax.dot_general(a, b, (((1,), (1,)), ((), ())), preferred_element_type=F32)


def mod(a, n):
    return lax.rem(a, jnp.int32(n))


def digits(ids):
    high = jnp.floor(ids * (1.0 / 256.0))
    rest = ids - 256.0 * high
    middle = jnp.floor(rest * (1.0 / 16.0))
    return high, middle, rest - 16.0 * middle


def on_lanes(values, rows):
    lane = lax.broadcasted_iota(jnp.int32, (rows, ID), 1)
    out = jnp.zeros((rows, ID), F32)
    for at, value in enumerate(values):
        out = jnp.where(lane == at, value, out)
    return out


def pair_gradient(inner, apart):
    sign = jnp.where(apart < 0.5, 1.0, -1.0).astype(F32)
    margin = -sign * (TEMPER * inner + BIAS)
    return (-SCALE * sign * jax.nn.sigmoid(margin)).astype(BF)


def kernel(
    lf_h, kf_h, lp_h, kp_h, lid_h, kid_h, out_g, out_w,
    lf, kf, lp, kp, lid, kid, og,
    lsend, lrecv, lacc, lrs, lrr, lls, llr, lall, lunit, lext,
    kacc, ksend, krecv, kysend, kyrecv, kfo, kf2, kido, kall, kunit,
    pg, kg, lg, gsend, grecv, grs, grr, gls, glr, back,
    zrs, zrr, zls, zlr, xrs, xrr, xls, xlr, mid, midsend, midrecv, mid16,
    kback, wbuf, wzr, wxr, wx, wy, wxs, wxzr, wys, wxz, wlast,
    ssem, rsem, lsem,
):
    d = lax.axis_index("dp")
    t = lax.axis_index("tensor")
    y = lax.div(d, jnp.int32(NX * NZ))
    x = mod(lax.div(d, jnp.int32(NZ)), NX)
    z = mod(d, NZ)
    h = lax.div(t, jnp.int32(2))
    c = mod(t, 2)

    def place(y=y, x=x, z=z, h=h, c=c):
        return {"dp": (y * NX + x) * NZ + z, "tensor": h * 2 + c}

    def rows(start, size, unit=16):
        return pl.ds(pl.multiple_of(start, unit), size)

    started = []

    class Send:
        def __init__(self, src, dst, to, land=None, core=None):
            self.src, self.dst, self.to, self.core = src, dst, to, core
            self.land = land or dst
            self.at = len(started)
            self.open, self.begun = True, False
            started.append(self)
            assert self.at < NSEM

        def copy(self, src, dst):
            return pltpu.make_async_remote_copy(
                src_ref=src(), dst_ref=dst(), send_sem=ssem.at[self.at], recv_sem=rsem.at[self.at],
                device_id=self.to, device_id_type=MESH,
            )

        def start(self):
            self.begun = True
            self.copy(self.src, self.dst).start()

        def recv(self):
            self.open = False
            self.copy(self.land, self.land).wait_recv()

        def sent(self):
            self.copy(self.src, self.dst).wait_send()

    def finish():
        for core in (None, 0, 1):

            def ends(core=core):
                for go in started:
                    if go.core == core and go.begun:
                        if go.open:
                            go.recv()
                        go.sent()

            if core is None:
                ends()
            else:
                pl.when(c == core)(ends)

    inputs = [
        pltpu.make_async_copy(a, b, lsem.at[i])
        for i, (a, b) in enumerate(((lf_h, lf), (lp_h, lp), (kf_h, kf), (kp_h, kp), (kid_h, kid), (lid_h, lid)))
    ]
    for go in inputs:
        go.start()

    partner = place(c=1 - c)
    ypeer = {(r, f): place(h=mod(h + r, NH), y=y if f == 0 else 1 - y) for r in range(NH) for f in (0, 1)}
    hpeer = [place(h=mod(h + r, NH)) for r in range(NH)]
    hfrom = [mod(h + NH - r, NH) for r in range(NH)]
    xpeer = [place(x=mod(x + r, NX)) for r in range(NX)]
    xfrom = [mod(x + NX - r, NX) for r in range(NX)]
    zpeer = [place(z=mod(z + r, NZ)) for r in range(NZ)]
    zfrom = [mod(z + NZ - r, NZ) for r in range(NZ)]

    barrier = pltpu.get_barrier_semaphore()
    peers = [partner] + [ypeer[k] for k in ypeer if k != (0, 0)] + xpeer[1:] + zpeer[1:]
    for device in peers:
        pl.semaphore_signal(barrier, inc=1, device_id=device, device_id_type=MESH)

    def on_core(run):
        for core in (0, 1):
            pl.when(c == core)(lambda core=core: run(core))

    def packed(v):
        if v.shape[1] < EK:
            v = jnp.concatenate([v, jnp.zeros((OWN, EK - v.shape[1]), F32)], axis=1)
        return jnp.concatenate([v[:, :PK], v[:, PK:]], axis=0).astype(BF)

    def unpacked(v):
        v = v.astype(F32)
        return jnp.concatenate([v[:OWN], v[OWN:]], axis=1)

    class Gather:
        def __init__(self, n, at, size, split, right, left, block, sign=1, core=None):
            self.n, self.go = n, []
            low, high = (0, split), (split, size - split)
            ways = [(right, -sign, low), (left, sign, high), (right, -sign, high), (left, sign, low)]
            for s in range(n // 2):
                step = []
                for to, way, part in ways if s < n // 2 - 1 else ways[:2]:
                    there, here = block(at + way * s, part), block(at + way * (s + 1), part)
                    step.append(Send(there, there, to, here, core))
                self.go.append(step)

        def step(self, s):
            for i, go in enumerate(self.go[s]):
                if s > 0:
                    self.go[s - 1][i].recv()
                go.start()

        def recv(self, s):
            for go in self.go[s]:
                if go.open:
                    go.recv()

        def end(self):
            for s in range(self.n // 2):
                self.recv(s)

    class Sum:
        def __init__(self, n, at, size, split, right, left, part, bufs, sign=1, core=None):
            self.n, self.at, self.size, self.part = n, at, size, part
            self.rs, self.rr, self.ls, self.lr = bufs
            low, high = (0, split), (split, size - split)
            r, l = (right, sign, self.rs, self.rr), (left, -sign, self.ls, self.lr)
            self.ways = [(*r, low), (*l, high), (*r, high), (*l, low)]
            self.go = []
            for s in range(n // 2):
                step = []
                for to, _, send, come, p in self.ways[:2] if s == 0 else self.ways:
                    src = lambda s=s, p=p, send=send: send.at[s, pl.ds(*p)]
                    dst = lambda s=s, p=p, come=come: come.at[s, pl.ds(*p)]
                    step.append(Send(src, dst, to, core=core))
                self.go.append(step)

        def step(self, s):
            for i in (0, 1) if s == 0 else (2, 3, 0, 1):
                _, way, send, come, p = self.ways[i]
                value = self.part(self.at + way * (self.n // 2 - s), *p)
                if s > 1 or (s == 1 and i < 2):
                    self.go[s - 1][i].recv()
                    value = value + come[s - 1, pl.ds(*p), :].astype(F32)
                send[s, pl.ds(*p), :] = value.astype(BF)
                self.go[s][i].start()

        def end(self):
            for go in self.go[-1]:
                go.recv()

        def result(self):
            last = self.n // 2 - 1
            return self.part(self.at, 0, self.size) + self.rr[last].astype(F32) + self.lr[last].astype(F32)

    turn = 1 - 2 * c
    h_right = place(h=mod(h + turn + NH, NH))
    h_left = place(h=mod(h - turn + NH, NH))

    def h_sum(own, come, bufs):
        def part(which, start, size):
            at = rows(BLK * mod(which + NH, NH) + start, size)
            return own[at, :] + come[at, :].astype(F32)

        return Sum(NH, h, BLK, CUT, h_right, h_left, part, bufs, turn)

    class Spread:
        def __init__(self, buffer):
            self.buffer = buffer

            def at_core(core):
                def block(hh, part=(0, BLK)):
                    return lambda: buffer.at[rows(HP * core + BLK * mod(hh + NH, NH) + part[0], part[1]), :]

                return block

            mine, other = at_core(c), at_core(1 - c)
            self.along = Gather(NH, h, BLK, CUT, h_right, h_left, mine, turn)
            self.across = {r: Send(mine(h - r), mine(h - r), partner, other(h - r)) for r in (0, 1, 3, 2)}

        def start(self, value):
            self.buffer[rows(HP * c + BLK * h, BLK), :] = value
            self.along.step(0)
            self.across[0].start()

        def step(self):
            self.along.step(1)
            self.along.recv(0)
            self.across[1].start()
            self.across[3].start()

        def last(self):
            self.along.recv(1)
            self.across[2].start()

        def end(self):
            for go in self.across.values():
                go.recv()

    inputs[0].wait()
    inputs[1].wait()
    lsend[:HALF, :] = dot(lf[rows(HALF * (1 - c), HALF), :], lp[...]).astype(BF)
    lsend[HALF:, :] = jnp.zeros((HP - HALF, E), BF)
    for go in inputs[2:]:
        go.wait()

    pl.semaphore_wait(barrier, len(peers))
    l_core = {}
    for r in (2, 1, 3, 0):
        out = lambda r=r: lsend.at[rows(BLK * mod(h + r, NH), BLK), :]
        come = lambda r=r: lrecv.at[rows(BLK * mod(h + r, NH), BLK), :]
        l_core[r] = Send(out, come, partner)
        l_core[r].start()
    kacc[...] = dot(kf[...], kp[...])
    ksend[...] = kacc[rows(32 * (1 - c), 32, 32), :].astype(BF)
    k_core = Send(lambda: ksend, lambda: krecv, partner)
    k_core.start()

    lacc[:HALF, :] = dot(lf[rows(HALF * c, HALF), :], lp[...])
    lacc[HALF:, :] = jnp.zeros((HP - HALF, E), F32)

    f_copy = Send(lambda: kf, lambda: kfo, ypeer[0, 1])
    f_copy.start()
    i_copy = Send(lambda: kid, lambda: kido, ypeer[0, 1])
    i_copy.start()

    l_sum = h_sum(lacc, lrecv, (lrs, lrr, lls, llr))
    l_core[2].recv()
    l_sum.step(0)
    for r in (1, 3, 0):
        l_core[r].recv()

    k_core.recv()
    kacc[rows(32 * c, 32, 32), :] += krecv[...].astype(F32)
    k_waits = []
    for r in (2, 1, 3, 0):
        kysend[r] = packed(kacc[rows(32 * c + OWN * mod(h + r, NH), OWN, OWN), :])
        for f in (0, 1):
            if (r, f) != (0, 0):
                go = Send(lambda r=r: kysend.at[r], lambda r=r, f=f: kyrecv.at[f, r], ypeer[r, f])
                go.start()
                k_waits.append(go)

    i_copy.recv()
    f_copy.recv()

    def by_group(own, other):
        return jnp.concatenate([jnp.where(y == 0, own, other), jnp.where(y == 0, other, own)], axis=0)

    row_ids = lax.broadcasted_iota(jnp.int32, (OWN, GROUP), 0) + (32 * c + OWN * h)
    col_ids = lax.broadcasted_iota(jnp.int32, (OWN, GROUP), 1)

    def id_column(ref):
        return jnp.sum(jnp.where(row_ids == col_ids, ref[...].astype(F32), 0.0), axis=1, keepdims=True)

    k_id = by_group(id_column(kid), id_column(kido))
    one = jnp.ones_like(k_id)
    k_digit = digits(k_id)
    k_ext = on_lanes(list(k_digit) + [g * g for g in k_digit] + [one] * 3, 2 * OWN)

    at = lax.broadcasted_iota(jnp.int32, (2 * HP, LOG), 0)
    upper = at >= HP
    inside = jnp.where(upper, at - HP, at)
    at = jnp.where(inside < HALF, jnp.where(upper, inside + HALF, inside), -1)
    col = lax.broadcasted_iota(jnp.int32, (2 * HP, LOG), 1)
    log_id = jnp.sum(jnp.where(at == col, lid[...].reshape(1, LOG).astype(F32), 0.0), axis=1, keepdims=True)
    one = jnp.ones_like(log_id)
    log_digit = digits(log_id)
    lext[...] = on_lanes([-2.0 * g for g in log_digit] + [one] * 3 + [g * g for g in log_digit], 2 * HP).astype(BF)

    l_sum.step(1)

    for go in k_waits:
        go.recv()
    own, other = unpacked(kysend[0]), unpacked(kyrecv[1, 0])
    for r in range(1, NH):
        own = own + unpacked(kyrecv[0, r])
        other = other + unpacked(kyrecv[1, r])
    unit = by_group(own, other)[:, :E]
    k_inv = lax.rsqrt(jnp.sum(unit * unit, axis=1, keepdims=True) + EPS)
    unit = unit * k_inv
    kunit[...] = unit
    both = jnp.concatenate([unit, k_ext], axis=1).astype(BF)

    def block0(zz, xx):
        return kall.at[rows(64 * zz + 16 * xx, 16), :]

    def block1(zz, xx):
        return kall.at[rows(128 * xx + 16 * zz, 16), :]

    own0 = lambda: block0(z, x)
    own1 = lambda: block1(z, x)
    first = [
        [Send(own0, own0, xpeer[r], lambda r=r: block0(z, xfrom[r]), 0) for r in XS],
        [Send(own1, own1, zpeer[r], lambda r=r: block1(zfrom[r], x), 1) for r in ZS],
    ]

    def k_block(n, size):
        return lambda which, part: lambda: kall.at[rows(size * mod(which + n, n) + part[0], part[1]), :]

    ring = [
        Gather(NZ, z, 64, 32, zpeer[1], zpeer[NZ - 1], k_block(NZ, 64), core=0),
        Gather(NX, x, 128, 64, xpeer[1], xpeer[NX - 1], k_block(NX, 128), core=1),
    ]

    @on_core
    def _(core):
        base = rows(64 * z + 16 * x, 16) if core == 0 else rows(128 * x + 16 * z, 16)
        kall[base, :] = both
        for go in first[core]:
            go.start()

    l_sum.end()
    row = l_sum.result()
    l_inv = lax.rsqrt(jnp.sum(row * row, axis=1, keepdims=True) + EPS)
    row = row * l_inv
    lunit[...] = row
    l_spread = Spread(lall)
    l_spread.start(row.astype(BF))

    @on_core
    def _(core):
        for go in first[core]:
            go.recv()
        ring[core].step(0)
        ring[core].step(1)

    l_spread.step()

    @on_core
    def _(core):
        for s in range(2, ring[core].n // 2):
            ring[core].step(s)

    l_spread.last()

    mine, theirs = kf[...].astype(F32), kfo[...].astype(F32)
    pieces = []
    for i in range(2 * NH):
        pieces.append(by_group(mine[OWN * i : OWN * (i + 1)], theirs[OWN * i : OWN * (i + 1)]))
    kf2[...] = jnp.concatenate(pieces, axis=0).astype(BF)

    @on_core
    def _(core):
        ring[core].end()

    l_spread.end()

    lead = jnp.where(c == 0, lax.div(mod(z + NZ // 2, NZ), jnp.int32(2)), mod(x + NX // 2, NX))

    def kpi_side(i, carry):
        at = rows(mod(lead + i, 4) * 128, 128, 128)
        inner = dot_t(kall[at, :E], lall[...])
        apart = dot_t(kall[at, E:], lext[...])
        kg[at, :] = dot(pair_gradient(inner, apart), lall[...])
        return carry

    def k_part_of(n, size):
        return lambda which, start, count: kg[rows(size * mod(which + n, n) + start, count), :]

    sums = [
        Sum(NZ, z, 64, 32, zpeer[1], zpeer[NZ - 1], k_part_of(NZ, 64), (zrs, zrr, zls, zlr), core=0),
        Sum(NX, x, 128, 64, xpeer[1], xpeer[NX - 1], k_part_of(NX, 128), (xrs, xrr, xls, xlr), core=1),
    ]

    def step(s):
        @on_core
        def _(core):
            if s < sums[core].n // 2:
                sums[core].step(s)

    kpi_side(0, 0)
    step(0)
    lax.fori_loop(1, COUNT // 128, kpi_side, 0)
    step(1)

    def log_pairs(i, carry):
        at = rows(i * 256, 256, 256)
        inner = dot_t(lall[...], kall[at, :E])
        apart = dot_t(lext[...], kall[at, E:])
        pg[:, at] = pair_gradient(inner, apart)
        return carry

    lax.fori_loop(0, COUNT // 256, log_pairs, 0)
    step(2)
    gsend[...] = dot(pg[rows(HP * (1 - c), HP), :], kall[:, :E]).astype(BF)
    g_core = Send(lambda: gsend, lambda: grecv, partner)
    g_core.start()
    lg[...] = dot(pg[rows(HP * c, HP), :], kall[:, :E])

    g_sum = h_sum(lg, grecv, (grs, grr, gls, glr))
    step(3)
    g_core.recv()
    g_sum.step(0)

    middle = [
        [Send(lambda r=r: midsend.at[r - 1], lambda r=r: midrecv.at[r - 1], xpeer[r], core=0) for r in XS],
        [Send(lambda r=r: midsend.at[r - 1], lambda r=r: midrecv.at[r - 1], zpeer[r], core=1) for r in ZS],
    ]

    @on_core
    def _(core):
        at, order = ((x, XS), (z, ZS))[core]
        n = len(order) + 1
        sums[core].end()
        mid[: 16 * n, :] = sums[core].result()
        for r, go in zip(order, middle[core]):
            midsend[r - 1] = mid[rows(16 * mod(at + r, n), 16), :].astype(BF)
            go.start()

    g_sum.step(1)

    @on_core
    def _(core):
        at, order = ((x, XS), (z, ZS))[core]
        n = len(order) + 1
        total = mid[rows(16 * at, 16), :]
        for go in middle[core]:
            go.recv()
        for r in range(n - 1):
            total = total + midrecv[r].astype(F32)
        mid16[...] = total

    total = mid16[...]
    unit = kunit[...]
    inner = jnp.sum(unit * total, axis=1, keepdims=True)

    def kblock(core, hh):
        return lambda: kback.at[rows(16 * (core * NH + hh), 16), :]

    kback[rows(16 * (c * NH + h), 16), :] = (k_inv * (total - unit * inner)).astype(BF)
    kb_waits = {r: Send(kblock(c, h), kblock(c, h), hpeer[r], kblock(c, hfrom[r])) for r in (2, 1, 3)}
    for go in kb_waits.values():
        go.start()
    kb_core = {
        r: Send(kblock(c, hfrom[r]), kblock(c, hfrom[r]), partner, kblock(1 - c, hfrom[r])) for r in range(NH)
    }
    kb_core[0].start()

    g_sum.end()
    row = g_sum.result()
    unit = lunit[...]
    inner = jnp.sum(unit * row, axis=1, keepdims=True)
    row = (l_inv * (row - unit * inner)).astype(BF)

    for r in (1, 3, 2):
        kb_waits[r].recv()
        kb_core[r].start()
    b_spread = Spread(back)
    b_spread.start(row)
    for r in (0, 1, 3, 2):
        kb_core[r].recv()

    part = lax.dot_general(
        kf2[...], kback[...], (((0,), (0,)), ((), ())), preferred_element_type=F32
    ).astype(BF)
    tall = part.shape[0]
    for j in range(E // 128):
        wbuf[tall * j : tall * (j + 1), :] = part[:, 128 * j : 128 * (j + 1)]
    wbuf[tall * (E // 128) :, :] = jnp.zeros((NZ * WZ - tall * (E // 128), 128), BF)

    def cut_of(ref, size, at):
        return lambda: ref.at[rows(size * at, size), :]

    def slot(ref, at):
        return lambda: ref.at[at]

    w_first = [
        [Send(cut_of(wbuf, WZ, mod(z + r, NZ)), slot(wzr, r - 1), zpeer[r], core=0) for r in ZS],
        [Send(cut_of(wbuf, WX, mod(x + r, NX)), slot(wxr, r - 1), xpeer[r], core=1) for r in XS],
    ]
    w_second = [
        [Send(slot(wx, x), slot(wx, x), xpeer[r], slot(wx, xfrom[r]), 0) for r in XS],
        [Send(cut_of(wxs, BLK, mod(z + r, NZ)), slot(wxzr, r - 1), zpeer[r], core=1) for r in ZS],
    ]
    w_pair = [
        [Send(slot(wy, y), slot(wy, y), ypeer[0, 1], slot(wy, 1 - y), 0)],
        [Send(slot(wys, y), slot(wys, y), ypeer[0, 1], slot(wys, 1 - y), 1)],
    ]
    w_third = [
        [],
        [Send(cut_of(wxz, BLK, z), cut_of(wxz, BLK, z), zpeer[r], cut_of(wxz, BLK, zfrom[r]), 1) for r in ZS],
    ]
    w_last = [
        [Send(slot(wlast, pl.ds(0, WZ)), cut_of(out_w, WZ, z), zpeer[r], cut_of(out_w, WZ, zfrom[r]), 0) for r in ZS],
        [Send(slot(wlast, pl.ds(0, WX)), cut_of(out_w, WX, x), xpeer[r], cut_of(out_w, WX, xfrom[r]), 1) for r in XS],
    ]

    def keep(core):
        size, at = ((WZ, z), (WX, x))[core]
        return pltpu.make_async_copy(wlast.at[pl.ds(0, size)], cut_of(out_w, size, at)(), lsem.at[7])

    def begin(copies):
        for go in copies:
            go.start()

    def arrive(copies):
        for go in copies:
            go.recv()

    @on_core
    def _(core):
        begin(w_first[core])

    @on_core
    def _(core):
        if core == 0:
            total = wbuf[rows(WZ * z, WZ), :].astype(F32)
            arrive(w_first[0])
            for r in range(NZ - 1):
                total = total + wzr[r].astype(F32)
            wx[x] = total.astype(BF)
        else:
            total = wbuf[rows(WX * x, WX), :].astype(F32)
            arrive(w_first[1])
            for r in range(NX - 1):
                total = total + wxr[r].astype(F32)
            wxs[:WX, :] = total.astype(BF)
            wxs[WX:, :] = jnp.zeros((NZ * BLK - WX, 128), BF)
        begin(w_second[core])

    b_spread.step()

    @on_core
    def _(core):
        arrive(w_second[core])
        if core == 0:
            total = wx[0].astype(F32)
            for i in range(1, NX):
                total = total + wx[i].astype(F32)
            wy[y] = total.astype(BF)
        else:
            total = wxs[rows(BLK * z, BLK), :].astype(F32)
            for r in range(NZ - 1):
                total = total + wxzr[r].astype(F32)
            wys[y] = total.astype(BF)
        begin(w_pair[core])


    @on_core
    def _(core):
        arrive(w_pair[core])
        if core == 0:
            wlast[:WZ, :] = (wy[0].astype(F32) + wy[1].astype(F32)).astype(BF)
        else:
            wxz[rows(BLK * z, BLK), :] = (wys[0].astype(F32) + wys[1].astype(F32)).astype(BF)
            begin(w_third[1])
            arrive(w_third[1])
            wlast[...] = wxz[:WX, :]
        begin(w_last[core])
        keep(core).start()

    b_spread.last()
    b_spread.end()
    for i in range(2):
        og[HALF * i : HALF * (i + 1), :] = dot_t(back[HP * i : HP * i + HALF, :], lp[...]).astype(BF)
    g_out = pltpu.make_async_copy(og, out_g, lsem.at[6])
    g_out.start()

    @on_core
    def _(core):
        arrive(w_last[core])
        keep(core).wait()

    finish()
    g_out.wait()


def deliver(g, w, out_g, out_w, held, wall, ow, sem):
    copies = [
        pltpu.make_async_copy(*pair, sem.at[i])
        for i, pair in enumerate(((w, wall), (g, held), (held, out_g), (ow, out_w)))
    ]
    copies[0].start()
    copies[1].start()
    copies[1].wait()
    copies[2].start()
    copies[0].wait()
    tall = out_w.shape[0]
    for j in range(E // 128):
        ow[:, 128 * j : 128 * (j + 1)] = wall[tall * j : tall * (j + 1), :].astype(F32)
    copies[3].start()
    copies[2].wait()
    copies[3].wait()


def body(log_feats, kpi_feats, log_proj, kpi_proj, log_ids, kpi_ids):
    v = pltpu.VMEM
    inputs = (log_feats, kpi_feats, log_proj, kpi_proj, log_ids, kpi_ids.reshape(1, -1))
    outs = (jax.ShapeDtypeStruct(log_feats.shape, BF), jax.ShapeDtypeStruct((NZ * WZ, 128), BF))
    hbm = pl.BlockSpec(memory_space=pltpu.HBM)
    scratch = [v(a.shape, a.dtype) for a in inputs + outs[:1]] + [
        v((HP, E), BF), v((HP, E), BF), v((HP, E), F32), *[v((2, BLK, E), BF)] * 4,
        v((2 * HP, E), BF), v((BLK, E), F32), v((2 * HP, ID), BF),
        v((GROUP, E), F32), v((32, E), BF), v((32, E), BF), v((NH, 16, PK), BF), v((2, NH, 16, PK), BF),
        v(kpi_feats.shape, BF), v((2 * GROUP, kpi_feats.shape[1]), BF), v((1, GROUP), jnp.int32),
        v((COUNT, EK), BF), v((2 * OWN, E), F32),
        v((2 * HP, COUNT), BF), v((COUNT, E), F32), v((HP, E), F32),
        v((HP, E), BF), v((HP, E), BF), *[v((2, BLK, E), BF)] * 4, v((2 * HP, E), BF),
        *[v((4, 64, E), BF)] * 4, *[v((2, 128, E), BF)] * 4,
        v((128, E), F32), v((7, 16, E), BF), v((7, 16, E), BF), v((16, E), F32),
        v((2 * NH * 16, E), BF), v((NZ * WZ, 128), BF), v((NZ - 1, WZ, 128), BF), v((NX - 1, WX, 128), BF),
        v((NX, WZ, 128), BF), v((NY, WZ, 128), BF), v((NZ * BLK, 128), BF), v((NZ - 1, BLK, 128), BF),
        v((NY, BLK, 128), BF), v((NZ * BLK, 128), BF), v((WX, 128), BF),
        pltpu.SemaphoreType.DMA((NSEM,)), pltpu.SemaphoreType.DMA((NSEM,)),
        pltpu.SemaphoreType.DMA((8,)),
    ]
    grads = pl.pallas_call(
        kernel,
        out_shape=outs,
        in_specs=[hbm] * 6,
        out_specs=(hbm,) * 2,
        scratch_shapes=scratch,
        compiler_params=pltpu.CompilerParams(
            collective_id=0, has_side_effects=True, vmem_limit_bytes=62 * 1024 * 1024
        ),
    )(*inputs)
    return pl.pallas_call(
        deliver,
        out_shape=(outs[0], jax.ShapeDtypeStruct(kpi_proj.shape, F32)),
        in_specs=[hbm] * 2,
        out_specs=(hbm,) * 2,
        scratch_shapes=[v(outs[0].shape, BF), v(outs[1].shape, BF), v(kpi_proj.shape, F32), pltpu.SemaphoreType.DMA((4,))],
        compiler_params=pltpu.CompilerParams(vmem_limit_bytes=62 * 1024 * 1024),
    )(*grads)


def solution(mesh):
    return jax.shard_map(
        body,
        mesh=mesh,
        in_specs=(
            P("dp", "tensor"),
            P("dp", "tensor"),
            P("tensor", None),
            P("tensor", None),
            P("dp"),
            P("dp"),
        ),
        out_specs=(P("dp", "tensor"), P("tensor", None)),
        check_vma=False,
    )
```
